32 devices in a mesh: slot: 2 (over y), seq: 16 (over z, x, core).
Axes of the slice: x: 2, y: 2, z: 4, core: 2. Of those that a mesh axis runs over, the one named last changes fastest.
Arguments:
- hidden: bfloat16 [2, 2, 2048, 768], P('slot', None, 'seq'), may hold values from -6 to 6
- out_grad: bfloat16 [2, 2, 2048, 768], P('slot', None, 'seq'), may hold values from -6 to 6
- lengths: int32 [2, 2], P('slot'), may hold values from 512 to 2048, as said below
- w_in: bfloat16 [768, 1536], P(('slot', 'seq')), may hold values from -0.21875 to 0.21875
- w_depth: bfloat16 [9, 768], P(None, ('slot', 'seq')), may hold values from -2 to 2
- w_point: bfloat16 [768, 384], P(('slot', 'seq')), may hold values from -0.21875 to 0.21875
- w_kern: bfloat16 [20736], P(('slot', 'seq')), may hold values from -0.3125 to 0.3125
- w_out: bfloat16 [768, 768], P(('slot', 'seq')), may hold values from -0.625 to 0.625
- ln_gain: bfloat16 [2, 768], P(None, ('slot', 'seq')), may hold values from 0.099609375 to 1.8984375
- ln_bias: bfloat16 [2, 768], P(None, ('slot', 'seq')), may hold values from -3 to 3
- w_up: bfloat16 [2, 384, 1536], P(None, None, ('slot', 'seq')), may hold values from -0.3125 to 0.3125
- w_down: bfloat16 [2, 1536, 384], P(None, ('slot', 'seq')), may hold values from -0.15625 to 0.15625
Outputs:
- output: bfloat16 [2, 2, 2048, 768], P('slot', None, 'seq')
- hidden_grad: bfloat16 [2, 2, 2048, 768], P('slot', None, 'seq')
- w_in_grad: float32 [768, 1536], P(('slot', 'seq'))
- w_depth_grad: float32 [9, 768], P(None, ('slot', 'seq'))
- w_point_grad: float32 [768, 384], P(('slot', 'seq'))
- w_kern_grad: float32 [20736], P(('slot', 'seq'))
- w_out_grad: float32 [768, 768], P(('slot', 'seq'))
- ln_gain_grad: float32 [2, 768], P(None, ('slot', 'seq'))
- ln_bias_grad: float32 [2, 768], P(None, ('slot', 'seq'))
- w_up_grad: float32 [2, 384, 1536], P(None, None, ('slot', 'seq'))
- w_down_grad: float32 [2, 1536, 384], P(None, ('slot', 'seq'))
The draws below stay inside these ranges and needn't reach their ends.
Inputs may be any that keep to these rules, and one draw needn't show every extreme that they name: lengths[s, b] valid positions open sequence b of slot s; in every draw one sequence has all 2048.
All inputs are finite; a program needn't handle non-finite values.
Results may differ from the reference program's by a relative error of at most 0.017.
Values may be sent and summed in bfloat16 or wider, within the bound.
No kernel may reach another device: no remote copies, remote signals or barrier semaphores. Data moves between devices by JAX's collectives and lax.ppermute only.
A program may use at most 192 MiB of HBM per device.

```python
import math
import jax
import jax.numpy as jnp
from jax import lax

D = 768
HEADS = 6
HEAD_DIM = 64
FF = 3072
KSIZE = 9
GROUPS = 2
MB = 2
DA = 384
SLOTS = 2
SEQLEN = 2048


def draw_lengths(key, part):
    first_key, second_key = jax.random.split(key)
    drawn = jax.random.randint(first_key, (SLOTS * MB,), SEQLEN // 4, SEQLEN + 1, dtype=jnp.int32)
    chosen = jax.random.randint(second_key, (), 0, SLOTS * MB, dtype=jnp.int32)
    filled = jnp.where(jnp.arange(SLOTS * MB, dtype=jnp.int32) == chosen, SEQLEN, drawn)
    return filled.reshape(SLOTS, MB).astype(jnp.int32)


def block_scale(rng, extent, cuts, least, largest):
    loudness = 1.0
    for position, blocks in cuts:
        heights = jax.random.uniform(jax.random.fold_in(jax.random.fold_in(rng, 6), position), (blocks,), jnp.float32, least / len(cuts), largest / len(cuts))
        loudness = loudness * jnp.repeat(jnp.exp(heights), extent[position] // blocks).reshape((-1,) + (1,) * (len(extent) - 1 - position))
    return loudness


def scatter_about(stream_key, shape, scale, bound, shards=(), kind=jnp.bfloat16):
    level = block_scale(stream_key, shape, shards, -0.22, 0.18) if shards else 1.0
    values = jax.random.normal(stream_key, shape, jnp.float32) * scale * level
    return jnp.minimum(jnp.maximum(values, -bound), bound).astype(kind)


def setup_inputs(seed: int = 0) -> dict:
    arg_keys = jax.random.split(jax.random.key(seed), 13)
    hidden = scatter_about(arg_keys[0], (SLOTS, MB, SEQLEN, D), 1.0, 6.0, ((0, 2), (2, 16)))
    out_grad = scatter_about(arg_keys[1], (SLOTS, MB, SEQLEN, D), 1.0, 6.0, ((0, 2), (2, 16)))
    lengths = draw_lengths(jax.random.fold_in(arg_keys[12], 71), 0)
    w_in = scatter_about(arg_keys[3], (D, 4 * DA), D ** -0.5, 0.21875, ((0, 32),))
    w_depth = scatter_about(arg_keys[4], (KSIZE, D), KSIZE ** -0.5, 2.0, ((1, 32),))
    w_point = scatter_about(arg_keys[5], (D, DA), D ** -0.5, 0.21875, ((0, 32),))
    w_kern = scatter_about(arg_keys[6], (DA * HEADS * KSIZE,), DA ** -0.5, 0.3125, ((0, 32),))
    w_out = scatter_about(arg_keys[7], (D, D), (D // 8) ** -0.5, 0.625, ((0, 32),))
    ln_gain = jnp.clip(1.0 + 0.18 * jax.random.normal(arg_keys[8], (2, D), jnp.float32), 0.099609375, 1.8984375).astype(jnp.bfloat16)
    ln_bias = scatter_about(arg_keys[9], (2, D), 0.5, 3.0, ((1, 32),))
    w_up = scatter_about(arg_keys[10], (GROUPS, D // GROUPS, FF // GROUPS), (D // GROUPS) ** -0.5, 0.3125, ((2, 32),))
    w_down = scatter_about(arg_keys[11], (GROUPS, FF // GROUPS, D // GROUPS), (FF // GROUPS) ** -0.5, 0.15625, ((1, 32),))
    return dict(hidden=hidden, out_grad=out_grad, lengths=lengths, w_in=w_in, w_depth=w_depth, w_point=w_point, w_kern=w_kern, w_out=w_out, ln_gain=ln_gain, ln_bias=ln_bias, w_up=w_up, w_down=w_down)


@jax.custom_vjp
def low(v):
    return lax.optimization_barrier(v.astype(jnp.bfloat16)).astype(jnp.float32)

@jax.custom_vjp
def low_back(v):
    return v

def low_keep(v):
    return (low(v), None)

def low_pass(kept, grad):
    return (grad,)

def back_keep(v):
    return (v, None)

def back_low(kept, grad):
    return (low(grad),)
low.defvjp(low_keep, low_pass)
low_back.defvjp(back_keep, back_low)
norm_eps = 1e-12
neg_fill = -1e+30
highest = lax.Precision.HIGHEST

def matmul(left, right):
    return jnp.dot(left, right, precision=highest, preferred_element_type=jnp.float32)

def normalize_rows(scores):
    top = lax.optimization_barrier(jnp.max(scores, axis=-1, keepdims=True))
    expo = jnp.exp(scores - top)
    return expo / lax.optimization_barrier(jnp.sum(expo, axis=-1, keepdims=True))

def layer_norm(value, gain, shift):
    centre = value - lax.optimization_barrier(jnp.mean(value, axis=-1, keepdims=True))
    spread = lax.optimization_barrier(jnp.mean(centre * centre, axis=-1, keepdims=True))
    return centre * lax.rsqrt(spread + norm_eps) * gain + shift

def forward(tokens, mask, w_in, w_depth, w_point, w_kern, w_out, ln_gain, ln_bias, w_up, w_down):
    length = tokens.shape[0]
    half = KSIZE // 2
    masked = tokens * mask[:, None]
    proj = low(low_back(matmul(masked, w_in)))
    query = proj[:, :DA]
    key_heads = proj[:, DA:2 * DA].reshape(length, HEADS, HEAD_DIM)
    value_heads = proj[:, 2 * DA:3 * DA].reshape(length, HEADS, HEAD_DIM)
    conv_vals = proj[:, 3 * DA:]
    scale = HEAD_DIM ** (-0.5)
    keep = mask > 0.5
    block = math.gcd(length, 1024)

    def attend(query_block):
        scores = low_back(jnp.einsum('qhd,khd->hqk', query_block, key_heads, precision=highest) * scale)
        scores = jnp.where(keep[None, None, :], scores, neg_fill)
        probs = low(normalize_rows(scores))
        return jnp.einsum('hqk,khd->qhd', probs, value_heads, precision=highest)
    context_a = lax.map(jax.checkpoint(attend), query.reshape(length // block, block, HEADS, HEAD_DIM))
    context_a = context_a.reshape(length, DA)
    padded = jnp.pad(masked, ((half, half), (0, 0)))
    depth_out = low(sum((w_depth[j] * padded[j:j + length] for j in range(KSIZE))))
    key_conv = low_back(matmul(depth_out, w_point))
    mixed = low(key_conv * query)
    logits = low_back(matmul(mixed, w_kern.reshape(DA, HEADS * KSIZE))).reshape(length, HEADS, KSIZE)
    kernel = normalize_rows(logits)
    conv_pad = jnp.pad(conv_vals, ((half, half), (0, 0))).reshape(length + 2 * half, HEADS, HEAD_DIM)
    context_c = sum((kernel[:, :, j, None] * conv_pad[j:j + length] for j in range(KSIZE))).reshape(length, DA)
    context = low(low_back(jnp.concatenate([context_a, context_c], axis=1)))
    branch = low_back(matmul(context, w_out))
    first = layer_norm(tokens + branch, ln_gain[0], ln_bias[0])
    grouped = low(first).reshape(length, GROUPS, D // GROUPS)
    inner = low_back(jnp.einsum('sgi,gio->sgo', grouped, w_up, precision=highest))
    active = low(0.5 * inner * (1.0 + lax.erf(inner * 0.7071067811865476)))
    down = low_back(jnp.einsum('sgo,goi->sgi', active, w_down, precision=highest)).reshape(length, D)
    return layer_norm(first + down, ln_gain[1], ln_bias[1])

def reference(hidden, out_grad, lengths, w_in, w_depth, w_point, w_kern, w_out, ln_gain, ln_bias, w_up, w_down):
    weights = tuple((piece.astype(jnp.float32) for piece in (w_in, w_depth, w_point, w_kern, w_out, ln_gain, ln_bias, w_up, w_down)))
    count = SLOTS * MB
    tokens = hidden.reshape(count, SEQLEN, D).astype(jnp.float32)
    cotangents = out_grad.reshape(count, SEQLEN, D).astype(jnp.float32)
    seq_lengths = lengths.reshape(count).astype(jnp.int32)
    positions = jnp.arange(SEQLEN, dtype=jnp.int32)

    def per_sequence(totals, item):
        seq_tokens, seq_cot, seq_len = item
        mask = (positions < seq_len).astype(jnp.float32)

        def run(tokens_in, *params):
            return forward(tokens_in, mask, *params)
        result, pullback = jax.vjp(run, seq_tokens, *weights)
        grads = pullback(seq_cot * mask[:, None])
        totals = tuple((total + grad for total, grad in zip(totals, grads[1:])))
        return (totals, (result.astype(jnp.bfloat16), grads[0].astype(jnp.bfloat16)))
    zeros = tuple((jnp.zeros(piece.shape, jnp.float32) for piece in weights))
    totals, (results, token_grads) = lax.scan(per_sequence, zeros, (tokens, cotangents, seq_lengths))
    return (results.reshape(hidden.shape), token_grads.reshape(hidden.shape), totals[0], totals[1], totals[2], totals[3], totals[4], totals[5], totals[6], totals[7], totals[8])
```

```python
import math

import jax
import jax.numpy as jnp
from jax import lax
from jax.experimental import pallas as pl
from jax.experimental.pallas import tpu as pltpu
from jax.sharding import Mesh, PartitionSpec as P

D = 768
HEADS = 6
HEAD_DIM = 64
KSIZE = 9
GROUPS = 2
DA = 384
HALF = KSIZE // 2

norm_eps = 1e-12
neg_fill = -1e30
bf16 = jnp.bfloat16
f32 = jnp.float32

AXES = ("slot", "grp", "pair", "core")


def swap(value, axis, step):
    count = lax.axis_size(axis)
    return lax.ppermute(value, axis, [(i, i ^ step) for i in range(count)])


def doubled(value, axis):
    count = lax.axis_size(axis)
    value = value[None]
    step = 1
    while step < count:
        value = jnp.concatenate([value, swap(value, axis, step)], axis=0)
        step *= 2
    return value


def halved(value, axis):
    count = lax.axis_size(axis)
    step = count // 2
    while step >= 1:
        got = swap(value[step:], axis, step)
        value = value[:step].astype(f32) + got.astype(f32)
        if step > 1 :
            value = value.astype(bf16)
        step //= 2
    return value[0]


def gather_direct(value, axis):
    count = lax.axis_size(axis)
    return jnp.stack([value] + [swap(value, axis, k) for k in range(1, count)])


def sum_direct(value, axis):
    count = lax.axis_size(axis)
    total = value[0].astype(f32)
    for k in range(1, count):
        total = total + swap(value[k], axis, k).astype(f32)
    return total


def gather_half(piece, order):
    for axis in order:
        piece = doubled(piece, axis)
    return piece


def scatter_half(total, order):
    for axis in reversed(order[1:]):
        total = halved(total, axis).astype(bf16)
    return halved(total, order[0])


ORDER_A = ("grp", "pair", "slot", "core")
ORDER_B = ("grp", "slot", "pair", "core")


def flips(order, to_device):
    axes = AXES if to_device else tuple(reversed(order))
    other = tuple(reversed(order)) if to_device else AXES
    grids = {}
    for d, axis in enumerate(axes):
        shape = [1] * len(axes)
        shape[d] = lax.axis_size(axis)
        grids[axis] = lax.broadcasted_iota(jnp.int32, tuple(shape), d) ^ lax.axis_index(axis)
    idx = jnp.zeros((), jnp.int32)
    for axis in other:
        idx = idx * lax.axis_size(axis) + grids[axis]
    return idx.reshape(-1)


def move_blocks(index, arr, pieces, to_device):
    if to_device:
        n = arr.shape[0]
        out = (pieces, n) + arr.shape[2:]
    else:
        n = arr.shape[1]
        out = (n, pieces) + arr.shape[2:]

    def body(index_ref, src, dst, sem):
        def step(i, carry):
            at = index_ref[i]
            for piece in range(pieces):
                if to_device:
                    pltpu.make_async_copy(src.at[at, piece], dst.at[piece, i], sem).start()
                else:
                    pltpu.make_async_copy(src.at[piece, at], dst.at[i, piece], sem).start()
            return carry

        lax.fori_loop(0, n, step, 0)
        pltpu.make_async_copy(dst, dst, sem).wait()

    return pl.pallas_call(
        body,
        out_shape=jax.ShapeDtypeStruct(out, arr.dtype),
        in_specs=[
            pl.BlockSpec(memory_space=pltpu.SMEM),
            pl.BlockSpec(memory_space=pl.ANY),
        ],
        out_specs=pl.BlockSpec(memory_space=pl.ANY),
        scratch_shapes=[pltpu.SemaphoreType.DMA],
    )(index, arr)


def to_devices(arr, order, pieces):
    flat = arr.reshape((-1,) + arr.shape[-3:])
    moved = move_blocks(flips(order, True), flat, pieces, True)
    return [moved[i].reshape(-1, moved.shape[-1]) for i in range(pieces)]


def from_devices(parts, order, rows):
    arr = jnp.stack([t.astype(bf16).reshape(-1, rows, t.shape[1]) for t in parts])
    return move_blocks(flips(order, False), arr, len(parts), False)


def unflat(arr, order):
    sizes = [lax.axis_size(axis) for axis in reversed(order)]
    return arr.reshape(*sizes, *arr.shape[1:])


def dot(left, right):
    return jnp.dot(left, right, preferred_element_type=f32)


def dot_nt(left, right):
    return lax.dot_general(left, right, (((1,), (1,)), ((), ())), preferred_element_type=f32)


def dot_tn(left, right):
    return lax.dot_general(left, right, (((0,), (0,)), ((), ())), preferred_element_type=f32)


def norm_parts(value):
    centre = value - jnp.mean(value, axis=-1, keepdims=True)
    spread = jnp.mean(centre * centre, axis=-1, keepdims=True)
    inv = lax.rsqrt(spread + norm_eps)
    return centre * inv, inv


def norm_back(hat, inv, grad, gain):
    scaled = grad * gain
    return inv * (
        scaled
        - jnp.mean(scaled, axis=-1, keepdims=True)
        - hat * jnp.mean(scaled * hat, axis=-1, keepdims=True)
    )


def heads_of(value):
    return value.reshape(value.shape[0], HEADS, HEAD_DIM)


def per_device(
    hidden, out_grad, lengths, w_in, w_depth, w_point, w_kern, w_out, ln_gain, ln_bias, w_up, w_down
):
    length = hidden.shape[2]
    groups = lax.axis_size("grp")
    grp, pair, core = (lax.axis_index(a) for a in ("grp", "pair", "core"))
    scale = HEAD_DIM ** (-0.5)
    wide = w_in.shape[0]
    strip = w_kern.shape[0] // wide

    small = jnp.concatenate([w_depth.T, ln_gain.T, ln_bias.T], axis=1)
    small = jnp.pad(small, ((0, 0), (0, 128 - small.shape[1])))
    kern = jnp.pad(w_kern.reshape(wide, strip), ((0, 0), (0, 256 - strip)))
    small = jnp.concatenate([small, kern], axis=1)
    w_q, w_k, w_v, w_c = (w_in[:, i * DA : (i + 1) * DA] for i in range(4))
    early_a = jnp.stack([w_k, w_q, w_point])
    early_b = jnp.stack([w_v, w_c, small])
    fold = w_down.shape[1] // wide
    up_t = w_up.transpose(0, 2, 1).reshape(GROUPS, fold, wide, DA)
    down_r = w_down.reshape(GROUPS, fold, wide, DA)
    late_a = jnp.concatenate([w_out[None, :, :DA], up_t[0], down_r[0]], axis=0)
    late_b = jnp.concatenate([w_out[None, :, DA:], up_t[1], down_r[1]], axis=0)

    tokens2 = jnp.stack([hidden[0], out_grad[0]])
    mine = lax.dynamic_index_in_dim(tokens2, pair, 1, keepdims=False)
    theirs = lax.dynamic_index_in_dim(tokens2, 1 - pair, 1, keepdims=False)
    got = swap(theirs, "pair", 1)
    own_tokens = jnp.stack([mine[0], got[0]])
    own_cot = jnp.stack([mine[1], got[1]]).reshape(2 * length, D).astype(f32)
    full = gather_direct(own_tokens, "grp")
    full = jnp.stack([full, swap(full, "core", 1)])
    seq_len = lax.dynamic_index_in_dim(lengths[0], pair, 0, keepdims=False)

    early_a = gather_half(early_a, ORDER_A)
    early_b = gather_half(early_b, ORDER_B)
    late_a = gather_half(late_a, ORDER_A)
    late_b = gather_half(late_b, ORDER_B)

    def block_id(crel, grel, prel):
        return ((grp ^ grel) * 2 + (pair ^ prel)) * 2 + (core ^ crel)

    crel = jnp.arange(2, dtype=jnp.int32)[:, None, None, None]
    grel = jnp.arange(groups, dtype=jnp.int32)[None, :, None, None]
    prel = jnp.arange(2, dtype=jnp.int32)[None, None, :, None]
    where = block_id(crel, grel, prel) * length + jnp.arange(length, dtype=jnp.int32)
    valid = where < seq_len
    masked = jnp.where(valid[..., None], full, jnp.zeros((), bf16))
    flat_masked = masked.reshape(-1, D)
    total = flat_masked.shape[0]
    blocks = masked.reshape(-1, length, D)
    count = blocks.shape[0]
    own_mask = valid[0, 0].reshape(2 * length).astype(f32)

    def rel_of(block):
        inside = (block >= 0) & (block < count)
        block = jnp.clip(block, 0, count - 1)
        c2, p2, g2 = block % 2, (block // 2) % 2, block // 4
        return ((c2 ^ core) * groups + (g2 ^ grp)) * 2 + (p2 ^ pair), inside

    edges = []
    exts = []
    for b in range(2):
        here = block_id(0, 0, b)
        before, in_b = rel_of(here - 1)
        after, in_a = rel_of(here + 1)
        edges.append((before, in_b, after, in_a))
        head = lax.dynamic_slice(blocks, (before, length - HALF, 0), (1, HALF, D))[0]
        tail = lax.dynamic_slice(blocks, (after, 0, 0), (1, HALF, D))[0]
        exts.append(
            jnp.concatenate(
                [
                    jnp.where(in_b, head, jnp.zeros_like(head)),
                    blocks[b],
                    jnp.where(in_a, tail, jnp.zeros_like(tail)),
                ],
                axis=0,
            )
        )
    ext = jnp.stack(exts)

    mat_k, mat_q, mat_point = to_devices(early_a, ORDER_A, 3)
    mat_v, mat_c, smalls = to_devices(early_b, ORDER_B, 3)
    depth = smalls[:, :KSIZE].T.astype(f32)
    gain = smalls[:, KSIZE : KSIZE + 2].T.astype(f32)
    shift = smalls[:, KSIZE + 2 : KSIZE + 4].T.astype(f32)
    mat_kern = smalls[:, 128 : 128 + strip].reshape(DA, HEADS * KSIZE)
    mat_out = jnp.concatenate(
        to_devices(late_a, ORDER_A, 1) + to_devices(late_b, ORDER_B, 1), axis=1
    )
    mat_up = [t[..., 1 : 1 + fold, :, :].reshape(-1, DA) for t in (late_a, late_b)]
    mat_down = [t[..., 1 + fold :, :, :].reshape(-1, DA) for t in (late_a, late_b)]

    own_masked = blocks[:2].reshape(2 * length, D)
    tokens = own_tokens.reshape(2 * length, D).astype(f32)
    query = dot(own_masked, mat_q).astype(bf16)
    keys = dot(flat_masked, mat_k).astype(bf16)
    values = dot(flat_masked, mat_v).astype(bf16)
    conv_ext = dot(ext.reshape(-1, D), mat_c).astype(bf16).reshape(2, -1, DA)
    ext32 = ext.astype(f32)
    depth_out = sum(depth[j] * ext32[:, j : j + length] for j in range(KSIZE))
    depth_out = depth_out.reshape(2 * length, D).astype(bf16)
    key_conv = dot(depth_out, mat_point)
    query32 = query.astype(f32)
    mixed = (key_conv * query32).astype(bf16)
    logits = dot(mixed, mat_kern).reshape(2 * length, HEADS, KSIZE)
    expo = jnp.exp(logits - jnp.max(logits, axis=-1, keepdims=True))
    kernel = expo / jnp.sum(expo, axis=-1, keepdims=True)
    kernel_wide = [
        jnp.repeat(kernel[:, :, j], HEAD_DIM, axis=1).reshape(2, length, DA) for j in range(KSIZE)
    ]
    conv32 = conv_ext.astype(f32)
    context_c = sum(kernel_wide[j] * conv32[:, j : j + length] for j in range(KSIZE))
    context_c = context_c.reshape(2 * length, DA)

    scores = jnp.einsum("qhd,khd->hqk", heads_of(query), heads_of(keys), preferred_element_type=f32)
    scores = jnp.where(valid.reshape(-1)[None, None, :], scores * scale, neg_fill)
    top = jnp.max(scores, axis=2, keepdims=True)
    probs = jnp.exp(scores - top)
    probs = (probs / jnp.sum(probs, axis=2, keepdims=True)).astype(bf16)
    context_a = jnp.einsum("hqk,khd->qhd", probs, heads_of(values), preferred_element_type=f32)
    context_a = context_a.reshape(2 * length, DA)
    context = jnp.concatenate([context_a, context_c], axis=1).astype(bf16)
    hat1, inv1 = norm_parts(tokens + dot(context, mat_out))
    first = hat1 * gain[0] + shift[0]
    first_low = first.astype(bf16)
    low_g = [first_low[:, :DA], first_low[:, DA:]]
    inner = [dot_nt(low_g[g], mat_up[g]) for g in range(GROUPS)]
    phi = [0.5 * (1.0 + lax.erf(v * 0.7071067811865476)) for v in inner]
    active = [(v * c).astype(bf16) for v, c in zip(inner, phi)]
    down = jnp.concatenate([dot(active[g], mat_down[g]) for g in range(GROUPS)], axis=1)
    hat2, inv2 = norm_parts(first + down)
    result = (hat2 * gain[1] + shift[1]).astype(bf16)

    cot = own_cot * own_mask[:, None]
    g_gain1 = jnp.sum(cot * hat2, axis=0)
    g_bias1 = jnp.sum(cot, axis=0)
    d_r2 = norm_back(hat2, inv2, cot, gain[1])
    d_down = d_r2.astype(bf16)
    d_down_g = [d_down[:, :DA], d_down[:, DA:]]
    g_down = [dot_tn(active[g], d_down_g[g]) for g in range(GROUPS)]
    slope = [
        c + v * jnp.exp(-0.5 * v * v) * 0.3989422804014327 for v, c in zip(inner, phi)
    ]
    d_inner = [(dot_nt(d_down_g[g], mat_down[g]) * slope[g]).astype(bf16) for g in range(GROUPS)]
    g_up = [dot_tn(d_inner[g], low_g[g]) for g in range(GROUPS)]
    d_first = d_r2 + jnp.concatenate([dot(d_inner[g], mat_up[g]) for g in range(GROUPS)], axis=1)
    g_gain0 = jnp.sum(d_first * hat1, axis=0)
    g_bias0 = jnp.sum(d_first, axis=0)
    d_r1 = norm_back(hat1, inv1, d_first, gain[0])
    d_branch = d_r1.astype(bf16)
    g_out = dot_tn(context, d_branch)
    d_context = dot_nt(d_branch, mat_out).astype(bf16)
    d_ctx_a, d_ctx_c = d_context[:, :DA], d_context[:, DA:]

    late_ga = [from_devices([g_out[:, :DA]], ORDER_A, wide)]
    late_gb = [from_devices([g_out[:, DA:]], ORDER_B, wide)]
    for piece in (g_up, g_down):
        late_ga.append(piece[0].astype(bf16).reshape(-1, fold, wide, DA))
        late_gb.append(piece[1].astype(bf16).reshape(-1, fold, wide, DA))
    late_ga = scatter_half(unflat(jnp.concatenate(late_ga, axis=1), ORDER_A), ORDER_A)
    late_gb = scatter_half(unflat(jnp.concatenate(late_gb, axis=1), ORDER_B), ORDER_B)

    p32 = probs.astype(f32)
    d_heads = heads_of(d_ctx_a)
    d_values = jnp.einsum("hqk,qhd->khd", probs, d_heads, preferred_element_type=f32)
    d_probs = jnp.einsum("qhd,khd->hqk", d_heads, heads_of(values), preferred_element_type=f32)
    delta = jnp.sum(p32 * d_probs, axis=2, keepdims=True)
    d_scores = (p32 * (d_probs - delta)).astype(bf16)
    d_query_a = jnp.einsum("hqk,khd->qhd", d_scores, heads_of(keys), preferred_element_type=f32)
    d_query_a = d_query_a.reshape(2 * length, DA) * scale
    d_keys = jnp.einsum("hqk,qhd->khd", d_scores, heads_of(query), preferred_element_type=f32)
    d_keys = (d_keys.reshape(-1, DA) * scale).astype(bf16)
    d_values = d_values.reshape(-1, DA).astype(bf16)

    d_ctx_c32 = d_ctx_c.astype(f32).reshape(2, length, DA)
    d_kernel = jnp.stack(
        [
            jnp.sum(
                (d_ctx_c32 * conv32[:, j : j + length]).reshape(2 * length, HEADS, HEAD_DIM), axis=2
            )
            for j in range(KSIZE)
        ],
        axis=2,
    )
    d_conv_ext = sum(
        jnp.pad(kernel_wide[j] * d_ctx_c32, ((0, 0), (j, KSIZE - 1 - j), (0, 0)))
        for j in range(KSIZE)
    )
    d_conv_ext = d_conv_ext.astype(bf16).reshape(-1, DA)
    d_logits = kernel * (d_kernel - jnp.sum(kernel * d_kernel, axis=2, keepdims=True))
    d_logits = d_logits.astype(bf16).reshape(2 * length, HEADS * KSIZE)
    g_kern = dot_tn(mixed, d_logits)
    d_mixed = dot_nt(d_logits, mat_kern)
    d_key_conv = (d_mixed * query32).astype(bf16)
    d_query = (d_query_a + d_mixed * key_conv).astype(bf16)
    g_point = dot_tn(depth_out, d_key_conv)
    d_depth = dot_nt(d_key_conv, mat_point).reshape(2, length, D)
    g_depth = jnp.stack(
        [jnp.sum(d_depth * ext32[:, j : j + length], axis=(0, 1)) for j in range(KSIZE)], axis=1
    )
    d_ext = sum(
        jnp.pad(depth[j] * d_depth, ((0, 0), (j, KSIZE - 1 - j), (0, 0))) for j in range(KSIZE)
    )
    d_ext = d_ext + dot_nt(d_conv_ext, mat_c).reshape(2, -1, D)

    d_full = dot_nt(d_keys, mat_k) + dot_nt(d_values, mat_v)
    d_full = d_full.reshape(count, length, D)
    d_own = d_ext[:, HALF : HALF + length] + dot_nt(d_query, mat_q).reshape(2, length, D)
    d_full = jnp.concatenate([d_full[:2] + d_own, d_full[2:]], axis=0)
    for b in range(2):
        before, in_b, after, in_a = edges[b]
        for place, row, rows, inside in (
            (before, length - HALF, d_ext[b, :HALF], in_b),
            (after, 0, d_ext[b, -HALF:], in_a),
        ):
            old = lax.dynamic_slice(d_full, (place, row, 0), (1, HALF, D))
            new = old + jnp.where(inside, rows, 0.0)[None]
            d_full = lax.dynamic_update_slice(d_full, new, (place, row, 0))
    d_full = d_full.astype(bf16).reshape(2, groups, 2, length, D)
    d_full = d_full[0].astype(f32) + swap(d_full[1], "core", 1).astype(f32)
    d_full = sum_direct(d_full.astype(bf16), "grp")
    d_hidden = d_r1 + d_full.reshape(2 * length, D) * own_mask[:, None]
    d_hidden = d_hidden.astype(bf16)

    g_q = dot_tn(own_masked, d_query)
    g_k = dot_tn(flat_masked, d_keys)
    g_v = dot_tn(flat_masked, d_values)
    g_c = dot_tn(ext.reshape(-1, D), d_conv_ext)
    g_small = jnp.concatenate(
        [g_depth, g_gain0[:, None], g_gain1[:, None], g_bias0[:, None], g_bias1[:, None]], axis=1
    )
    g_small = jnp.pad(g_small, ((0, 0), (0, 128 - g_small.shape[1])))
    g_kern = jnp.pad(g_kern.reshape(D, strip), ((0, 0), (0, 256 - strip)))
    g_small = jnp.concatenate([g_small, g_kern], axis=1)
    early_ga = from_devices([g_k, g_q, g_point], ORDER_A, wide)
    early_gb = from_devices([g_v, g_c, g_small], ORDER_B, wide)
    early_ga = scatter_half(unflat(early_ga, ORDER_A), ORDER_A)
    early_gb = scatter_half(unflat(early_gb, ORDER_B), ORDER_B)

    outs = jnp.stack([result, d_hidden]).reshape(2, 2, length, D)
    got = swap(outs[:, 1], "pair", 1)
    kept = outs[:, 0]
    final = jnp.where(
        pair == 0, jnp.stack([kept, got], axis=1), jnp.stack([got, kept], axis=1)
    )
    g_small = early_gb[2]
    late = [late_ga, late_gb]
    return (
        final[0][None],
        final[1][None],
        jnp.concatenate([early_ga[1], early_ga[0], early_gb[0], early_gb[1]], axis=1),
        g_small[:, :KSIZE].T,
        early_ga[2],
        g_small[:, 128 : 128 + strip].reshape(-1),
        jnp.concatenate([late_ga[0], late_gb[0]], axis=1),
        g_small[:, KSIZE : KSIZE + 2].T,
        g_small[:, KSIZE + 2 : KSIZE + 4].T,
        jnp.stack([t[1 : 1 + fold].reshape(-1, DA).T for t in late]),
        jnp.stack([t[1 + fold :].reshape(-1, DA) for t in late]),
    )


def solution(mesh):
    slots, places = mesh.shape["slot"], mesh.shape["seq"]
    fine = Mesh(mesh.devices.reshape(slots, places // 4, 2, 2), AXES)
    seq = AXES[1:]
    placed = (
        P("slot", None, seq, None),
        P("slot", None, seq, None),
        P("slot", None),
        P(AXES, None),
        P(None, AXES),
        P(AXES, None),
        P(AXES),
        P(AXES, None),
        P(None, AXES),
        P(None, AXES),
        P(None, None, AXES),
        P(None, AXES, None),
    )
    return jax.shard_map(
        per_device,
        mesh=fine,
        in_specs=placed,
        out_specs=(placed[0], placed[1]) + placed[3:],
        check_vma=False,
    )
```

```python
import math

import jax
import jax.numpy as jnp
from jax import lax
from jax.experimental import pallas as pl
from jax.experimental.pallas import tpu as pltpu
from jax.sharding import Mesh, PartitionSpec as P

D = 768
HEADS = 6
HEAD_DIM = 64
KSIZE = 9
GROUPS = 2
DA = 384
HALF = KSIZE // 2

norm_eps = 1e-12
neg_fill = -1e30
bf16 = jnp.bfloat16
f32 = jnp.float32

AXES = ("slot", "grp", "pair", "core")


def swap(value, axis, step):
    count = lax.axis_size(axis)
    return lax.ppermute(value, axis, [(i, i ^ step) for i in range(count)])


def bits_of(axis):
    step = lax.axis_size(axis) // 2
    bits = []
    while step >= 1:
        bits.append((axis, step))
        step //= 2
    return bits


def all_bits():
    return [bit for axis in AXES for bit in bits_of(axis)]


def upper(bit):
    axis, step = bit
    return (lax.axis_index(axis) & step) != 0


def spread(arr):
    return arr.reshape(arr.shape[:1] + (1,) * len(all_bits()) + arr.shape[1:])


def gather_bit(arr, bit):
    dim = 1 + all_bits().index(bit)
    got = swap(arr, *bit)
    up = upper(bit)
    return jnp.concatenate([jnp.where(up, got, arr), jnp.where(up, arr, got)], axis=dim)


def scatter_bit(arr, bit, kind=bf16):
    dim = 1 + all_bits().index(bit)
    low_half = lax.slice_in_dim(arr, 0, 1, axis=dim)
    high_half = lax.slice_in_dim(arr, 1, 2, axis=dim)
    up = upper(bit)
    got = swap(jnp.where(up, low_half, high_half), *bit)
    kept = jnp.where(up, high_half, low_half)
    return (kept.astype(f32) + got.astype(f32)).astype(kind)


def flatten(arr):
    return arr.reshape(arr.shape[0], -1, arr.shape[-1])


def unflatten(arr, rows):
    return arr.reshape(arr.shape[0], *(2,) * len(all_bits()), rows, arr.shape[-1])


def sides():
    pair, slot, core = bits_of("pair"), bits_of("slot"), bits_of("core")
    return (pair + slot + core, slot + pair + core)


def gather_blocks(arr, axis):
    arr = arr[None]
    for bit in bits_of(axis):
        got = swap(arr, *bit)
        arr = jnp.stack([arr, got], axis=1).reshape((-1,) + arr.shape[1:])
    return arr


def scatter_blocks(arr, axis):
    for bit in reversed(bits_of(axis)):
        split = arr.reshape((arr.shape[0] // 2, 2) + arr.shape[1:])
        got = swap(split[:, 1], *bit)
        arr = (split[:, 0].astype(f32) + got.astype(f32)).astype(bf16)
    return arr[0]


def dot(left, right):
    return jnp.dot(left, right, preferred_element_type=f32)


def dot_nt(left, right):
    return lax.dot_general(left, right, (((1,), (1,)), ((), ())), preferred_element_type=f32)


def dot_tn(left, right):
    return lax.dot_general(left, right, (((0,), (0,)), ((), ())), preferred_element_type=f32)


def norm_parts(value):
    centre = value - jnp.mean(value, axis=-1, keepdims=True)
    spread = jnp.mean(centre * centre, axis=-1, keepdims=True)
    inv = lax.rsqrt(spread + norm_eps)
    return centre * inv, inv


def norm_back(hat, inv, grad, gain):
    scaled = grad * gain
    return inv * (
        scaled
        - jnp.mean(scaled, axis=-1, keepdims=True)
        - hat * jnp.mean(scaled * hat, axis=-1, keepdims=True)
    )


PAD = 16
VMEM_LIMIT = 60 << 20


def kernel_call(body, name, meta, args, outs, scratch=(), flops=0, exps=0):
    moved = sum(a.size * a.dtype.itemsize for a in args)
    moved += sum(math.prod(s) * jnp.dtype(d).itemsize for s, d in outs)
    return pl.pallas_call(
        body,
        out_shape=[jax.ShapeDtypeStruct(s, d) for s, d in outs],
        in_specs=[pl.BlockSpec(memory_space=pltpu.SMEM)]
        + [pl.BlockSpec(memory_space=pltpu.VMEM)] * len(args),
        out_specs=[pl.BlockSpec(memory_space=pltpu.VMEM)] * len(outs),
        scratch_shapes=[pltpu.VMEM(s, d) for s, d in scratch],
        compiler_params=pltpu.CompilerParams(vmem_limit_bytes=VMEM_LIMIT),
        cost_estimate=pl.CostEstimate(flops=flops, bytes_accessed=moved, transcendentals=exps),
        name=name,
    )(meta, *args)


def rows_of(ref, piece):
    return ref[piece * D : (piece + 1) * D, :]


def row_iota(shape):
    return lax.broadcasted_iota(jnp.int32, shape, 0)


def head_mask(shape, half):
    lane = lax.broadcasted_iota(jnp.int32, shape, 1)
    return (lane < HEAD_DIM) if half == 0 else (lane >= HEAD_DIM)


def tap_spread(j):
    r = lax.broadcasted_iota(jnp.int32, (128, DA), 0)
    c = lax.broadcasted_iota(jnp.int32, (128, DA), 1)
    hit = jnp.zeros((128, DA), jnp.bool_)
    for h in range(HEADS):
        hit = hit | ((r == h * KSIZE + j) & (c >= h * HEAD_DIM) & (c < (h + 1) * HEAD_DIM))
    return jnp.where(hit, 1.0, 0.0).astype(bf16)


def tap_pick(j):
    r = lax.broadcasted_iota(jnp.int32, (DA, 128), 0)
    c = lax.broadcasted_iota(jnp.int32, (DA, 128), 1)
    hit = jnp.zeros((DA, 128), jnp.bool_)
    for h in range(HEADS):
        hit = hit | ((r == h * HEAD_DIM) & (c == h * KSIZE + j))
    return jnp.where(hit, 1.0, 0.0).astype(bf16)


def head_sums():
    r = lax.broadcasted_iota(jnp.int32, (DA, DA), 0)
    c = lax.broadcasted_iota(jnp.int32, (DA, DA), 1)
    hit = jnp.zeros((DA, DA), jnp.bool_)
    for h in range(HEADS):
        lo, hi = h * HEAD_DIM, (h + 1) * HEAD_DIM
        hit = hit | ((r >= lo) & (r < hi) & (c >= lo) & (c < hi))
    return jnp.where(hit, 1.0, 0.0).astype(bf16)


def small_rows(small_ref):
    return small_ref[2 * D : 3 * D, :128].astype(f32).T


def conv_forward(
    meta, full, early_a, early_b, kern, ext, query, conv, depth_out, key_conv, mixed, taps, context,
    ext32, conv32, logits,
):
    blocks, size, _ = full.shape
    seq_len = meta[0]
    for b in range(2):
        base = meta[1 + b]
        head = full[meta[1 + blocks + b], size - PAD :, :].astype(f32)
        row = row_iota((PAD, D))
        at = row + (base - PAD)
        head = jnp.where((row >= PAD - HALF) & (at >= 0) & (at < seq_len), head, 0.0)
        tail = full[meta[3 + blocks + b], :PAD, :].astype(f32)
        tail = jnp.where((row < HALF) & (row + (base + size) < seq_len), tail, 0.0)
        body = full[b].astype(f32)
        body = jnp.where(row_iota((size, D)) + base < seq_len, body, 0.0)
        ext32[b, :PAD, :] = head
        ext32[b, PAD : PAD + size, :] = body
        ext32[b, PAD + size :, :] = tail
        ext[b] = ext32[b].astype(bf16)
    par = small_rows(early_b)
    for b in range(2):
        for c in range(0, D, 128):
            acc = par[0:1, c : c + 128] * ext32[b, PAD - HALF : PAD - HALF + size, c : c + 128]
            for j in range(1, KSIZE):
                lo = PAD - HALF + j
                acc = acc + par[j : j + 1, c : c + 128] * ext32[b, lo : lo + size, c : c + 128]
            depth_out[b * size : (b + 1) * size, c : c + 128] = acc.astype(bf16)
    own = jnp.concatenate([ext[b, PAD : PAD + size, :] for b in range(2)], axis=0)
    q = dot(own, rows_of(early_a, 1)).astype(bf16)
    query[...] = q
    for b in range(2):
        vals = dot(ext[b], rows_of(early_b, 1)).astype(bf16)
        conv[b] = vals
        conv32[b] = vals.astype(f32)
    kc = dot(depth_out[...], rows_of(early_a, 2))
    key_conv[...] = kc
    mix = (kc * q.astype(f32)).astype(bf16)
    mixed[...] = mix
    for j in range(KSIZE):
        wide = dot(kern[...], tap_spread(j)).astype(bf16)
        logits[j] = dot(mix, wide)
    step = 32
    for r in range(0, 2 * size, step):
        b, o = r // size, r % size
        vals = [logits[j, r : r + step, :] for j in range(KSIZE)]
        top = vals[0]
        for v in vals[1:]:
            top = jnp.maximum(top, v)
        vals = [jnp.exp(v - top) for v in vals]
        total = vals[0]
        for v in vals[1:]:
            total = total + v
        inv = 1.0 / total
        acc = jnp.zeros((step, DA), f32)
        for j in range(KSIZE):
            k = vals[j] * inv
            taps[j, r : r + step, :] = k.astype(bf16)
            lo = PAD - HALF + j + o
            acc = acc + k * conv32[b, lo : lo + step, :]
        context[r : r + step, :] = acc.astype(bf16)


def attend_forward(meta, full, early_a, early_b, query, keys, values, probs, inverse, context, scores):
    blocks, size, _ = full.shape
    chunk = 2 * size
    count = blocks // 2
    queries = query.shape[0]
    seq_len = meta[0]
    w_k, w_v = rows_of(early_a, 0), rows_of(early_b, 0)
    for n in range(count):
        x = full[2 * n : 2 * n + 2].reshape(chunk, D)
        at = slice(n * chunk, (n + 1) * chunk)
        keys[at, :] = dot(x, w_k).astype(bf16)
        values[at, :] = dot(x, w_v).astype(bf16)
    inverse[...] = jnp.zeros(inverse.shape, f32)
    row = row_iota((size, queries))
    for pr in range(HEADS // 2):
        cols = slice(pr * 128, (pr + 1) * 128)
        q = query[:, cols].astype(f32) * (HEAD_DIM ** (-0.5))
        halves = []
        for h in range(2):
            qh = jnp.where(head_mask((queries, 128), h), q, 0.0).astype(bf16)
            top = jnp.full((1, queries), neg_fill, f32)
            for n in range(count):
                s = dot_nt(keys[n * chunk : (n + 1) * chunk, cols], qh)
                for i in range(2):
                    part = s[i * size : (i + 1) * size]
                    part = jnp.where(row < seq_len - meta[1 + 2 * n + i], part, neg_fill)
                    lo = (2 * n + i) * size
                    scores[lo : lo + size, :] = part
                    top = jnp.maximum(top, jnp.max(part, axis=0, keepdims=True))
            total = jnp.zeros((1, queries), f32)
            acc = jnp.zeros((128, queries), f32)
            for n in range(count):
                at = slice(n * chunk, (n + 1) * chunk)
                e = jnp.exp(scores[at, :] - top)
                total = total + jnp.sum(e, axis=0, keepdims=True)
                e = e.astype(bf16)
                probs[2 * pr + h, at, :] = e
                acc = acc + dot_tn(values[at, cols], e)
            inv = 1.0 / total
            inverse[2 * pr + h : 2 * pr + h + 1, :] = inv
            halves.append((acc * inv)[h * HEAD_DIM : (h + 1) * HEAD_DIM])
        context[:, cols] = jnp.concatenate(halves, axis=0).T


def attend_backward(meta, d_ctx, context, query, keys, values, probs, inverse, d_keys, d_values, d_query):
    total, queries = keys.shape[0], query.shape[0]
    chunk = min(total, 256)
    scale = HEAD_DIM ** (-0.5)
    for pr in range(HEADS // 2):
        cols = slice(pr * 128, (pr + 1) * 128)
        grads = d_ctx[:, cols].astype(f32)
        prod = grads * context[:, cols]
        q = query[:, cols].astype(f32)
        d_o, d_os, q_s, deltas = [], [], [], []
        for h in range(2):
            mask = head_mask((queries, 128), h)
            inv = inverse[2 * pr + h : 2 * pr + h + 1, :]
            col = jnp.broadcast_to(inv, (128, queries)).T
            d_o.append(jnp.where(mask, grads, 0.0).astype(bf16))
            d_os.append(jnp.where(mask, grads * col, 0.0).astype(bf16))
            q_s.append(jnp.where(mask, q * col * scale, 0.0).astype(bf16))
            delta = lax.dot_general(
                jnp.ones((8, 128), f32),
                jnp.where(mask, prod, 0.0),
                (((1,), (1,)), ((), ())),
                precision=lax.Precision.HIGHEST,
                preferred_element_type=f32,
            )
            deltas.append(delta[0:1])
        acc = [jnp.zeros((128, queries), f32) for _ in range(2)]
        for n in range(total // chunk):
            at = slice(n * chunk, (n + 1) * chunk)
            k, v = keys[at, cols], values[at, cols]
            dv = jnp.zeros((chunk, 128), f32)
            dk = jnp.zeros((chunk, 128), f32)
            for h in range(2):
                e = probs[2 * pr + h, at, :]
                dv = dv + dot(e, d_os[h])
                dp = dot_nt(v, d_o[h])
                ds = (e.astype(f32) * (dp - deltas[h])).astype(bf16)
                dk = dk + dot(ds, q_s[h])
                acc[h] = acc[h] + dot_tn(k, ds)
            d_keys[at, cols] = dk.astype(bf16)
            d_values[at, cols] = dv.astype(bf16)
        halves = []
        for h in range(2):
            inv = inverse[2 * pr + h : 2 * pr + h + 1, :] * scale
            halves.append((acc[h] * inv)[h * HEAD_DIM : (h + 1) * HEAD_DIM])
        d_query[:, cols] = jnp.concatenate(halves, axis=0).T


def middle(
    meta, ctx_a, ctx_c, tokens, cot, early_b, late_a, late_b,
    result, d_r1_out, d_ctx, late_ga, late_gb, norms,
    slope, active, d_inner,
):
    size = tokens.shape[0] // 2
    seq_len = meta[0]
    par = small_rows(early_b)
    gain0, gain1 = par[KSIZE : KSIZE + 1], par[KSIZE + 1 : KSIZE + 2]
    bias0, bias1 = par[KSIZE + 2 : KSIZE + 3], par[KSIZE + 3 : KSIZE + 4]
    late, late_g = (late_a, late_b), (late_ga, late_gb)
    ff = active.shape[2]
    up = [t[D : D + ff, :] for t in late]
    down = [t[D + ff : D + 2 * ff, :] for t in late]
    ctx = jnp.concatenate([ctx_a[...].astype(bf16), ctx_c[...]], axis=1)
    branch = jnp.concatenate([dot(ctx, rows_of(t, 0)) for t in late], axis=1)
    hat1, inv1 = norm_parts(tokens[...].astype(f32) + branch)
    first = hat1 * gain0 + bias0
    low = first.astype(bf16)
    lows = [low[:, :DA], low[:, DA:]]
    part = 512
    downs = []
    for g in range(GROUPS):
        for c in range(0, ff, part):
            v = dot_nt(lows[g], late[g][D + c : D + c + part, :])
            phi = 0.5 * (1.0 + lax.erf(v * 0.7071067811865476))
            active[g, :, c : c + part] = (v * phi).astype(bf16)
            slope[g, :, c : c + part] = phi + v * (jnp.exp(-0.5 * v * v) * 0.3989422804014327)
        downs.append(dot(active[g], down[g]))
    hat2, inv2 = norm_parts(first + jnp.concatenate(downs, axis=1))
    result[...] = (hat2 * gain1 + bias1).astype(bf16)

    row = row_iota((size, D))
    grad = jnp.concatenate(
        [
            jnp.where(row < seq_len - meta[1 + b], cot[b * size : (b + 1) * size, :].astype(f32), 0.0)
            for b in range(2)
        ],
        axis=0,
    )
    norms[...] = jnp.zeros(norms.shape, f32)
    norms[1:2, :] = jnp.sum(grad * hat2, axis=0, keepdims=True)
    norms[3:4, :] = jnp.sum(grad, axis=0, keepdims=True)
    d_r2 = norm_back(hat2, inv2, grad, gain1)
    d_down = d_r2.astype(bf16)
    firsts = []
    for g in range(GROUPS):
        dd = d_down[:, g * DA : (g + 1) * DA]
        for c in range(0, ff, part):
            da = dot_nt(dd, late[g][D + ff + c : D + ff + c + part, :])
            d_inner[g, :, c : c + part] = (da * slope[g, :, c : c + part]).astype(bf16)
            late_g[g][D + ff + c : D + ff + c + part, :] = dot_tn(
                active[g, :, c : c + part], dd
            ).astype(bf16)
            late_g[g][D + c : D + c + part, :] = dot_tn(
                d_inner[g, :, c : c + part], lows[g]
            ).astype(bf16)
        firsts.append(dot(d_inner[g], up[g]))
    d_first = d_r2 + jnp.concatenate(firsts, axis=1)
    norms[0:1, :] = jnp.sum(d_first * hat1, axis=0, keepdims=True)
    norms[2:3, :] = jnp.sum(d_first, axis=0, keepdims=True)
    d_r1 = norm_back(hat1, inv1, d_first, gain0)
    d_r1_out[...] = d_r1
    d_branch = d_r1.astype(bf16)
    for g in range(GROUPS):
        late_g[g][:D, :] = dot_tn(ctx, d_branch[:, g * DA : (g + 1) * DA]).astype(bf16)
    d_context = dot_nt(d_branch[:, :DA], rows_of(late_a, 0))
    d_context = d_context + dot_nt(d_branch[:, DA:], rows_of(late_b, 0))
    d_ctx[...] = d_context.astype(bf16)


def conv_backward(
    meta, d_ctx, ext, query, conv, depth_out, key_conv, mixed, taps, early_a, early_b, kern,
    d_query, d_ext, g_point, g_c, g_kern, g_depth,
    ext32, conv32, d_kern, d_conv, d_dep,
):
    size = query.shape[0] // 2
    step = 32
    par = small_rows(early_b)
    for b in range(2):
        ext32[b] = ext[b].astype(f32)
        conv32[b] = conv[b].astype(f32)
    d_conv[...] = jnp.zeros(d_conv.shape, f32)
    sums = head_sums()
    for j in range(KSIZE):
        for b in range(2):
            lo = PAD - HALF + j
            rows = slice(b * size, (b + 1) * size)
            grad = d_ctx[rows, DA:].astype(f32)
            prod = (grad * conv32[b, lo : lo + size, :]).astype(bf16)
            d_kern[j, rows, :] = dot(prod, sums)
            d_conv[b, lo : lo + size, :] += taps[j, rows, :].astype(f32) * grad
    picks = [tap_pick(j) for j in range(KSIZE)]
    compact = jnp.zeros((2 * size, 128), f32)
    total = jnp.zeros((2 * size, DA), f32)
    for j in range(KSIZE):
        total = total + taps[j].astype(f32) * d_kern[j]
    for j in range(KSIZE):
        dl = (taps[j].astype(f32) * (d_kern[j] - total)).astype(bf16)
        compact = compact + dot(dl, picks[j])
    compact = compact.astype(bf16)
    g_kern[...] = dot_tn(mixed[...], compact)
    d_mixed = dot_nt(compact, kern[...])
    d_kc = (d_mixed * query[...].astype(f32)).astype(bf16)
    d_query[...] = d_mixed * key_conv[...]
    g_point[...] = dot_tn(depth_out[...], d_kc).astype(bf16)
    d_dep[...] = dot_nt(d_kc, rows_of(early_a, 2))
    gc = None
    for b in range(2):
        dc = d_conv[b].astype(bf16)
        d_ext[b] = dot_nt(dc, rows_of(early_b, 1))
        part = dot_tn(ext[b], dc)
        gc = part if gc is None else gc + part
    g_c[...] = gc.astype(bf16)
    g_depth[...] = jnp.zeros(g_depth.shape, f32)
    for c in range(0, D, 128):
        cols = slice(c, c + 128)
        for j in range(KSIZE):
            lo = PAD - HALF + j
            acc = jnp.zeros((1, 128), f32)
            for b in range(2):
                dd = d_dep[b * size : (b + 1) * size, cols]
                acc = acc + jnp.sum(dd * ext32[b, lo : lo + size, cols], axis=0, keepdims=True)
                d_ext[b, lo : lo + size, cols] += par[j : j + 1, cols] * dd
            g_depth[j : j + 1, cols] = acc


def project_backward(meta, d_keys, d_values, dq_a, dq_c, d_ext, early_a, early_b, d_full, d_query):
    blocks, size, _ = d_full.shape
    chunk = 2 * size
    dq = (dq_a[...] + dq_c[...]).astype(bf16)
    d_query[...] = dq
    for n in range(blocks // 2):
        at = slice(n * chunk, (n + 1) * chunk)
        both = dot_nt(d_keys[at, :], rows_of(early_a, 0))
        both = both + dot_nt(d_values[at, :], rows_of(early_b, 0))
        if n == 0:
            both = both + dot_nt(dq, rows_of(early_a, 1))
            both = both + jnp.concatenate(
                [d_ext[b, PAD : PAD + size, :] for b in range(2)], axis=0
            )
        d_full[2 * n : 2 * n + 2] = both.astype(bf16).reshape(2, size, D)
    for b in range(2):
        base = meta[1 + b]
        before, after = meta[1 + blocks + b], meta[3 + blocks + b]
        rim = jnp.where(row_iota((PAD, D)) + (base - PAD) >= 0, d_ext[b, :PAD, :], 0.0)
        old = d_full[before, size - PAD :, :].astype(f32)
        d_full[before, size - PAD :, :] = (old + rim).astype(bf16)
        inside = row_iota((PAD, D)) + (base + size) < blocks * size
        rim = jnp.where(inside, d_ext[b, PAD + size :, :], 0.0)
        old = d_full[after, :PAD, :].astype(f32)
        d_full[after, :PAD, :] = (old + rim).astype(bf16)


def project_grads(meta, full, d_keys, d_values, ext, d_query, g_point, g_c, g_kern, g_depth, norms, early_ga, early_gb):
    size = full.shape[1]
    x = full[...].reshape(-1, D)
    early_ga[:D, :] = dot_tn(x, d_keys[...]).astype(bf16)
    own = jnp.concatenate([ext[b, PAD : PAD + size, :] for b in range(2)], axis=0)
    early_ga[D : 2 * D, :] = dot_tn(own, d_query[...]).astype(bf16)
    early_ga[2 * D :, :] = g_point[...]
    early_gb[:D, :] = dot_tn(x, d_values[...]).astype(bf16)
    early_gb[D : 2 * D, :] = g_c[...]
    rows = jnp.concatenate(
        [g_depth[:KSIZE, :], norms[:4, :], jnp.zeros((128 - KSIZE - 4, D), f32)], axis=0
    )
    early_gb[2 * D :, :128] = rows.T.astype(bf16)
    early_gb[2 * D :, 128:256] = g_kern[...].astype(bf16)
    early_gb[2 * D :, 256:] = jnp.zeros((D, 128), bf16)


def per_device(
    hidden, out_grad, lengths, w_in, w_depth, w_point, w_kern, w_out, ln_gain, ln_bias, w_up, w_down
):
    length = hidden.shape[2]
    groups = lax.axis_size("grp")
    grp, pair, core = (lax.axis_index(a) for a in ("grp", "pair", "core"))
    wide = w_in.shape[0]
    strip = w_kern.shape[0] // wide

    small = jnp.concatenate([w_depth.T, ln_gain.T, ln_bias.T], axis=1)
    small = jnp.pad(small, ((0, 0), (0, 128 - small.shape[1])))
    kern = jnp.pad(w_kern.reshape(wide, strip), ((0, 0), (0, 256 - strip)))
    small = jnp.concatenate([small, kern], axis=1)
    w_q, w_k, w_v, w_c = (w_in[:, i * DA : (i + 1) * DA] for i in range(4))
    fold = w_down.shape[1] // wide
    up_t = w_up.transpose(0, 2, 1).reshape(GROUPS, fold, wide, DA)
    down_r = w_down.reshape(GROUPS, fold, wide, DA)
    early, late = 3, 1 + 2 * fold
    packed = jnp.concatenate(
        [
            jnp.stack([w_k, w_q, w_point, w_v, w_c, small]),
            w_out[None, :, :DA],
            up_t[0],
            down_r[0],
            w_out[None, :, DA:],
            up_t[1],
            down_r[1],
        ],
        axis=0,
    )

    tokens2 = jnp.stack([hidden[0], out_grad[0]])
    mine = lax.dynamic_index_in_dim(tokens2, pair, 1, keepdims=False)
    theirs = lax.dynamic_index_in_dim(tokens2, 1 - pair, 1, keepdims=False)
    got = swap(theirs, "pair", 1)
    own_tokens = jnp.stack([mine[0], got[0]])
    own_cot = jnp.stack([mine[1], got[1]]).reshape(2 * length, D)
    packed = spread(packed)
    for bit in bits_of("grp"):
        packed = gather_bit(packed, bit)
    cuts = [0, early, 2 * early, 2 * early + late, 2 * early + 2 * late]
    parts = [packed[lo:hi] for lo, hi in zip(cuts[:-1], cuts[1:])]
    for i, order in enumerate(sides() * 2):
        for bit in order:
            parts[i] = gather_bit(parts[i], bit)
    early_a, early_b, late_a, late_b = (flatten(t) for t in parts)
    full = gather_blocks(own_tokens, "grp")
    full = jnp.stack([full, swap(full, "core", 1)])
    seq_len = lax.dynamic_index_in_dim(lengths[0], pair, 0, keepdims=False)

    count = 4 * groups
    total = count * length
    crel, grel, prel = (
        lax.broadcasted_iota(jnp.int32, (2, groups, 2), d) for d in range(3)
    )
    owner = ((grp ^ grel) * 2 + (pair ^ prel)) * 2 + (core ^ crel)
    owner = owner.reshape(-1)

    def place_of(block):
        block = jnp.clip(block, 0, count - 1)
        c2, p2, g2 = block & 1, (block >> 1) & 1, block >> 2
        return ((c2 ^ core) * groups + (g2 ^ grp)) * 2 + (p2 ^ pair)

    meta = jnp.concatenate(
        [seq_len[None], owner * length, place_of(owner[:2] - 1), place_of(owner[:2] + 1)]
    ).astype(jnp.int32)
    blocks = full.reshape(count, length, D)
    own = 2 * length
    kern = early_b[2][:, 128 : 128 + strip].reshape(DA, HEADS * KSIZE)
    kern = jnp.pad(kern, ((0, 0), (0, 128 - HEADS * KSIZE)))
    early_a, early_b = early_a.reshape(-1, DA), early_b.reshape(-1, DA)
    late_a, late_b = late_a.reshape(-1, DA), late_b.reshape(-1, DA)
    ff = fold * D
    tall = length + 2 * PAD

    ext, query, conv, depth_out, key_conv, mixed, taps, context_c = kernel_call(
        conv_forward,
        "conv_forward",
        meta,
        (blocks, early_a, early_b, kern),
        (
            ((2, tall, D), bf16),
            ((own, DA), bf16),
            ((2, tall, DA), bf16),
            ((own, D), bf16),
            ((own, DA), f32),
            ((own, DA), bf16),
            ((KSIZE, own, DA), bf16),
            ((own, DA), bf16),
        ),
        (((2, tall, D), f32), ((2, tall, DA), f32), ((KSIZE, own, DA), f32)),
        flops=2 * own * DA * (3 * D + KSIZE * DA),
        exps=KSIZE * own * DA,
    )
    keys, values, probs, inverse, context_a = kernel_call(
        attend_forward,
        "attend_forward",
        meta,
        (blocks, early_a, early_b, query),
        (
            ((total, DA), bf16),
            ((total, DA), bf16),
            ((HEADS, total, own), bf16),
            ((8, own), f32),
            ((own, DA), f32),
        ),
        (((total, own), f32),),
        flops=4 * total * D * DA + 16 * own * total * DA,
        exps=HEADS * own * total,
    )
    result, d_r1, d_context, late_ga, late_gb, norms = kernel_call(
        middle,
        "middle",
        meta,
        (context_a, context_c, own_tokens.reshape(own, D), own_cot, early_b, late_a, late_b),
        (
            ((own, D), bf16),
            ((own, D), f32),
            ((own, D), bf16),
            (late_a.shape, bf16),
            (late_b.shape, bf16),
            ((8, D), f32),
        ),
        (
            ((GROUPS, own, ff), f32),
            ((GROUPS, own, ff), bf16),
            ((GROUPS, own, ff), bf16),
        ),
        flops=6 * own * (D * D + 4 * D * ff // GROUPS),
        exps=4 * own * ff,
    )
    late_g = [t.reshape(late, -1, DA) for t in (late_ga, late_gb)]
    for i, order in enumerate(sides()):
        late_g[i] = unflatten(late_g[i], wide)
        for bit in reversed(order):
            late_g[i] = scatter_bit(late_g[i], bit)
    late_g = jnp.concatenate(late_g, axis=0)
    for n, bit in enumerate(reversed(bits_of("grp"))):
        late_g = scatter_bit(late_g, bit, bf16 if n + 1 < len(bits_of("grp")) else f32)
    late_g = flatten(late_g)

    dq_c, d_ext, g_point, g_c, g_kern, g_depth = kernel_call(
        conv_backward,
        "conv_backward",
        meta,
        (
            d_context, ext, query, conv, depth_out, key_conv, mixed, taps, early_a, early_b, kern,
        ),
        (
            ((own, DA), f32),
            ((2, tall, D), f32),
            ((D, DA), bf16),
            ((D, DA), bf16),
            ((DA, 128), f32),
            ((16, D), f32),
        ),
        (
            ((2, tall, D), f32),
            ((2, tall, DA), f32),
            ((KSIZE, own, DA), f32),
            ((2, tall, DA), f32),
            ((own, D), f32),
        ),
        flops=2 * own * DA * (4 * D + 2 * KSIZE * DA),
    )
    d_keys, d_values, dq_a = kernel_call(
        attend_backward,
        "attend_backward",
        meta,
        (d_context, context_a, query, keys, values, probs, inverse),
        (((total, DA), bf16), ((total, DA), bf16), ((own, DA), f32)),
        flops=40 * own * total * DA,
    )
    d_full, d_query = kernel_call(
        project_backward,
        "project_backward",
        meta,
        (d_keys, d_values, dq_a, dq_c, d_ext, early_a, early_b),
        (((count, length, D), bf16), ((own, DA), bf16)),
        flops=4 * (total + own) * D * DA,
    )
    d_full = d_full.reshape(2, groups, 2, length, D)
    d_full = (d_full[0].astype(f32) + swap(d_full[1], "core", 1).astype(f32)).astype(bf16)
    d_full = scatter_blocks(d_full, "grp").astype(f32).reshape(own, D)
    own_mask = jnp.arange(length, dtype=jnp.int32)[None] + (owner[:2] * length)[:, None] < seq_len
    d_hidden = (d_r1 + jnp.where(own_mask.reshape(own, 1), d_full, 0.0)).astype(bf16)

    g_kern = jnp.pad(g_kern[:, : HEADS * KSIZE].reshape(D, strip), ((0, 0), (0, 128 - strip)))
    early_g = kernel_call(
        project_grads,
        "project_grads",
        meta,
        (blocks, d_keys, d_values, ext, d_query, g_point, g_c, g_kern, g_depth, norms),
        ((early_a.shape, bf16), (early_b.shape, bf16)),
        flops=4 * (total + own) * D * DA,
    )
    early_g = [t.reshape(early, -1, DA) for t in early_g]
    for i, order in enumerate(sides()):
        early_g[i] = unflatten(early_g[i], wide)
        for bit in reversed(order):
            early_g[i] = scatter_bit(early_g[i], bit)
    early_g = jnp.concatenate(early_g, axis=0)
    for n, bit in enumerate(reversed(bits_of("grp"))):
        early_g = scatter_bit(early_g, bit, bf16 if n + 1 < len(bits_of("grp")) else f32)
    early_ga = flatten(early_g)

    outs = jnp.stack([result, d_hidden]).reshape(2, 2, length, D)
    got = swap(outs[:, 1], "pair", 1)
    kept = outs[:, 0]
    final = jnp.where(
        pair == 0, jnp.stack([kept, got], axis=1), jnp.stack([got, kept], axis=1)
    )
    g_k, g_q, g_point, g_v, g_c, g_small = early_ga
    late_g = [late_g[:late], late_g[late:]]
    return (
        final[0][None],
        final[1][None],
        jnp.concatenate([g_q, g_k, g_v, g_c], axis=1),
        g_small[:, :KSIZE].T,
        g_point,
        g_small[:, 128 : 128 + strip].reshape(-1),
        jnp.concatenate([t[0] for t in late_g], axis=1),
        g_small[:, KSIZE : KSIZE + 2].T,
        g_small[:, KSIZE + 2 : KSIZE + 4].T,
        jnp.stack([t[1 : 1 + fold].reshape(-1, DA).T for t in late_g]),
        jnp.stack([t[1 + fold :].reshape(-1, DA) for t in late_g]),
    )


def solution(mesh):
    slots, places = mesh.shape["slot"], mesh.shape["seq"]
    fine = Mesh(mesh.devices.reshape(slots, places // 4, 2, 2), AXES)
    seq = AXES[1:]
    placed = (
        P("slot", None, seq, None),
        P("slot", None, seq, None),
        P("slot", None),
        P(AXES, None),
        P(None, AXES),
        P(AXES, None),
        P(AXES),
        P(AXES, None),
        P(None, AXES),
        P(None, AXES),
        P(None, None, AXES),
        P(None, AXES, None),
    )
    return jax.shard_map(
        per_device,
        mesh=fine,
        in_specs=placed,
        out_specs=(placed[0], placed[1]) + placed[3:],
        check_vma=False,
    )
```

```python
import functools
import math

import jax
import jax.numpy as jnp
from jax import lax
from jax.experimental import pallas as pl
from jax.experimental.pallas import tpu as pltpu
from jax.sharding import Mesh, PartitionSpec as P

D = 768
HEADS = 6
HEAD_DIM = 64
KSIZE = 9
GROUPS = 2
DA = 384
HALF = KSIZE // 2
PAD = 16
PARTS = 32
ROWS = D // PARTS
UNIT = 2 * ROWS
OUT_SPAN = (2 * UNIT, 2 * UNIT + 32)
FF_SPAN = (0, 2 * UNIT)
LATE_ROWS = 128
VMEM_LIMIT = 60 << 20

norm_eps = 1e-12
neg_fill = -1e30
bf16 = jnp.bfloat16
f32 = jnp.float32

AXES = ("slot", "half", "grp", "mate", "core")


def swap(value, axis, step=1):
    count = lax.axis_size(axis)
    return lax.ppermute(value, axis, [(i, i ^ step) for i in range(count)])


def bits_of(axis):
    step = lax.axis_size(axis) // 2
    bits = []
    while step >= 1:
        bits.append((axis, step))
        step //= 2
    return bits


def first_bits():
    return bits_of("half") + bits_of("grp")


def sides():
    mate, slot = bits_of("mate"), bits_of("slot")
    return (mate + slot, slot + mate)


def routes():
    bits = bits_of("grp") + bits_of("mate")
    return (bits, bits[::-1])


def gather_bit(arr, bit):
    return jnp.concatenate([arr, swap(arr, *bit)], axis=0)


def scatter_bit(arr, bit, kind=bf16):
    n = arr.shape[0] // 2
    got = swap(arr[n:], *bit)
    return (arr[:n].astype(f32) + got.astype(f32)).astype(kind)


def scatter_blocks(arr, order):
    bits = routes()[0]
    arr = arr.reshape((2,) * len(bits) + arr.shape[1:])
    for n, bit in enumerate(reversed(order)):
        dim = bits.index(bit)
        got = swap(lax.slice_in_dim(arr, 1, 2, axis=dim), *bit)
        arr = lax.slice_in_dim(arr, 0, 1, axis=dim).astype(f32) + got.astype(f32)
        if n + 1 < len(order):
            arr = arr.astype(bf16)
    return arr.reshape(arr.shape[len(bits) :])


def dot(left, right):
    return jnp.dot(left, right, preferred_element_type=f32)


def dot_nt(left, right):
    return lax.dot_general(left, right, (((1,), (1,)), ((), ())), preferred_element_type=f32)


def dot_tn(left, right):
    return lax.dot_general(left, right, (((0,), (0,)), ((), ())), preferred_element_type=f32)


def norm_parts(value):
    centre = value - jnp.mean(value, axis=-1, keepdims=True)
    spread = jnp.mean(centre * centre, axis=-1, keepdims=True)
    inv = lax.rsqrt(spread + norm_eps)
    return centre * inv, inv


def norm_back(hat, inv, grad, gain):
    scaled = grad * gain
    return inv * (
        scaled
        - jnp.mean(scaled, axis=-1, keepdims=True)
        - hat * jnp.mean(scaled * hat, axis=-1, keepdims=True)
    )


class Staged:
    def __init__(self, ref, fetch=(), store=()):
        self.ref, self.fetch, self.store = ref, dict(fetch), dict(store)
        self.flying = []

    @property
    def shape(self):
        return self.ref.shape

    def rows(self, span):
        if span in self.fetch:
            self.fetch.pop(span).wait()
        return self.ref

    def __getitem__(self, at):
        for span in list(self.fetch):
            self.fetch.pop(span).wait()
        return self.ref[at]

    def __setitem__(self, at, value):
        self.ref[at] = value

    def flush(self, *spans):
        for span in spans or list(self.store):
            copy = self.store.pop(span)
            copy.start()
            self.flying.append(copy)

    def finish(self):
        self.flush(*self.store)
        for copy in self.flying:
            copy.wait()


def once(method):
    def found(self, *args):
        key = (method.__name__, *args)
        if key not in self.known:
            self.known[key] = method(self, *args)
        return self.known[key]

    return found


class Numbers:
    def __init__(self, ref, grps, packed):
        self.seq_len = ref[0]
        self.slot, self.half, self.grp, self.mate, self.core = (ref[i] for i in range(1, 6))
        self.grps, self.packed = grps, packed
        self.side = self.core if packed else 0
        self.known = {}

    @once
    def owner(self, n):
        h, m = n % 2, n // 2 % 2
        g, c = n // 4 % self.grps, n // (4 * self.grps)
        left = (self.half ^ h) * self.grps + (self.grp ^ g)
        return (left * 2 + (self.mate ^ m)) * 2 + (self.core ^ c)

    def place(self, block):
        count = 8 * self.grps
        block = jnp.clip(block, 0, count - 1)
        c, m = block & 1, (block >> 1) & 1
        g, h = (block >> 2) & (self.grps - 1), block >> (1 + self.grps.bit_length())
        left = (c ^ self.core) * self.grps + (g ^ self.grp)
        return (left * 2 + (m ^ self.mate)) * 2 + (h ^ self.half)

    @once
    def weight_place(self, which, k):
        if not self.packed:
            return k
        slot, half, grp, mate = (k // 8) % 2, (k // 4) % 2, (k // 2) % 2, k % 2
        slot, half, grp, mate = slot ^ self.slot, half ^ self.half, grp ^ self.grp, mate ^ self.mate
        if which == 0:
            return ((slot * 2 + mate) * 2 + grp) * 2 + half
        return ((mate * 2 + slot) * 2 + grp) * 2 + half

    @once
    def sum_place_of(self, k, core):
        if not self.packed:
            return 2 * k + core
        slot, half, grp, mate = (k // 8) % 2, (k // 4) % 2, (k // 2) % 2, k % 2
        return ((slot * 2 + mate) * 2 + core) * 4 + (grp ^ self.grp) * 2 + (half ^ self.half)


def flush(*arrays):
    for arr in arrays:
        if isinstance(arr, Staged):
            arr.flush()


def staged(shape, kind):
    return len(shape) > 1 and shape[-2] % 16 == 0 and math.prod(shape) * jnp.dtype(kind).itemsize >= 1 << 17


def kernel_call(body, name, meta, args, outs, scratch=(), flops=0, exps=0, waits=(), form=(), in_spans={}, out_spans={}):
    moved = sum(a.size * a.dtype.itemsize for a in args)
    moved += sum(math.prod(s) * jnp.dtype(d).itemsize for s, d in outs)
    ins_at = [i for i, a in enumerate(args) if staged(a.shape, a.dtype)]
    outs_at = [i for i, (s, d) in enumerate(outs) if staged(s, d)]
    places = [pltpu.VMEM(args[i].shape, args[i].dtype) for i in ins_at]
    places += [pltpu.VMEM(*outs[i]) for i in outs_at]

    def whole(*refs):
        refs = list(refs)

        def take(n):
            got = refs[:n]
            del refs[:n]
            return got

        (numbers,) = take(1)
        ins, _, results = take(len(args)), take(len(waits)), take(len(outs))
        (zero,) = take(1)
        mine = take(len(scratch))
        in_place = dict(zip(ins_at, take(len(ins_at))))
        out_place = dict(zip(outs_at, take(len(outs_at))))
        in_sems, out_sems = take(2)
        zero[0] = 0


        def copies(source, target, spans, sems, n):
            made = {}
            for j, (lo, hi) in enumerate(spans):
                at = (slice(None),) * (len(source.shape) - 2) + (slice(lo, hi),)
                pair = (source.at[at], target.at[at]) if hi else (source, target)
                made[lo, hi] = pltpu.make_async_copy(*pair, sems.at[n, j])
            return made

        fetches = []
        for n, i in enumerate(ins_at):
            made = copies(ins[i], in_place[i], in_spans.get(i, ((0, 0),)), in_sems, n)
            fetches += [(j, copy) for j, copy in enumerate(made.values())]
            ins[i] = Staged(in_place[i], fetch=made)
        for _, copy in sorted(fetches, key=lambda t: t[0]):
            copy.start()
        for n, i in enumerate(outs_at):
            made = copies(out_place[i], results[i], out_spans.get(i, ((0, 0),)), out_sems, n)
            results[i] = Staged(out_place[i], store=made)
        body(Numbers(numbers, *form), *ins, *results, *mine)
        for i in outs_at:
            results[i].finish()

    def space(i, chosen):
        return pl.BlockSpec(memory_space=pl.ANY if i in chosen else pltpu.VMEM)

    *results, mark = pl.pallas_call(
        whole,
        out_shape=[jax.ShapeDtypeStruct(s, d) for s, d in outs]
        + [jax.ShapeDtypeStruct((1,), jnp.int32)],
        in_specs=[pl.BlockSpec(memory_space=pltpu.SMEM)]
        + [space(i, ins_at) for i in range(len(args))]
        + [pl.BlockSpec(memory_space=pl.ANY)] * len(waits),
        out_specs=[space(i, outs_at) for i in range(len(outs))]
        + [pl.BlockSpec(memory_space=pltpu.SMEM)],
        scratch_shapes=[pltpu.VMEM(s, d) for s, d in scratch]
        + places
        + [pltpu.SemaphoreType.DMA((max(len(t), 1), 4)) for t in (ins_at, outs_at)],
        compiler_params=pltpu.CompilerParams(vmem_limit_bytes=VMEM_LIMIT),
        cost_estimate=pl.CostEstimate(flops=flops, bytes_accessed=moved, transcendentals=exps),
        name=name,
    )(meta, *args, *waits)
    return *results, mark[0]


def rows_of(ref, piece):
    return ref[piece * D : (piece + 1) * D, :]


def row_iota(shape):
    return lax.broadcasted_iota(jnp.int32, shape, 0)


def head_mask(shape, half):
    lane = lax.broadcasted_iota(jnp.int32, shape, 1)
    return (lane < HEAD_DIM) if half == 0 else (lane >= HEAD_DIM)


def tap_spread(j):
    r = lax.broadcasted_iota(jnp.int32, (128, DA), 0)
    c = lax.broadcasted_iota(jnp.int32, (128, DA), 1)
    hit = jnp.zeros((128, DA), jnp.bool_)
    for h in range(HEADS):
        hit = hit | ((r == h * KSIZE + j) & (c >= h * HEAD_DIM) & (c < (h + 1) * HEAD_DIM))
    return jnp.where(hit, 1.0, 0.0).astype(bf16)


def tap_pick(j):
    r = lax.broadcasted_iota(jnp.int32, (DA, 128), 0)
    c = lax.broadcasted_iota(jnp.int32, (DA, 128), 1)
    hit = jnp.zeros((DA, 128), jnp.bool_)
    for h in range(HEADS):
        hit = hit | ((r == h * HEAD_DIM) & (c == h * KSIZE + j))
    return jnp.where(hit, 1.0, 0.0).astype(bf16)


def head_sums():
    r = lax.broadcasted_iota(jnp.int32, (DA, DA), 0)
    c = lax.broadcasted_iota(jnp.int32, (DA, DA), 1)
    hit = jnp.zeros((DA, DA), jnp.bool_)
    for h in range(HEADS):
        lo, hi = h * HEAD_DIM, (h + 1) * HEAD_DIM
        hit = hit | ((r >= lo) & (r < hi) & (c >= lo) & (c < hi))
    return jnp.where(hit, 1.0, 0.0).astype(bf16)


def on_even(meta, shape):
    return jnp.zeros(shape, jnp.int32) + meta.side == 0


def fill_rows(own, got, at, piece, even, out):
    for k in range(PARTS // 2):
        one, two = own[at(k), piece].astype(f32), got[at(k), piece].astype(f32)
        out[2 * k * ROWS : (2 * k + 1) * ROWS, :] = jnp.where(even, one, two)
        out[(2 * k + 1) * ROWS : (2 * k + 2) * ROWS, :] = jnp.where(even, two, one)


def deal_rows(value, at, piece, even, keep, send):
    for k in range(PARTS // 2):
        one = value[2 * k * ROWS : (2 * k + 1) * ROWS]
        two = value[(2 * k + 1) * ROWS : (2 * k + 2) * ROWS]
        keep[at(k), piece] = jnp.where(even, one, two).astype(bf16)
        send[at(k), piece] = jnp.where(even, two, one).astype(bf16)


def weave(width, odd):
    r = lax.broadcasted_iota(jnp.int32, (D, DA), 0)
    c = lax.broadcasted_iota(jnp.int32, (D, DA), 1)
    return jnp.where(r == 2 * c + odd, 1.0, 0.0).astype(bf16)


def shift_lanes(width, odd):
    r = lax.broadcasted_iota(jnp.int32, (128, 128), 0)
    c = lax.broadcasted_iota(jnp.int32, (128, 128), 1)
    return jnp.where((r < width) & (c == r + odd * width), 1.0, 0.0).astype(bf16)


STRIP = DA * HEADS * KSIZE // D


def conv_forward(
    meta, full_a, full_b, more_a, more_b, mats, par, kern, query, ext, conv, depth_out, key_conv, mixed, taps, context,
    ext32, conv32, logits,
):
    near, size, _ = full_a.shape
    blocks = 2 * near
    seq_len = meta.seq_len

    def slab(place, lo, hi):
        here = jnp.minimum(place, near - 1)
        there = jnp.maximum(place - near, 0)
        pick = jnp.zeros((hi - lo, D), jnp.int32) + place < near
        one = jnp.concatenate([full_a[here, lo:hi, :], full_b[here, lo:hi, :]], axis=1)
        two = jnp.concatenate([more_a[there, lo:hi, :], more_b[there, lo:hi, :]], axis=1)
        return jnp.where(pick, one.astype(f32), two.astype(f32))

    for b in range(2):
        base = meta.owner(b) * size
        head = slab(meta.place(meta.owner(b) - 1), size - PAD, size)
        row = row_iota((PAD, D))
        at = row + (base - PAD)
        head = jnp.where((row >= PAD - HALF) & (at >= 0) & (at < seq_len), head, 0.0)
        tail = slab(meta.place(meta.owner(b) + 1), 0, PAD)
        tail = jnp.where((row < HALF) & (row + (base + size) < seq_len), tail, 0.0)
        body = jnp.concatenate([full_a[b], full_b[b]], axis=1).astype(f32)
        body = jnp.where(row_iota((size, D)) + base < seq_len, body, 0.0)
        ext32[b, :PAD, :] = head
        ext32[b, PAD : PAD + size, :] = body
        ext32[b, PAD + size :, :] = tail
        ext[b] = ext32[b].astype(bf16)
    for b in range(2):
        for c in range(0, D, 128):
            acc = par[0:1, c : c + 128] * ext32[b, PAD - HALF : PAD - HALF + size, c : c + 128]
            for j in range(1, KSIZE):
                lo = PAD - HALF + j
                acc = acc + par[j : j + 1, c : c + 128] * ext32[b, lo : lo + size, c : c + 128]
            depth_out[b * size : (b + 1) * size, c : c + 128] = acc.astype(bf16)
    for b in range(2):
        vals = dot(ext[b], rows_of(mats, 4)).astype(bf16)
        conv[b] = vals
        conv32[b] = vals.astype(f32)
    kc = dot(depth_out[...], rows_of(mats, 2))
    key_conv[...] = kc
    mix = (kc * query[...].astype(f32)).astype(bf16)
    mixed[...] = mix
    for j in range(KSIZE):
        wide = dot(kern[...], tap_spread(j)).astype(bf16)
        logits[j] = dot(mix, wide)
    step = 32
    for r in range(0, 2 * size, step):
        b, o = r // size, r % size
        vals = [logits[j, r : r + step, :] for j in range(KSIZE)]
        top = vals[0]
        for v in vals[1:]:
            top = jnp.maximum(top, v)
        vals = [jnp.exp(v - top) for v in vals]
        total = vals[0]
        for v in vals[1:]:
            total = total + v
        inv = 1.0 / total
        acc = jnp.zeros((step, DA), f32)
        for j in range(KSIZE):
            k = vals[j] * inv
            taps[j, r : r + step, :] = k.astype(bf16)
            lo = PAD - HALF + j + o
            acc = acc + k * conv32[b, lo : lo + step, :]
        context[r : r + step, :] = acc.astype(bf16)


def sequence_rows(parts, n):
    full_a, full_b, more_a, more_b = parts
    near = full_a.shape[0]
    left, right, at = (full_a, full_b, 2 * n) if 2 * n < near else (more_a, more_b, 2 * n - near)
    rows = jnp.concatenate([left[at : at + 2], right[at : at + 2]], axis=2)
    return rows.reshape(-1, D)


def project_forward(
    meta, full_a, full_b, more_a, more_b, own_a, got_a, own_b, got_b,
    query, keys, values, mats, par, kern, rows32,
):
    near, size, _ = full_a.shape
    blocks = 2 * near
    chunk = 2 * size
    seq_len = meta.seq_len
    even = on_even(meta, (ROWS, DA))
    for side, own, got in ((0, own_a, got_a), (1, own_b, got_b)):
        for piece in range(3):
            fill_rows(own, got, lambda k: meta.weight_place(side, k), piece, even, rows32)
            to = side * 3 + piece
            if to < 5:
                mats[to * D : (to + 1) * D, :] = rows32[...].astype(bf16)
    par[...] = rows32[:, :128].T[:16]
    strips = rows32[:, 128:256].astype(bf16)
    wide = None
    for odd in range(2):
        part = dot(dot_tn(weave(STRIP, odd), strips).astype(bf16), shift_lanes(STRIP, odd))
        wide = part if wide is None else wide + part
    kern[...] = wide.astype(bf16)
    for n in range(near):
        x = sequence_rows((full_a, full_b, more_a, more_b), n)
        at = slice(n * chunk, (n + 1) * chunk)
        keys[at, :] = dot(x, rows_of(mats, 0)).astype(bf16)
        values[at, :] = dot(x, rows_of(mats, 3)).astype(bf16)
        if n == 0:
            q = dot(x, rows_of(mats, 1))
            row = row_iota((size, DA))
            for b in range(2):
                part = q[b * size : (b + 1) * size]
                part = jnp.where(row < seq_len - meta.owner(b) * size, part, 0.0)
                query[b * size : (b + 1) * size, :] = part.astype(bf16)


def attend_forward(meta, query, keys, values, probs, inverse, context, scores):
    queries = query.shape[0]
    size = queries // 2
    chunk = queries
    count = keys.shape[0] // chunk
    seq_len = meta.seq_len
    inverse[...] = jnp.zeros(inverse.shape, f32)
    row = row_iota((size, queries))
    for pr in range(HEADS // 2):
        cols = slice(pr * 128, (pr + 1) * 128)
        q = query[:, cols].astype(f32) * (HEAD_DIM ** (-0.5))
        halves = []
        for h in range(2):
            qh = jnp.where(head_mask((queries, 128), h), q, 0.0).astype(bf16)
            top = jnp.full((1, queries), neg_fill, f32)
            for n in range(count):
                s = dot_nt(keys[n * chunk : (n + 1) * chunk, cols], qh)
                for i in range(2):
                    part = s[i * size : (i + 1) * size]
                    part = jnp.where(row < seq_len - meta.owner(2 * n + i) * size, part, neg_fill)
                    lo = (2 * n + i) * size
                    scores[lo : lo + size, :] = part
                    top = jnp.maximum(top, jnp.max(part, axis=0, keepdims=True))
            total = jnp.zeros((1, queries), f32)
            acc = jnp.zeros((128, queries), f32)
            for n in range(count):
                at = slice(n * chunk, (n + 1) * chunk)
                e = jnp.exp(scores[at, :] - top)
                total = total + jnp.sum(e, axis=0, keepdims=True)
                e = e.astype(bf16)
                probs[2 * pr + h, at, :] = e
                acc = acc + dot_tn(values[at, cols], e)
            inv = 1.0 / total
            inverse[2 * pr + h : 2 * pr + h + 1, :] = inv
            halves.append((acc * inv)[h * HEAD_DIM : (h + 1) * HEAD_DIM])
        context[:, cols] = jnp.concatenate(halves, axis=0).T


def attend_backward(meta, d_ctx, context, query, keys, values, probs, inverse, d_keys, d_values, d_query):
    total, queries = keys.shape[0], query.shape[0]
    chunk = min(total, 256)
    scale = HEAD_DIM ** (-0.5)
    for pr in range(HEADS // 2):
        cols = slice(pr * 128, (pr + 1) * 128)
        grads = d_ctx[:, cols].astype(f32)
        prod = grads * context[:, cols]
        q = query[:, cols].astype(f32)
        d_o, d_os, q_s, deltas = [], [], [], []
        for h in range(2):
            mask = head_mask((queries, 128), h)
            inv = inverse[2 * pr + h : 2 * pr + h + 1, :]
            col = jnp.broadcast_to(inv, (128, queries)).T
            d_o.append(jnp.where(mask, grads, 0.0).astype(bf16))
            d_os.append(jnp.where(mask, grads * col, 0.0).astype(bf16))
            q_s.append(jnp.where(mask, q * col * scale, 0.0).astype(bf16))
            delta = lax.dot_general(
                jnp.ones((8, 128), f32),
                jnp.where(mask, prod, 0.0),
                (((1,), (1,)), ((), ())),
                precision=lax.Precision.HIGHEST,
                preferred_element_type=f32,
            )
            deltas.append(delta[0:1])
        acc = [jnp.zeros((128, queries), f32) for _ in range(2)]
        for n in range(total // chunk):
            at = slice(n * chunk, (n + 1) * chunk)
            k, v = keys[at, cols], values[at, cols]
            dv = jnp.zeros((chunk, 128), f32)
            dk = jnp.zeros((chunk, 128), f32)
            for h in range(2):
                e = probs[2 * pr + h, at, :]
                dv = dv + dot(e, d_os[h])
                dp = dot_nt(v, d_o[h])
                ds = (e.astype(f32) * (dp - deltas[h])).astype(bf16)
                dk = dk + dot(ds, q_s[h])
                acc[h] = acc[h] + dot_tn(k, ds)
            d_keys[at, cols] = dk.astype(bf16)
            d_values[at, cols] = dv.astype(bf16)
        halves = []
        for h in range(2):
            inv = inverse[2 * pr + h : 2 * pr + h + 1, :] * scale
            halves.append((acc[h] * inv)[h * HEAD_DIM : (h + 1) * HEAD_DIM])
        d_query[:, cols] = jnp.concatenate(halves, axis=0).T


def middle(
    meta, ctx_a, ctx_c, mine, theirs, cot_mine, cot_theirs, late, par,
    result, d_r1_out, d_ctx, late_g, norms,
    slope, active, rows32, out_a, out_b,
):
    size = mine.shape[0]
    seq_len = meta.seq_len
    gain0, gain1 = par[KSIZE : KSIZE + 1, :], par[KSIZE + 1 : KSIZE + 2, :]
    bias0, bias1 = par[KSIZE + 2 : KSIZE + 3, :], par[KSIZE + 3 : KSIZE + 4, :]
    near = PARTS // 4
    part = near * UNIT
    count = 4
    outs = (out_a, out_b)

    for g in range(GROUPS):
        span = (g * LATE_ROWS + 2 * UNIT, (g + 1) * LATE_ROWS)
        for v in range(PARTS):
            block = late.rows(span)[v, span[0] : span[1], :].astype(f32)
            rows32[v * ROWS : (v + 1) * ROWS, :] = block[:ROWS]
        outs[g][...] = rows32[...].astype(bf16)

    def rows(g, lo, c):
        span = (g * LATE_ROWS, g * LATE_ROWS + 2 * UNIT)
        lo = g * LATE_ROWS + lo
        return late.rows(span)[c * near : (c + 1) * near, lo : lo + UNIT, :].reshape(part, DA)

    def deal(value, g, lo, c):
        lo = g * LATE_ROWS + lo
        for k in range(near):
            v = c * near + k
            at = meta.sum_place_of(v // 2, v % 2)
            late_g[at, lo : lo + UNIT, :] = value[k * UNIT : (k + 1) * UNIT].astype(bf16)

    ctx = jnp.concatenate([ctx_a[...].astype(bf16), ctx_c[...]], axis=1)
    branch = jnp.concatenate([dot(ctx, t[...]) for t in outs], axis=1)
    tokens = jnp.concatenate([mine[...], theirs[...]], axis=0).astype(f32)
    hat1, inv1 = norm_parts(tokens + branch)
    first = hat1 * gain0 + bias0
    low = first.astype(bf16)
    lows = [low[:, :DA], low[:, DA:]]
    downs = []
    for g in range(GROUPS):
        acc = None
        for c in range(count):
            at = slice(c * part, (c + 1) * part)
            v = dot_nt(lows[g], rows(g, 0, c))
            phi = 0.5 * (1.0 + lax.erf(v * 0.7071067811865476))
            act = (v * phi).astype(bf16)
            active[g, :, at] = act
            slope[g, :, at] = phi + v * (jnp.exp(-0.5 * v * v) * 0.3989422804014327)
            term = dot(act, rows(g, UNIT, c))
            acc = term if acc is None else acc + term
        downs.append(acc)
    hat2, inv2 = norm_parts(first + jnp.concatenate(downs, axis=1))
    result[...] = (hat2 * gain1 + bias1).astype(bf16)
    flush(result)

    row = row_iota((size, D))
    grad = jnp.concatenate(
        [
            jnp.where(row < seq_len - meta.owner(b) * size, t[...].astype(f32), 0.0)
            for b, t in enumerate((cot_mine, cot_theirs))
        ],
        axis=0,
    )
    norms[...] = jnp.zeros(norms.shape, f32)
    norms[1:2, :] = jnp.sum(grad * hat2, axis=0, keepdims=True)
    norms[3:4, :] = jnp.sum(grad, axis=0, keepdims=True)
    d_r2 = norm_back(hat2, inv2, grad, gain1)
    d_down = d_r2.astype(bf16)
    firsts = []
    for g in range(GROUPS):
        dd = d_down[:, g * DA : (g + 1) * DA]
        acc = None
        for c in range(count):
            at = slice(c * part, (c + 1) * part)
            da = dot_nt(dd, rows(g, UNIT, c))
            di = (da * slope[g, :, at]).astype(bf16)
            deal(dot_tn(active[g, :, at], dd), g, UNIT, c)
            deal(dot_tn(di, lows[g]), g, 0, c)
            term = dot(di, rows(g, 0, c))
            acc = term if acc is None else acc + term
        firsts.append(acc)
        late_g.flush((g * LATE_ROWS, g * LATE_ROWS + 2 * UNIT))
    d_first = d_r2 + jnp.concatenate(firsts, axis=1)
    norms[0:1, :] = jnp.sum(d_first * hat1, axis=0, keepdims=True)
    norms[2:3, :] = jnp.sum(d_first, axis=0, keepdims=True)
    d_r1 = norm_back(hat1, inv1, d_first, gain0)
    d_r1_out[...] = d_r1
    flush(d_r1_out)
    d_branch = d_r1.astype(bf16)
    gap = jnp.zeros((32 - ROWS, DA), f32)
    for g in range(GROUPS):
        value = dot_tn(ctx, d_branch[:, g * DA : (g + 1) * DA])
        lo = g * LATE_ROWS + 2 * UNIT
        for v in range(PARTS):
            at = meta.sum_place_of(v // 2, v % 2)
            block = jnp.concatenate([value[v * ROWS : (v + 1) * ROWS], gap], axis=0)
            late_g[at, lo : lo + 32, :] = block.astype(bf16)
    d_context = dot_nt(d_branch[:, :DA], out_a[...]) + dot_nt(d_branch[:, DA:], out_b[...])
    d_ctx[...] = d_context.astype(bf16)


def conv_backward(
    meta, d_ctx, ext, query, conv, depth_out, key_conv, mixed, taps, mats, par, kern,
    d_query, d_ext, g_point, g_c, g_kern, g_depth,
    ext32, conv32, d_kern, d_conv, d_dep,
):
    size = query.shape[0] // 2
    for b in range(2):
        ext32[b] = ext[b].astype(f32)
        conv32[b] = conv[b].astype(f32)
    d_conv[...] = jnp.zeros(d_conv.shape, f32)
    sums = head_sums()
    for j in range(KSIZE):
        for b in range(2):
            lo = PAD - HALF + j
            rows = slice(b * size, (b + 1) * size)
            grad = d_ctx[rows, DA:].astype(f32)
            prod = (grad * conv32[b, lo : lo + size, :]).astype(bf16)
            d_kern[j, rows, :] = dot(prod, sums)
            d_conv[b, lo : lo + size, :] += taps[j, rows, :].astype(f32) * grad
    picks = [tap_pick(j) for j in range(KSIZE)]
    compact = jnp.zeros((2 * size, 128), f32)
    total = jnp.zeros((2 * size, DA), f32)
    for j in range(KSIZE):
        total = total + taps[j].astype(f32) * d_kern[j]
    for j in range(KSIZE):
        dl = (taps[j].astype(f32) * (d_kern[j] - total)).astype(bf16)
        compact = compact + dot(dl, picks[j])
    compact = compact.astype(bf16)
    wide = dot_tn(mixed[...], compact).astype(bf16)
    strips = None
    for odd in range(2):
        r = lax.broadcasted_iota(jnp.int32, (128, 128), 0)
        c = lax.broadcasted_iota(jnp.int32, (128, 128), 1)
        pick = jnp.where((c < STRIP) & (r == c + odd * STRIP), 1.0, 0.0).astype(bf16)
        part = dot(weave(STRIP, odd), dot(wide, pick).astype(bf16))
        strips = part if strips is None else strips + part
    g_kern[...] = strips
    d_mixed = dot_nt(compact, kern[...])
    d_kc = (d_mixed * query[...].astype(f32)).astype(bf16)
    d_query[...] = d_mixed * key_conv[...]
    g_point[...] = dot_tn(depth_out[...], d_kc).astype(bf16)
    d_dep[...] = dot_nt(d_kc, rows_of(mats, 2))
    gc = None
    for b in range(2):
        dc = d_conv[b].astype(bf16)
        d_ext[b] = dot_nt(dc, rows_of(mats, 4))
        part = dot_tn(ext[b], dc)
        gc = part if gc is None else gc + part
    g_c[...] = gc.astype(bf16)
    g_depth[...] = jnp.zeros(g_depth.shape, f32)
    for c in range(0, D, 128):
        cols = slice(c, c + 128)
        for j in range(KSIZE):
            lo = PAD - HALF + j
            acc = jnp.zeros((1, 128), f32)
            for b in range(2):
                dd = d_dep[b * size : (b + 1) * size, cols]
                acc = acc + jnp.sum(dd * ext32[b, lo : lo + size, cols], axis=0, keepdims=True)
                d_ext[b, lo : lo + size, cols] += par[j : j + 1, cols] * dd
            g_depth[j : j + 1, cols] = acc


def project_backward(
    meta, d_keys, d_values, d_query, d_ext, mats, full_a, full_b, more_a, more_b, d_full,
):
    near, size, _ = full_a.shape
    blocks = 2 * near
    chunk = 2 * size
    dq = d_query[...]
    for n in range(blocks // 2):
        at = slice(n * chunk, (n + 1) * chunk)
        both = dot_nt(d_keys[at, :], rows_of(mats, 0))
        both = both + dot_nt(d_values[at, :], rows_of(mats, 3))
        if n == 0:
            both = both + dot_nt(dq, rows_of(mats, 1))
            both = both + jnp.concatenate(
                [d_ext[b, PAD : PAD + size, :] for b in range(2)], axis=0
            )
        d_full[2 * n : 2 * n + 2] = both.astype(bf16).reshape(2, size, D)
    for b in range(2):
        base = meta.owner(b) * size
        before, after = meta.place(meta.owner(b) - 1), meta.place(meta.owner(b) + 1)
        rim = jnp.where(row_iota((PAD, D)) + (base - PAD) >= 0, d_ext[b, :PAD, :], 0.0)
        old = d_full[before, size - PAD :, :].astype(f32)
        d_full[before, size - PAD :, :] = (old + rim).astype(bf16)
        inside = row_iota((PAD, D)) + (base + size) < blocks * size
        rim = jnp.where(inside, d_ext[b, PAD + size :, :], 0.0)
        old = d_full[after, :PAD, :].astype(f32)
        d_full[after, :PAD, :] = (old + rim).astype(bf16)
    for n in range(blocks):
        left, right, at = (full_a, full_b, n) if n < near else (more_a, more_b, n - near)
        rows = d_full[n]
        left[at] = rows[:, :DA]
        right[at] = rows[:, DA:]


def project_grads(
    meta, full_a, full_b, more_a, more_b, d_keys, d_values, ext, d_query, g_point, g_c, g_kern,
    g_depth, norms, keep_a, send_a, keep_b, send_b,
):
    near, size, _ = full_a.shape
    blocks = 2 * near
    even = on_even(meta, (ROWS, DA))
    x = jnp.concatenate(
        [sequence_rows((full_a, full_b, more_a, more_b), n) for n in range(near)], axis=0
    )
    own = jnp.concatenate([ext[b, PAD : PAD + size, :] for b in range(2)], axis=0)
    dq = d_query[...]
    rows = jnp.concatenate(
        [g_depth[:KSIZE, :], norms[:4, :], jnp.zeros((128 - KSIZE - 4, D), f32)], axis=0
    )
    small = jnp.concatenate([rows.T, g_kern[...], jnp.zeros((D, 128), f32)], axis=1)
    g_kv = dot_tn(x, jnp.concatenate([d_keys[...], d_values[...]], axis=1))
    for side, keep, send, values in (
        (0, keep_a, send_a, (g_kv[:, :DA], dot_tn(own, dq), g_point[...].astype(f32))),
        (1, keep_b, send_b, (g_kv[:, DA:], g_c[...].astype(f32), small)),
    ):
        for piece, value in enumerate(values):
            deal_rows(value, lambda k: meta.weight_place(side, k), piece, even, keep, send)


def pack_early(meta, w_in, w_point, kern, w_depth, ln_gain, ln_bias, early, turn):
    for to, at in ((0, 1), (1, 0), (3, 2), (4, 3)):
        early[to] = w_in[:, at * DA : (at + 1) * DA]
    early[2] = w_point[...]
    wide = w_in.shape[0]
    turn[...] = jnp.zeros(turn.shape, f32)
    turn[:KSIZE, :wide] = w_depth[...].astype(f32)
    turn[KSIZE : KSIZE + 2, :wide] = ln_gain[...].astype(f32)
    turn[KSIZE + 2 : KSIZE + 4, :wide] = ln_bias[...].astype(f32)
    small = turn[...].T[:wide]
    early[5] = jnp.zeros(early.shape[1:], bf16)
    early[5, :, :128] = small.astype(bf16)
    early[5, :, 128 : 128 + STRIP] = kern[...]


def pack_late(meta, w_up, w_down, w_out, late):
    wide = w_out.shape[0]
    for g in range(GROUPS):
        lo = g * LATE_ROWS
        late[lo : lo + UNIT, :] = w_up[g]
        late[lo + UNIT : lo + 2 * UNIT, :] = w_down[g]
        out = w_out[:, g * DA : (g + 1) * DA].astype(f32)
        out = jnp.concatenate([out, jnp.zeros((32 - wide, DA), f32)], axis=0)
        late[lo + 2 * UNIT : lo + LATE_ROWS, :] = out.astype(bf16)


def front(
    meta, full_a, full_b, more_a, more_b, own_a, got_a, own_b, got_b,
    query, keys, values, mats, par, kern, probs, inverse, context_a,
    ext, conv, depth_out, key_conv, mixed, taps, context_c,
    rows32, scores, ext32, conv32, logits,
):
    full = (full_a, full_b, more_a, more_b)
    project_forward(
        meta, *full, own_a, got_a, own_b, got_b, query, keys, values, mats, par, kern, rows32
    )
    flush(query, mats)
    attend_forward(meta, query, keys, values, probs, inverse, context_a, scores)
    flush(keys, values, probs, context_a)
    conv_forward(
        meta, *full, mats, par, kern, query, ext, conv, depth_out, key_conv, mixed, taps, context_c,
        ext32, conv32, logits,
    )


def back(
    meta, d_ctx, conv, taps, query, mixed, key_conv, depth_out, mats, ext, context_a, keys, values,
    probs, full_a, full_b, more_a, more_b, inverse, par, kern, norms,
    here_a, here_b, there_a, there_b, keep_a, send_a, keep_b, send_b,
    ext32, conv32, d_kern, d_conv, d_dep, dq_c, dq_a, g_point, g_c, g_kern, g_depth, d_ext, d_query,
    d_full,
):
    conv_backward(
        meta, d_ctx, ext, query, conv, depth_out, key_conv, mixed, taps, mats, par, kern,
        dq_c, d_ext, g_point, g_c, g_kern, g_depth, ext32, conv32, d_kern, d_conv, d_dep,
    )
    attend_backward(
        meta, d_ctx, context_a, query, keys, values, probs, inverse, keys, values, dq_a
    )
    d_query[...] = (dq_a[...] + dq_c[...]).astype(bf16)
    project_backward(
        meta, keys, values, d_query, d_ext, mats, here_a, here_b, there_a, there_b, d_full
    )
    flush(here_a, here_b, there_a, there_b)
    project_grads(
        meta, full_a, full_b, more_a, more_b, keys, values, ext, d_query, g_point, g_c, g_kern,
        g_depth, norms, keep_a, send_a, keep_b, send_b,
    )


def blocks_of(full):
    cut = full.reshape(full.shape[0], PARTS // 2, 2, ROWS, DA).transpose(2, 1, 0, 3, 4)
    return cut[0], cut[1]


def whole_of(keep, send):
    both = jnp.stack([keep, send]).transpose(2, 1, 0, 3, 4)
    return both.reshape(both.shape[0], D, DA)


def gathered(weights):
    dims = (0, 1, 0, 0, 0, 1, 1, 2, 1)
    w_in, w_depth, w_point, w_kern, w_out, gain, bias, w_up, w_down = (
        lax.all_gather(t, AXES, axis=d, tiled=True) for t, d in zip(weights, dims)
    )
    w_q, w_k, w_v, w_c = (w_in[:, i * DA : (i + 1) * DA] for i in range(4))
    small = jnp.concatenate([w_depth.T, gain.T, bias.T], axis=1)
    small = jnp.pad(small, ((0, 0), (0, 128 - small.shape[1])))
    strips = jnp.pad(w_kern.reshape(D, STRIP), ((0, 0), (0, 256 - STRIP)))
    small = jnp.concatenate([small, strips], axis=1)
    early = blocks_of(jnp.stack([w_k, w_q, w_point])) + blocks_of(jnp.stack([w_v, w_c, small]))
    late = []
    for g in range(GROUPS):
        out = w_out[:, g * DA : (g + 1) * DA].reshape(PARTS, ROWS, DA)
        side = jnp.concatenate(
            [
                w_up[g].T.reshape(PARTS, UNIT, DA),
                w_down[g].reshape(PARTS, UNIT, DA),
                jnp.pad(out, ((0, 0), (0, 32 - ROWS), (0, 0))),
            ],
            axis=1,
        )
        late.append(side)
    late = jnp.concatenate(late, axis=1)
    return early, late


def scattered(early_g, late):
    g_k, g_q, g_point = whole_of(*early_g[:2])
    g_v, g_c, g_small = whole_of(*early_g[2:])
    late = late.reshape(PARTS, GROUPS, LATE_ROWS, DA)
    g_up = jnp.stack([late[:, g, :UNIT].reshape(-1, DA).T for g in range(GROUPS)])
    g_down = jnp.stack([late[:, g, UNIT : 2 * UNIT].reshape(-1, DA) for g in range(GROUPS)])
    g_out = jnp.concatenate(
        [late[:, g, 2 * UNIT : 2 * UNIT + ROWS].reshape(D, DA) for g in range(GROUPS)], axis=1
    )
    grads = (
        jnp.concatenate([g_q, g_k, g_v, g_c], axis=1),
        g_small[:, :KSIZE].T,
        g_point,
        g_small[:, 128 : 128 + STRIP].reshape(-1),
        g_out,
        g_small[:, KSIZE : KSIZE + 2].T,
        g_small[:, KSIZE + 2 : KSIZE + 4].T,
        g_up,
        g_down,
    )
    dims = (0, 1, 0, 0, 0, 1, 1, 2, 1)
    return tuple(
        lax.psum_scatter(t.astype(f32), AXES, scatter_dimension=d, tiled=True)
        for t, d in zip(grads, dims)
    )


def per_device(hidden, out_grad, lengths, *weights):
    w_in, w_depth, w_point, w_kern, w_out, ln_gain, ln_bias, w_up, w_down = weights
    length = hidden.shape[2]
    half, grp, mate, core = (lax.axis_index(a) for a in AXES[1:])
    grps = lax.axis_size("grp")
    groups = grps * lax.axis_size("mate")
    wide = w_in.shape[0]
    packed = wide == ROWS and grps == 2 and lax.axis_size("slot") == 2

    mine = lax.dynamic_index_in_dim(hidden[0], half, 0, keepdims=False)
    theirs = lax.dynamic_index_in_dim(hidden[0], 1 - half, 0, keepdims=False)
    seq_len = lax.dynamic_index_in_dim(lengths[0], half, 0, keepdims=False)
    given, theirs = theirs, swap(theirs, "half")
    own_tokens = jnp.stack([mine, theirs])
    count = 4 * groups
    total = count * length
    own = 2 * length
    meta = jnp.stack([seq_len, lax.axis_index("slot"), half, grp, mate, core]).astype(jnp.int32)
    call = functools.partial(kernel_call, form=(grps, packed))

    full, met = [], []
    for i, order in enumerate(routes()):
        rows = own_tokens[..., i * DA : (i + 1) * DA]
        rows = rows.reshape((1,) * len(order) + rows.shape)
        for n, bit in enumerate(order):
            got = swap(rows, *bit)
            if n == 0:
                met.append(got)
            rows = jnp.concatenate([rows, got], axis=routes()[0].index(bit))
        full.append(rows.reshape(-1, length, DA))
    full = full + [swap(t, "core") for t in full]

    if packed:
        one, mark = call(
            pack_early,
            "pack_early",
            jnp.zeros((6,), jnp.int32),
            (w_in, w_point, w_kern.reshape(wide, STRIP), w_depth, ln_gain, ln_bias),
            (((6, wide, DA), bf16),),
            (((128, 128), f32),),
            waits=(given,),
        )
        two, mark = call(
            pack_late,
            "pack_late",
            jnp.zeros((6,), jnp.int32),
            (w_up.transpose(0, 2, 1), w_down, w_out),
            (((GROUPS * LATE_ROWS, DA), bf16),),
            waits=(one,),
        )
        late = lax.all_gather(two, AXES, axis=0)
        one = one[None]
        for bit in first_bits():
            one = gather_bit(one, bit)
        early = []
        for i, order in enumerate(sides()):
            part = one[:, 3 * i : 3 * i + 3]
            for bit in order:
                part = gather_bit(part, bit)
            early += [part, swap(part, "core")]
    else:
        early, late = gathered(weights)
    waits = []
    turn = half
    cot_mine = lax.dynamic_index_in_dim(out_grad[0], turn, 0, keepdims=False)
    cot_theirs = swap(lax.dynamic_index_in_dim(out_grad[0], 1 - turn, 0, keepdims=False), "half")

    tall = length + 2 * PAD
    (
        query, keys, values, mats, par, kern, probs, inverse, context_a,
        ext, conv, depth_out, key_conv, mixed, taps, context_c, mark,
    ) = call(
        front,
        "front",
        meta,
        (*full, *early),
        (
            ((own, DA), bf16),
            ((total, DA), bf16),
            ((total, DA), bf16),
            ((5 * D, DA), bf16),
            ((16, D), f32),
            ((DA, 128), bf16),
            ((HEADS, total, own), bf16),
            ((8, own), f32),
            ((own, DA), f32),
            ((2, tall, D), bf16),
            ((2, tall, DA), bf16),
            ((own, D), bf16),
            ((own, DA), f32),
            ((own, DA), bf16),
            ((KSIZE, own, DA), bf16),
            ((own, DA), bf16),
        ),
        (
            ((D, DA), f32),
            ((total, own), f32),
            ((2, tall, D), f32),
            ((2, tall, DA), f32),
            ((KSIZE, own, DA), f32),
        ),
        flops=4 * (total + own) * D * DA + 16 * own * total * DA + 2 * own * DA * (3 * D + KSIZE * DA),
        exps=HEADS * own * total + KSIZE * own * DA,
        waits=waits,
    )
    cot_theirs = jnp.where(mark == 0, cot_theirs, 0)
    ff = UNIT * PARTS
    spans = tuple(
        (g * LATE_ROWS + lo, g * LATE_ROWS + hi)
        for lo, hi in (OUT_SPAN, FF_SPAN)
        for g in range(GROUPS)
    )
    result, d_r1, d_context, late_g, norms, mark = call(
        middle,
        "middle",
        meta,
        (context_a, context_c, mine, theirs, cot_mine, cot_theirs, late, par),
        (
            ((own, D), bf16),
            ((own, D), f32),
            ((own, D), bf16),
            ((PARTS, GROUPS * LATE_ROWS, DA), bf16),
            ((8, D), f32),
        ),
        (
            ((GROUPS, own, ff), f32),
            ((GROUPS, own, ff), bf16),
            ((D, DA), f32),
            ((D, DA), bf16),
            ((D, DA), bf16),
        ),
        flops=6 * own * (D * D + 4 * D * ff // GROUPS),
        exps=4 * own * ff,
        in_spans={6: spans},
        out_spans={3: spans},
    )
    if packed:
        late_g = lax.psum_scatter(late_g, ("slot", "mate", "core"), scatter_dimension=0, tiled=True)

    early_shape = (PARTS // 2, 3, ROWS, DA)
    *both, mark = call(
        back,
        "back",
        meta,
        (
            d_context, conv, taps, query, mixed, key_conv, depth_out, mats, ext, context_a, keys,
            values, probs, *full, inverse, par, kern, norms,
        ),
        (((2 * groups, length, DA), bf16),) * 4 + ((early_shape, bf16),) * 4,
        (
            ((2, tall, D), f32),
            ((2, tall, DA), f32),
            ((KSIZE, own, DA), f32),
            ((2, tall, DA), f32),
            ((own, D), f32),
            ((own, DA), f32),
            ((own, DA), f32),
            ((D, DA), bf16),
            ((D, DA), bf16),
            ((D, 128), f32),
            ((16, D), f32),
            ((2, tall, D), f32),
            ((own, DA), bf16),
            ((count, length, D), bf16),
        ),
        flops=40 * own * total * DA + 4 * total * D * DA,
    )
    d_full, early_g = both[:4], both[4:]
    res_kept = result[:length]
    res_got = jnp.where(mark == 0, swap(result[length:], "half"), 0)
    if packed:
        sums = []
        for i in range(2):
            got = swap(early_g[2 * i + 1], "core")
            sums.append((early_g[2 * i].astype(f32) + got.astype(f32)).astype(bf16))
    parts = []
    for i, order in enumerate(routes()):
        near = d_full[i].astype(f32) + swap(d_full[2 + i], "core").astype(f32)
        near = near.astype(bf16).reshape(groups, 2, length, DA)
        parts.append(scatter_blocks(near, order))
    d_full = jnp.concatenate(parts, axis=-1).reshape(own, D)
    here = ((half * grps + grp) * 2 + mate) * 2 + core
    there = (((1 - half) * grps + grp) * 2 + mate) * 2 + core
    starts = jnp.stack([here, there]) * length
    own_mask = jnp.arange(length, dtype=jnp.int32)[None] + starts[:, None] < seq_len
    d_hidden = (d_r1 + jnp.where(own_mask.reshape(own, 1), d_full, 0.0)).astype(bf16)

    if packed:
        for i, order in enumerate(sides()):
            for bit in reversed(order):
                sums[i] = scatter_bit(sums[i], bit)
        four = sums[0].shape[0]
        rest = [t.reshape(four, -1, DA) for t in (*sums, late_g)]
        rest = jnp.concatenate(rest, axis=1)
        last = first_bits()[::-1]
        for n, bit in enumerate(last):
            rest = scatter_bit(rest, bit, bf16 if n + 1 < len(last) else f32)
        g_k, g_q, g_point, g_v, g_c, g_small = rest[0, : 6 * ROWS].reshape(6, ROWS, DA)
        late_g = rest[0, 6 * ROWS :]
        late_g = late_g.reshape(GROUPS, LATE_ROWS, DA)
        grads = (
            jnp.concatenate([g_q, g_k, g_v, g_c], axis=1),
            g_small[:, :KSIZE].T,
            g_point,
            g_small[:, 128 : 128 + STRIP].reshape(-1),
            jnp.concatenate([t[2 * UNIT :][:ROWS] for t in late_g], axis=1),
            g_small[:, KSIZE : KSIZE + 2].T,
            g_small[:, KSIZE + 2 : KSIZE + 4].T,
            late_g[:, :UNIT].transpose(0, 2, 1),
            late_g[:, UNIT : 2 * UNIT],
        )
    else:
        grads = scattered(early_g, late_g)

    got = swap(d_hidden[length:], "half")
    kept = d_hidden[:length]

    def in_order(kept, got):
        return jnp.where(half == 0, jnp.stack([kept, got]), jnp.stack([got, kept]))[None]

    return (in_order(res_kept, res_got), in_order(kept, got), *grads)


def solution(mesh):
    slots, seqs = mesh.shape["slot"], mesh.shape["seq"]
    fine = Mesh(mesh.devices.reshape(slots, 2, seqs // 8, 2, 2), AXES)
    seq = AXES[1:]
    placed = (
        P("slot", None, seq, None),
        P("slot", None, seq, None),
        P("slot", None),
        P(AXES, None),
        P(None, AXES),
        P(AXES, None),
        P(AXES),
        P(AXES, None),
        P(None, AXES),
        P(None, AXES),
        P(None, None, AXES),
        P(None, AXES, None),
    )
    return jax.shard_map(
        per_device,
        mesh=fine,
        in_specs=placed,
        out_specs=(placed[0], placed[1]) + placed[3:],
        check_vma=False,
    )
```

```python
import functools
import math

import jax
import jax.numpy as jnp
from jax import lax
from jax.experimental import pallas as pl
from jax.experimental.pallas import tpu as pltpu
from jax.sharding import Mesh, PartitionSpec as P

D = 768
HEADS = 6
HEAD_DIM = 64
KSIZE = 9
GROUPS = 2
DA = 384
HALF = KSIZE // 2
PAD = 16
PARTS = 32
ROWS = D // PARTS
UNIT = 2 * ROWS
OUT_SPAN = (2 * UNIT, 2 * UNIT + 32)
FF_SPAN = (0, 2 * UNIT)
LATE_ROWS = 128
VMEM_LIMIT = 60 << 20

norm_eps = 1e-12
neg_fill = -1e30
bf16 = jnp.bfloat16
f32 = jnp.float32

AXES = ("slot", "half", "grp", "mate", "core")


def swap(value, axis, step=1):
    count = lax.axis_size(axis)
    return lax.ppermute(value, axis, [(i, i ^ step) for i in range(count)])


def bits_of(axis):
    step = lax.axis_size(axis) // 2
    bits = []
    while step >= 1:
        bits.append((axis, step))
        step //= 2
    return bits


def first_bits():
    return bits_of("half") + bits_of("grp")


def sides():
    mate, slot = bits_of("mate"), bits_of("slot")
    return (mate + slot, slot + mate)


def routes():
    bits = bits_of("grp") + bits_of("mate")
    return (bits, bits[::-1])


def gather_bit(arr, bit):
    return jnp.concatenate([arr, swap(arr, *bit)], axis=0)


def scatter_bit(arr, bit, kind=bf16):
    n = arr.shape[0] // 2
    got = swap(arr[n:], *bit)
    return (arr[:n].astype(f32) + got.astype(f32)).astype(kind)


def scatter_blocks(arr, order):
    bits = routes()[0]
    arr = arr.reshape((2,) * len(bits) + arr.shape[1:])
    for n, bit in enumerate(reversed(order)):
        dim = bits.index(bit)
        got = swap(lax.slice_in_dim(arr, 1, 2, axis=dim), *bit)
        arr = lax.slice_in_dim(arr, 0, 1, axis=dim).astype(f32) + got.astype(f32)
        if n + 1 < len(order):
            arr = arr.astype(bf16)
    return arr.reshape(arr.shape[len(bits) :])


def dot(left, right):
    return jnp.dot(left, right, preferred_element_type=f32)


def dot_nt(left, right):
    return lax.dot_general(left, right, (((1,), (1,)), ((), ())), preferred_element_type=f32)


def dot_tn(left, right):
    return lax.dot_general(left, right, (((0,), (0,)), ((), ())), preferred_element_type=f32)


def norm_parts(value):
    centre = value - jnp.mean(value, axis=-1, keepdims=True)
    spread = jnp.mean(centre * centre, axis=-1, keepdims=True)
    inv = lax.rsqrt(spread + norm_eps)
    return centre * inv, inv


def norm_back(hat, inv, grad, gain):
    scaled = grad * gain
    return inv * (
        scaled
        - jnp.mean(scaled, axis=-1, keepdims=True)
        - hat * jnp.mean(scaled * hat, axis=-1, keepdims=True)
    )


class Staged:
    def __init__(self, ref, fetch=(), store=()):
        self.ref, self.fetch, self.store = ref, dict(fetch), dict(store)
        self.flying = []

    @property
    def shape(self):
        return self.ref.shape

    def rows(self, span):
        if span in self.fetch:
            self.fetch.pop(span).wait()
        return self.ref

    def settle(self):
        for span in list(self.fetch):
            self.fetch.pop(span).wait()

    def __getitem__(self, at):
        self.settle()
        return self.ref[at]

    def __setitem__(self, at, value):
        self.ref[at] = value

    def flush(self, *spans):
        for span in spans or list(self.store):
            copy = self.store.pop(span)
            copy.start()
            self.flying.append(copy)

    def finish(self):
        self.flush(*self.store)
        for copy in self.flying:
            copy.wait()


def once(method):
    def found(self, *args):
        key = (method.__name__, *args)
        if key not in self.known:
            self.known[key] = method(self, *args)
        return self.known[key]

    return found


class Numbers:
    def __init__(self, ref, grps, packed):
        self.seq_len = ref[0]
        self.slot, self.half, self.grp, self.mate, self.core = (ref[i] for i in range(1, 6))
        self.grps, self.packed = grps, packed
        self.side = self.core if packed else 0
        self.known = {}

    @once
    def owner(self, n):
        h, m = n % 2, n // 2 % 2
        g, c = n // 4 % self.grps, n // (4 * self.grps)
        left = (self.half ^ h) * self.grps + (self.grp ^ g)
        return (left * 2 + (self.mate ^ m)) * 2 + (self.core ^ c)

    def place(self, block):
        count = 8 * self.grps
        block = jnp.clip(block, 0, count - 1)
        c, m = block & 1, (block >> 1) & 1
        g, h = (block >> 2) & (self.grps - 1), block >> (1 + self.grps.bit_length())
        left = (c ^ self.core) * self.grps + (g ^ self.grp)
        return (left * 2 + (m ^ self.mate)) * 2 + (h ^ self.half)

    @once
    def weight_place(self, which, k):
        if not self.packed:
            return k
        slot, half, grp, mate = (k // 8) % 2, (k // 4) % 2, (k // 2) % 2, k % 2
        slot, half, grp, mate = slot ^ self.slot, half ^ self.half, grp ^ self.grp, mate ^ self.mate
        if which == 0:
            return ((slot * 2 + mate) * 2 + grp) * 2 + half
        return ((mate * 2 + slot) * 2 + grp) * 2 + half

    @once
    def sum_place_of(self, k, core):
        if not self.packed:
            return 2 * k + core
        slot, half, grp, mate = (k // 8) % 2, (k // 4) % 2, (k // 2) % 2, k % 2
        return ((slot * 2 + mate) * 2 + core) * 4 + (grp ^ self.grp) * 2 + (half ^ self.half)


class View:
    def __init__(self, ref, lo, shape, span=None):
        self.ref, self.lo, self.shape, self.span = ref, lo, shape, span

    def find(self, at):
        at = at if isinstance(at, tuple) else (at,)
        lo = self.lo
        if len(self.shape) == 3:
            lo, at = lo + at[0] * self.shape[1], at[1:]
        rows = at[0] if at and at[0] is not Ellipsis else slice(None)
        start, stop, _ = rows.indices(self.shape[-2])
        return (slice(lo + start, lo + stop), *(at[1:] or (slice(None),)))

    def __getitem__(self, at):
        if self.span is not None:
            return self.ref.rows(self.span)[self.find(at)]
        return self.ref[self.find(at)]

    def __setitem__(self, at, value):
        self.ref[self.find(at)] = value


def views(ref, shapes, spans=None):
    found, lo = [], 0
    for i, shape in enumerate(shapes):
        span = None if spans is None else spans[i]
        found.append(View(ref, lo, shape, span))
        lo += math.prod(shape[:-1])
    return found


def flush(*arrays):
    for arr in arrays:
        if isinstance(arr, Staged):
            arr.flush()


def staged(shape, kind):
    return len(shape) > 1 and shape[-2] % 16 == 0 and math.prod(shape) * jnp.dtype(kind).itemsize >= 1 << 17


def kernel_call(body, name, meta, args, outs, scratch=(), flops=0, exps=0, waits=(), form=(), in_spans={}, out_spans={}):
    moved = sum(a.size * a.dtype.itemsize for a in args)
    moved += sum(math.prod(s) * jnp.dtype(d).itemsize for s, d in outs)
    ins_at = [i for i, a in enumerate(args) if staged(a.shape, a.dtype)]
    outs_at = [i for i, (s, d) in enumerate(outs) if staged(s, d)]
    places = [pltpu.VMEM(args[i].shape, args[i].dtype) for i in ins_at]
    places += [pltpu.VMEM(*outs[i]) for i in outs_at]

    def whole(*refs):
        refs = list(refs)

        def take(n):
            got = refs[:n]
            del refs[:n]
            return got

        (numbers,) = take(1)
        ins, _, results = take(len(args)), take(len(waits)), take(len(outs))
        (zero,) = take(1)
        mine = take(len(scratch))
        in_place = dict(zip(ins_at, take(len(ins_at))))
        out_place = dict(zip(outs_at, take(len(outs_at))))
        in_sems, out_sems = take(2)
        zero[0] = 0


        def copies(source, target, spans, sems, n):
            made = {}
            for j, (lo, hi) in enumerate(spans):
                at = (slice(None),) * (len(source.shape) - 2) + (slice(lo, hi),)
                pair = (source.at[at], target.at[at]) if hi else (source, target)
                made[lo, hi] = pltpu.make_async_copy(*pair, sems.at[n, j])
            return made

        fetches = []
        for n, i in enumerate(ins_at):
            made = copies(ins[i], in_place[i], in_spans.get(i, ((0, 0),)), in_sems, n)
            fetches += [(j, copy) for j, copy in enumerate(made.values())]
            ins[i] = Staged(in_place[i], fetch=made)
        for _, copy in sorted(fetches, key=lambda t: t[0]):
            copy.start()
        for n, i in enumerate(outs_at):
            made = copies(out_place[i], results[i], out_spans.get(i, ((0, 0),)), out_sems, n)
            results[i] = Staged(out_place[i], store=made)
        body(Numbers(numbers, *form), *ins, *results, *mine)
        for i in ins_at:
            ins[i].settle()
        for i in outs_at:
            results[i].finish()

    def space(i, chosen):
        return pl.BlockSpec(memory_space=pl.ANY if i in chosen else pltpu.VMEM)

    *results, mark = pl.pallas_call(
        whole,
        out_shape=[jax.ShapeDtypeStruct(s, d) for s, d in outs]
        + [jax.ShapeDtypeStruct((1,), jnp.int32)],
        in_specs=[pl.BlockSpec(memory_space=pltpu.SMEM)]
        + [space(i, ins_at) for i in range(len(args))]
        + [pl.BlockSpec(memory_space=pl.ANY)] * len(waits),
        out_specs=[space(i, outs_at) for i in range(len(outs))]
        + [pl.BlockSpec(memory_space=pltpu.SMEM)],
        scratch_shapes=[pltpu.VMEM(s, d) for s, d in scratch]
        + places
        + [pltpu.SemaphoreType.DMA((max(len(t), 1), 4)) for t in (ins_at, outs_at)],
        compiler_params=pltpu.CompilerParams(vmem_limit_bytes=VMEM_LIMIT),
        cost_estimate=pl.CostEstimate(flops=flops, bytes_accessed=moved, transcendentals=exps),
        name=name,
    )(meta, *args, *waits)
    return *results, mark[0]


def rows_of(ref, piece):
    return ref[piece * D : (piece + 1) * D, :]


def row_iota(shape):
    return lax.broadcasted_iota(jnp.int32, shape, 0)


def head_mask(shape, half):
    lane = lax.broadcasted_iota(jnp.int32, shape, 1)
    return (lane < HEAD_DIM) if half == 0 else (lane >= HEAD_DIM)


def tap_spread(j):
    r = lax.broadcasted_iota(jnp.int32, (128, DA), 0)
    c = lax.broadcasted_iota(jnp.int32, (128, DA), 1)
    hit = jnp.zeros((128, DA), jnp.bool_)
    for h in range(HEADS):
        hit = hit | ((r == h * KSIZE + j) & (c >= h * HEAD_DIM) & (c < (h + 1) * HEAD_DIM))
    return jnp.where(hit, 1.0, 0.0).astype(bf16)


def tap_pick(j):
    r = lax.broadcasted_iota(jnp.int32, (DA, 128), 0)
    c = lax.broadcasted_iota(jnp.int32, (DA, 128), 1)
    hit = jnp.zeros((DA, 128), jnp.bool_)
    for h in range(HEADS):
        hit = hit | ((r == h * HEAD_DIM) & (c == h * KSIZE + j))
    return jnp.where(hit, 1.0, 0.0).astype(bf16)


def head_sums():
    r = lax.broadcasted_iota(jnp.int32, (DA, DA), 0)
    c = lax.broadcasted_iota(jnp.int32, (DA, DA), 1)
    hit = jnp.zeros((DA, DA), jnp.bool_)
    for h in range(HEADS):
        lo, hi = h * HEAD_DIM, (h + 1) * HEAD_DIM
        hit = hit | ((r >= lo) & (r < hi) & (c >= lo) & (c < hi))
    return jnp.where(hit, 1.0, 0.0).astype(bf16)


def on_even(meta, shape):
    return jnp.zeros(shape, jnp.int32) + meta.side == 0


def fill_rows(own, got, at, piece, even, out):
    for k in range(PARTS // 2):
        one, two = own[at(k), piece].astype(f32), got[at(k), piece].astype(f32)
        out[2 * k * ROWS : (2 * k + 1) * ROWS, :] = jnp.where(even, one, two)
        out[(2 * k + 1) * ROWS : (2 * k + 2) * ROWS, :] = jnp.where(even, two, one)


def deal_rows(value, at, piece, even, keep, send):
    for k in range(PARTS // 2):
        one = value[2 * k * ROWS : (2 * k + 1) * ROWS]
        two = value[(2 * k + 1) * ROWS : (2 * k + 2) * ROWS]
        keep[at(k), piece] = jnp.where(even, one, two).astype(bf16)
        send[at(k), piece] = jnp.where(even, two, one).astype(bf16)


def weave(width, odd):
    r = lax.broadcasted_iota(jnp.int32, (D, DA), 0)
    c = lax.broadcasted_iota(jnp.int32, (D, DA), 1)
    return jnp.where(r == 2 * c + odd, 1.0, 0.0).astype(bf16)


def shift_lanes(width, odd):
    r = lax.broadcasted_iota(jnp.int32, (128, 128), 0)
    c = lax.broadcasted_iota(jnp.int32, (128, 128), 1)
    return jnp.where((r < width) & (c == r + odd * width), 1.0, 0.0).astype(bf16)


STRIP = DA * HEADS * KSIZE // D


def conv_forward(
    meta, full_a, full_b, more_a, more_b, mats, par, kern, query, ext, conv, depth_out, key_conv, mixed, taps, context,
    ext32, conv32, logits,
):
    near, size, _ = full_a.shape
    blocks = 2 * near
    seq_len = meta.seq_len

    def slab(place, lo, hi):
        here = jnp.minimum(place, near - 1)
        there = jnp.maximum(place - near, 0)
        pick = jnp.zeros((hi - lo, D), jnp.int32) + place < near
        one = jnp.concatenate([full_a[here, lo:hi, :], full_b[here, lo:hi, :]], axis=1)
        two = jnp.concatenate([more_a[there, lo:hi, :], more_b[there, lo:hi, :]], axis=1)
        return jnp.where(pick, one.astype(f32), two.astype(f32))

    for b in range(2):
        base = meta.owner(b) * size
        head = slab(meta.place(meta.owner(b) - 1), size - PAD, size)
        row = row_iota((PAD, D))
        at = row + (base - PAD)
        head = jnp.where((row >= PAD - HALF) & (at >= 0) & (at < seq_len), head, 0.0)
        tail = slab(meta.place(meta.owner(b) + 1), 0, PAD)
        tail = jnp.where((row < HALF) & (row + (base + size) < seq_len), tail, 0.0)
        body = jnp.concatenate([full_a[b], full_b[b]], axis=1).astype(f32)
        body = jnp.where(row_iota((size, D)) + base < seq_len, body, 0.0)
        ext32[b, :PAD, :] = head
        ext32[b, PAD : PAD + size, :] = body
        ext32[b, PAD + size :, :] = tail
        ext[b] = ext32[b].astype(bf16)
    for b in range(2):
        for c in range(0, D, 128):
            acc = par[0:1, c : c + 128] * ext32[b, PAD - HALF : PAD - HALF + size, c : c + 128]
            for j in range(1, KSIZE):
                lo = PAD - HALF + j
                acc = acc + par[j : j + 1, c : c + 128] * ext32[b, lo : lo + size, c : c + 128]
            depth_out[b * size : (b + 1) * size, c : c + 128] = acc.astype(bf16)
    for b in range(2):
        vals = dot(ext[b], rows_of(mats, 4)).astype(bf16)
        conv[b] = vals
        conv32[b] = vals.astype(f32)
    kc = dot(depth_out[...], rows_of(mats, 2))
    key_conv[...] = kc
    mix = (kc * query[...].astype(f32)).astype(bf16)
    mixed[...] = mix
    for j in range(KSIZE):
        wide = dot(kern[...], tap_spread(j)).astype(bf16)
        logits[j] = dot(mix, wide)
    step = 32
    for r in range(0, 2 * size, step):
        b, o = r // size, r % size
        vals = [logits[j, r : r + step, :] for j in range(KSIZE)]
        top = vals[0]
        for v in vals[1:]:
            top = jnp.maximum(top, v)
        vals = [jnp.exp(v - top) for v in vals]
        total = vals[0]
        for v in vals[1:]:
            total = total + v
        inv = 1.0 / total
        acc = jnp.zeros((step, DA), f32)
        for j in range(KSIZE):
            k = vals[j] * inv
            taps[j, r : r + step, :] = k.astype(bf16)
            lo = PAD - HALF + j + o
            acc = acc + k * conv32[b, lo : lo + step, :]
        context[r : r + step, :] = acc.astype(bf16)


def sequence_rows(parts, n):
    full_a, full_b, more_a, more_b = parts
    near = full_a.shape[0]
    left, right, at = (full_a, full_b, 2 * n) if 2 * n < near else (more_a, more_b, 2 * n - near)
    rows = jnp.concatenate([left[at : at + 2], right[at : at + 2]], axis=2)
    return rows.reshape(-1, D)


def project_forward(
    meta, full_a, full_b, more_a, more_b, own_a, got_a, own_b, got_b,
    query, keys, values, mats, par, kern, rows32,
):
    near, size, _ = full_a.shape
    blocks = 2 * near
    chunk = 2 * size
    seq_len = meta.seq_len
    even = on_even(meta, (ROWS, DA))
    for side, own, got in ((0, own_a, got_a), (1, own_b, got_b)):
        for piece in range(3):
            fill_rows(own, got, lambda k: meta.weight_place(side, k), piece, even, rows32)
            to = side * 3 + piece
            if to < 5:
                mats[to * D : (to + 1) * D, :] = rows32[...].astype(bf16)
    par[...] = rows32[:, :128].T[:16]
    strips = rows32[:, 128:256].astype(bf16)
    wide = None
    for odd in range(2):
        part = dot(dot_tn(weave(STRIP, odd), strips).astype(bf16), shift_lanes(STRIP, odd))
        wide = part if wide is None else wide + part
    kern[...] = wide.astype(bf16)
    for n in range(near):
        x = sequence_rows((full_a, full_b, more_a, more_b), n)
        at = slice(n * chunk, (n + 1) * chunk)
        keys[at, :] = dot(x, rows_of(mats, 0)).astype(bf16)
        values[at, :] = dot(x, rows_of(mats, 3)).astype(bf16)
        if n == 0:
            q = dot(x, rows_of(mats, 1))
            row = row_iota((size, DA))
            for b in range(2):
                part = q[b * size : (b + 1) * size]
                part = jnp.where(row < seq_len - meta.owner(b) * size, part, 0.0)
                query[b * size : (b + 1) * size, :] = part.astype(bf16)


def attend_forward(meta, query, keys, values, inverse, context, scores):
    queries = query.shape[0]
    size = queries // 2
    chunk = min(keys.shape[0], 256)
    count = keys.shape[0] // chunk
    each = chunk // size
    seq_len = meta.seq_len
    inverse[...] = jnp.zeros(inverse.shape, f32)
    row = row_iota((size, queries))
    for pr in range(HEADS // 2):
        cols = slice(pr * 128, (pr + 1) * 128)
        q = query[:, cols].astype(f32) * (HEAD_DIM ** (-0.5))
        halves = []
        for h in range(2):
            qh = jnp.where(head_mask((queries, 128), h), q, 0.0).astype(bf16)
            top = jnp.full((1, queries), neg_fill, f32)
            for n in range(count):
                s = dot_nt(keys[n * chunk : (n + 1) * chunk, cols], qh)
                for i in range(each):
                    part = s[i * size : (i + 1) * size]
                    part = jnp.where(row < seq_len - meta.owner(each * n + i) * size, part, neg_fill)
                    lo = (each * n + i) * size
                    scores[lo : lo + size, :] = part
                    top = jnp.maximum(top, jnp.max(part, axis=0, keepdims=True))
            total = jnp.zeros((1, queries), f32)
            acc = jnp.zeros((128, queries), f32)
            for n in range(count):
                at = slice(n * chunk, (n + 1) * chunk)
                e = jnp.exp(scores[at, :] - top)
                total = total + jnp.sum(e, axis=0, keepdims=True)
                e = e.astype(bf16)
                acc = acc + dot_tn(values[at, cols], e)
            inv = 1.0 / total
            inverse[2 * pr + h : 2 * pr + h + 1, :] = inv
            inverse[8 + 2 * pr + h : 9 + 2 * pr + h, :] = top
            halves.append((acc * inv)[h * HEAD_DIM : (h + 1) * HEAD_DIM])
        context[:, cols] = jnp.concatenate(halves, axis=0).T


def attend_backward(meta, d_ctx, context, query, keys, values, inverse, d_keys, d_values, d_query):
    total, queries = keys.shape[0], query.shape[0]
    size = queries // 2
    chunk = min(total, 512)
    each = chunk // size
    row = row_iota((size, queries))
    scale = HEAD_DIM ** (-0.5)
    for pr in range(HEADS // 2):
        cols = slice(pr * 128, (pr + 1) * 128)
        grads = d_ctx[:, cols].astype(f32)
        prod = grads * context[:, cols]
        q = query[:, cols].astype(f32)
        d_o, d_os, q_s, q_h, deltas = [], [], [], [], []
        for h in range(2):
            mask = head_mask((queries, 128), h)
            inv = inverse[2 * pr + h : 2 * pr + h + 1, :]
            col = jnp.broadcast_to(inv, (128, queries)).T
            d_o.append(jnp.where(mask, grads, 0.0).astype(bf16))
            d_os.append(jnp.where(mask, grads * col, 0.0).astype(bf16))
            q_s.append(jnp.where(mask, q * col * scale, 0.0).astype(bf16))
            q_h.append(jnp.where(mask, q * scale, 0.0).astype(bf16))
            delta = lax.dot_general(
                jnp.ones((8, 128), f32),
                jnp.where(mask, prod, 0.0),
                (((1,), (1,)), ((), ())),
                precision=lax.Precision.HIGHEST,
                preferred_element_type=f32,
            )
            deltas.append(delta[0:1])
        acc = [jnp.zeros((128, queries), f32) for _ in range(2)]
        for n in range(total // chunk):
            at = slice(n * chunk, (n + 1) * chunk)
            k, v = keys[at, cols], values[at, cols]
            dv = jnp.zeros((chunk, 128), f32)
            dk = jnp.zeros((chunk, 128), f32)
            for h in range(2):
                e = jnp.exp(dot_nt(k, q_h[h]) - inverse[8 + 2 * pr + h : 9 + 2 * pr + h, :])
                parts = []
                for i in range(each):
                    inside = row < meta.seq_len - meta.owner(each * n + i) * size
                    parts.append(jnp.where(inside, e[i * size : (i + 1) * size], 0.0))
                e = jnp.concatenate(parts, axis=0).astype(bf16)
                dv = dv + dot(e, d_os[h])
                dp = dot_nt(v, d_o[h])
                ds = (e.astype(f32) * (dp - deltas[h])).astype(bf16)
                dk = dk + dot(ds, q_s[h])
                acc[h] = acc[h] + dot_tn(k, ds)
            d_keys[at, cols] = dk.astype(bf16)
            d_values[at, cols] = dv.astype(bf16)
        halves = []
        for h in range(2):
            inv = inverse[2 * pr + h : 2 * pr + h + 1, :] * scale
            halves.append((acc[h] * inv)[h * HEAD_DIM : (h + 1) * HEAD_DIM])
        d_query[:, cols] = jnp.concatenate(halves, axis=0).T


def middle(
    meta, exact, small, mine, theirs, cot_mine, cot_theirs, late, par,
    result, d_r1_out, d_ctx, late_g, norms,
    slope, active, rows32, out_a, out_b,
):
    size = mine.shape[0]
    seq_len = meta.seq_len
    gain0, gain1 = par[KSIZE : KSIZE + 1, :], par[KSIZE + 1 : KSIZE + 2, :]
    bias0, bias1 = par[KSIZE + 2 : KSIZE + 3, :], par[KSIZE + 3 : KSIZE + 4, :]
    near = PARTS // 4
    part = near * UNIT
    count = 4
    outs = (out_a, out_b)

    for g in range(GROUPS):
        span = (g * LATE_ROWS + 2 * UNIT, (g + 1) * LATE_ROWS)
        for v in range(PARTS):
            block = late.rows(span)[v, span[0] : span[1], :].astype(f32)
            rows32[v * ROWS : (v + 1) * ROWS, :] = block[:ROWS]
        outs[g][...] = rows32[...].astype(bf16)

    def rows(g, lo, c):
        span = (g * LATE_ROWS, g * LATE_ROWS + 2 * UNIT)
        lo = g * LATE_ROWS + lo
        return late.rows(span)[c * near : (c + 1) * near, lo : lo + UNIT, :].reshape(part, DA)

    def deal(value, g, lo, c):
        lo = g * LATE_ROWS + lo
        for k in range(near):
            v = c * near + k
            at = meta.sum_place_of(v // 2, v % 2)
            late_g[at, lo : lo + UNIT, :] = value[k * UNIT : (k + 1) * UNIT].astype(bf16)

    tall = size + 2 * PAD
    lo = 2 * tall + 2 * size
    ctx_a = exact[: 2 * size, :].astype(bf16)
    ctx_c = small[lo : lo + 2 * size, :]
    ctx = jnp.concatenate([ctx_a, ctx_c], axis=1)
    branch = jnp.concatenate([dot(ctx, t[...]) for t in outs], axis=1)
    tokens = jnp.concatenate([mine[...], theirs[...]], axis=0).astype(f32)
    hat1, inv1 = norm_parts(tokens + branch)
    first = hat1 * gain0 + bias0
    low = first.astype(bf16)
    lows = [low[:, :DA], low[:, DA:]]
    downs = []
    for g in range(GROUPS):
        acc = None
        for c in range(count):
            at = slice(c * part, (c + 1) * part)
            v = dot_nt(lows[g], rows(g, 0, c))
            phi = 0.5 * (1.0 + lax.erf(v * 0.7071067811865476))
            act = (v * phi).astype(bf16)
            active[g, :, at] = act
            slope[g, :, at] = phi + v * (jnp.exp(-0.5 * v * v) * 0.3989422804014327)
            term = dot(act, rows(g, UNIT, c))
            acc = term if acc is None else acc + term
        downs.append(acc)
    hat2, inv2 = norm_parts(first + jnp.concatenate(downs, axis=1))
    result[...] = (hat2 * gain1 + bias1).astype(bf16)
    flush(result)

    row = row_iota((size, D))
    grad = jnp.concatenate(
        [
            jnp.where(row < seq_len - meta.owner(b) * size, t[...].astype(f32), 0.0)
            for b, t in enumerate((cot_mine, cot_theirs))
        ],
        axis=0,
    )
    norms[...] = jnp.zeros(norms.shape, f32)
    norms[1:2, :] = jnp.sum(grad * hat2, axis=0, keepdims=True)
    norms[3:4, :] = jnp.sum(grad, axis=0, keepdims=True)
    d_r2 = norm_back(hat2, inv2, grad, gain1)
    d_down = d_r2.astype(bf16)
    firsts = []
    for g in range(GROUPS):
        dd = d_down[:, g * DA : (g + 1) * DA]
        acc = None
        for c in range(count):
            at = slice(c * part, (c + 1) * part)
            da = dot_nt(dd, rows(g, UNIT, c))
            di = (da * slope[g, :, at]).astype(bf16)
            deal(dot_tn(active[g, :, at], dd), g, UNIT, c)
            deal(dot_tn(di, lows[g]), g, 0, c)
            term = dot(di, rows(g, 0, c))
            acc = term if acc is None else acc + term
        firsts.append(acc)
        late_g.flush((g * LATE_ROWS, g * LATE_ROWS + 2 * UNIT))
    d_first = d_r2 + jnp.concatenate(firsts, axis=1)
    norms[0:1, :] = jnp.sum(d_first * hat1, axis=0, keepdims=True)
    norms[2:3, :] = jnp.sum(d_first, axis=0, keepdims=True)
    d_r1 = norm_back(hat1, inv1, d_first, gain0)
    d_r1_out[...] = d_r1
    flush(d_r1_out)
    d_branch = d_r1.astype(bf16)
    gap = jnp.zeros((32 - ROWS, DA), f32)
    for g in range(GROUPS):
        value = dot_tn(ctx, d_branch[:, g * DA : (g + 1) * DA])
        lo = g * LATE_ROWS + 2 * UNIT
        for v in range(PARTS):
            at = meta.sum_place_of(v // 2, v % 2)
            block = jnp.concatenate([value[v * ROWS : (v + 1) * ROWS], gap], axis=0)
            late_g[at, lo : lo + 32, :] = block.astype(bf16)
    d_context = dot_nt(d_branch[:, :DA], out_a[...]) + dot_nt(d_branch[:, DA:], out_b[...])
    d_ctx[...] = d_context.astype(bf16)


def conv_backward(
    meta, d_ctx, ext, query, conv, depth_out, key_conv, mixed, taps, mats, par, kern,
    d_query, d_ext, g_point, g_c, g_kern, g_depth,
    ext32, conv32, d_kern, d_conv, d_dep,
):
    size = query.shape[0] // 2
    for b in range(2):
        ext32[b] = ext[b].astype(f32)
        conv32[b] = conv[b].astype(f32)
    d_conv[...] = jnp.zeros(d_conv.shape, f32)
    sums = head_sums()
    for j in range(KSIZE):
        for b in range(2):
            lo = PAD - HALF + j
            rows = slice(b * size, (b + 1) * size)
            grad = d_ctx[rows, DA:].astype(f32)
            prod = (grad * conv32[b, lo : lo + size, :]).astype(bf16)
            d_kern[j, rows, :] = dot(prod, sums)
            d_conv[b, lo : lo + size, :] += taps[j, rows, :].astype(f32) * grad
    picks = [tap_pick(j) for j in range(KSIZE)]
    compact = jnp.zeros((2 * size, 128), f32)
    total = jnp.zeros((2 * size, DA), f32)
    for j in range(KSIZE):
        total = total + taps[j].astype(f32) * d_kern[j]
    for j in range(KSIZE):
        dl = (taps[j].astype(f32) * (d_kern[j] - total)).astype(bf16)
        compact = compact + dot(dl, picks[j])
    compact = compact.astype(bf16)
    wide = dot_tn(mixed[...], compact).astype(bf16)
    strips = None
    for odd in range(2):
        r = lax.broadcasted_iota(jnp.int32, (128, 128), 0)
        c = lax.broadcasted_iota(jnp.int32, (128, 128), 1)
        pick = jnp.where((c < STRIP) & (r == c + odd * STRIP), 1.0, 0.0).astype(bf16)
        part = dot(weave(STRIP, odd), dot(wide, pick).astype(bf16))
        strips = part if strips is None else strips + part
    g_kern[...] = strips
    d_mixed = dot_nt(compact, kern[...])
    d_kc = (d_mixed * query[...].astype(f32)).astype(bf16)
    d_query[...] = d_mixed * key_conv[...]
    g_point[...] = dot_tn(depth_out[...], d_kc).astype(bf16)
    d_dep[...] = dot_nt(d_kc, rows_of(mats, 2))
    gc = None
    for b in range(2):
        dc = d_conv[b].astype(bf16)
        d_ext[b] = dot_nt(dc, rows_of(mats, 4))
        part = dot_tn(ext[b], dc)
        gc = part if gc is None else gc + part
    g_c[...] = gc.astype(bf16)
    g_depth[...] = jnp.zeros(g_depth.shape, f32)
    for c in range(0, D, 128):
        cols = slice(c, c + 128)
        for j in range(KSIZE):
            lo = PAD - HALF + j
            acc = jnp.zeros((1, 128), f32)
            for b in range(2):
                dd = d_dep[b * size : (b + 1) * size, cols]
                acc = acc + jnp.sum(dd * ext32[b, lo : lo + size, cols], axis=0, keepdims=True)
                d_ext[b, lo : lo + size, cols] += par[j : j + 1, cols] * dd
            g_depth[j : j + 1, cols] = acc


def project_backward(
    meta, d_keys, d_values, d_query, d_ext, mats, full_a, full_b, more_a, more_b, d_full,
):
    near, size, _ = full_a.shape
    blocks = 2 * near
    chunk = 2 * size
    dq = d_query[...]
    for n in range(blocks // 2):
        at = slice(n * chunk, (n + 1) * chunk)
        both = dot_nt(d_keys[at, :], rows_of(mats, 0))
        both = both + dot_nt(d_values[at, :], rows_of(mats, 3))
        if n == 0:
            both = both + dot_nt(dq, rows_of(mats, 1))
            both = both + jnp.concatenate(
                [d_ext[b, PAD : PAD + size, :] for b in range(2)], axis=0
            )
        d_full[2 * n : 2 * n + 2] = both.astype(bf16).reshape(2, size, D)
    for b in range(2):
        base = meta.owner(b) * size
        before, after = meta.place(meta.owner(b) - 1), meta.place(meta.owner(b) + 1)
        rim = jnp.where(row_iota((PAD, D)) + (base - PAD) >= 0, d_ext[b, :PAD, :], 0.0)
        old = d_full[before, size - PAD :, :].astype(f32)
        d_full[before, size - PAD :, :] = (old + rim).astype(bf16)
        inside = row_iota((PAD, D)) + (base + size) < blocks * size
        rim = jnp.where(inside, d_ext[b, PAD + size :, :], 0.0)
        old = d_full[after, :PAD, :].astype(f32)
        d_full[after, :PAD, :] = (old + rim).astype(bf16)
    for n in range(blocks):
        left, right, at = (full_a, full_b, n) if n < near else (more_a, more_b, n - near)
        rows = d_full[n]
        left[at] = rows[:, :DA]
        right[at] = rows[:, DA:]


def project_grads(
    meta, full_a, full_b, more_a, more_b, d_keys, d_values, ext, d_query, g_point, g_c, g_kern,
    g_depth, norms, keep_a, send_a, keep_b, send_b,
):
    near, size, _ = full_a.shape
    blocks = 2 * near
    even = on_even(meta, (ROWS, DA))
    x = jnp.concatenate(
        [sequence_rows((full_a, full_b, more_a, more_b), n) for n in range(near)], axis=0
    )
    own = jnp.concatenate([ext[b, PAD : PAD + size, :] for b in range(2)], axis=0)
    dq = d_query[...]
    rows = jnp.concatenate(
        [g_depth[:KSIZE, :], norms[:4, :], jnp.zeros((128 - KSIZE - 4, D), f32)], axis=0
    )
    small = jnp.concatenate([rows.T, g_kern[...], jnp.zeros((D, 128), f32)], axis=1)
    g_kv = dot_tn(x, jnp.concatenate([d_keys[...], d_values[...]], axis=1))
    for side, keep, send, values in (
        (0, keep_a, send_a, (g_kv[:, :DA], dot_tn(own, dq), g_point[...].astype(f32))),
        (1, keep_b, send_b, (g_kv[:, DA:], g_c[...].astype(f32), small)),
    ):
        for piece, value in enumerate(values):
            deal_rows(value, lambda k: meta.weight_place(side, k), piece, even, keep, send)


def pack_early(meta, w_in, w_point, kern, w_depth, ln_gain, ln_bias, early, turn):
    for to, at in ((0, 1), (1, 0), (3, 2), (4, 3)):
        early[to] = w_in[:, at * DA : (at + 1) * DA]
    early[2] = w_point[...]
    wide = w_in.shape[0]
    turn[...] = jnp.zeros(turn.shape, f32)
    turn[:KSIZE, :wide] = w_depth[...].astype(f32)
    turn[KSIZE : KSIZE + 2, :wide] = ln_gain[...].astype(f32)
    turn[KSIZE + 2 : KSIZE + 4, :wide] = ln_bias[...].astype(f32)
    small = turn[...].T[:wide]
    early[5] = jnp.zeros(early.shape[1:], bf16)
    early[5, :, :128] = small.astype(bf16)
    early[5, :, 128 : 128 + STRIP] = kern[...]


def pack_late(meta, w_up, w_down, w_out, late):
    wide = w_out.shape[0]
    for g in range(GROUPS):
        lo = g * LATE_ROWS
        late[lo : lo + UNIT, :] = w_up[g]
        late[lo + UNIT : lo + 2 * UNIT, :] = w_down[g]
        out = w_out[:, g * DA : (g + 1) * DA].astype(f32)
        out = jnp.concatenate([out, jnp.zeros((32 - wide, DA), f32)], axis=0)
        late[lo + 2 * UNIT : lo + LATE_ROWS, :] = out.astype(bf16)


def kept_shapes(total, own, tall):
    return (
        ((5 * D, DA), (own, DA), (total, DA), (total, DA)),
        ((2, tall, DA), (own, DA), (own, DA), (KSIZE, own, DA)),
        ((2, tall, D), (own, D)),
        ((own, DA), (own, DA)),
    )


def front(
    meta, full_a, full_b, more_a, more_b, own_a, got_a, own_b, got_b,
    proj, small, wide, exact, inverse, par, kern,
    rows32, scores, ext32, conv32, logits,
):
    near, size, _ = full_a.shape
    shapes = kept_shapes(2 * near * size, 2 * size, size + 2 * PAD)
    mats, query, keys, values = views(proj, shapes[0])
    conv, mixed, context_c, taps = views(small, shapes[1])
    ext, depth_out = views(wide, shapes[2])
    context_a, key_conv = views(exact, shapes[3])
    full = (full_a, full_b, more_a, more_b)
    project_forward(
        meta, *full, own_a, got_a, own_b, got_b, query, keys, values, mats, par, kern, rows32
    )
    flush(proj)
    attend_forward(meta, query, keys, values, inverse, context_a, scores)
    conv_forward(
        meta, *full, mats, par, kern, query, ext, conv, depth_out, key_conv, mixed, taps, context_c,
        ext32, conv32, logits,
    )


def back(
    meta, d_ctx, small, wide, exact, proj, full_a, full_b, more_a, more_b, inverse, par, kern, norms,
    here_a, here_b, there_a, there_b, keep_a, send_a, keep_b, send_b,
    ext32, conv32, d_kern, d_conv, d_dep, dq_c, dq_a, g_point, g_c, g_kern, g_depth, d_ext, d_query,
    d_full,
):
    near, size, _ = full_a.shape
    shapes = kept_shapes(2 * near * size, 2 * size, size + 2 * PAD)
    mats, query, keys, values = views(proj, shapes[0])
    conv, mixed, context_c, taps = views(small, shapes[1])
    ext, depth_out = views(wide, shapes[2])
    context_a, key_conv = views(exact, shapes[3])
    conv_backward(
        meta, d_ctx, ext, query, conv, depth_out, key_conv, mixed, taps, mats, par, kern,
        dq_c, d_ext, g_point, g_c, g_kern, g_depth, ext32, conv32, d_kern, d_conv, d_dep,
    )
    attend_backward(
        meta, d_ctx, context_a, query, keys, values, inverse, keys, values, dq_a
    )
    d_query[...] = (dq_a[...] + dq_c[...]).astype(bf16)
    project_backward(
        meta, keys, values, d_query, d_ext, mats, here_a, here_b, there_a, there_b, d_full
    )
    flush(here_a, here_b, there_a, there_b)
    project_grads(
        meta, full_a, full_b, more_a, more_b, keys, values, ext, d_query, g_point, g_c, g_kern,
        g_depth, norms, keep_a, send_a, keep_b, send_b,
    )


def blocks_of(full):
    cut = full.reshape(full.shape[0], PARTS // 2, 2, ROWS, DA).transpose(2, 1, 0, 3, 4)
    return cut[0], cut[1]


def whole_of(keep, send):
    both = jnp.stack([keep, send]).transpose(2, 1, 0, 3, 4)
    return both.reshape(both.shape[0], D, DA)


def gathered(weights):
    dims = (0, 1, 0, 0, 0, 1, 1, 2, 1)
    w_in, w_depth, w_point, w_kern, w_out, gain, bias, w_up, w_down = (
        lax.all_gather(t, AXES, axis=d, tiled=True) for t, d in zip(weights, dims)
    )
    w_q, w_k, w_v, w_c = (w_in[:, i * DA : (i + 1) * DA] for i in range(4))
    small = jnp.concatenate([w_depth.T, gain.T, bias.T], axis=1)
    small = jnp.pad(small, ((0, 0), (0, 128 - small.shape[1])))
    strips = jnp.pad(w_kern.reshape(D, STRIP), ((0, 0), (0, 256 - STRIP)))
    small = jnp.concatenate([small, strips], axis=1)
    early = blocks_of(jnp.stack([w_k, w_q, w_point])) + blocks_of(jnp.stack([w_v, w_c, small]))
    late = []
    for g in range(GROUPS):
        out = w_out[:, g * DA : (g + 1) * DA].reshape(PARTS, ROWS, DA)
        side = jnp.concatenate(
            [
                w_up[g].T.reshape(PARTS, UNIT, DA),
                w_down[g].reshape(PARTS, UNIT, DA),
                jnp.pad(out, ((0, 0), (0, 32 - ROWS), (0, 0))),
            ],
            axis=1,
        )
        late.append(side)
    late = jnp.concatenate(late, axis=1)
    return early, late


def scattered(early_g, late):
    g_k, g_q, g_point = whole_of(*early_g[:2])
    g_v, g_c, g_small = whole_of(*early_g[2:])
    late = late.reshape(PARTS, GROUPS, LATE_ROWS, DA)
    g_up = jnp.stack([late[:, g, :UNIT].reshape(-1, DA).T for g in range(GROUPS)])
    g_down = jnp.stack([late[:, g, UNIT : 2 * UNIT].reshape(-1, DA) for g in range(GROUPS)])
    g_out = jnp.concatenate(
        [late[:, g, 2 * UNIT : 2 * UNIT + ROWS].reshape(D, DA) for g in range(GROUPS)], axis=1
    )
    grads = (
        jnp.concatenate([g_q, g_k, g_v, g_c], axis=1),
        g_small[:, :KSIZE].T,
        g_point,
        g_small[:, 128 : 128 + STRIP].reshape(-1),
        g_out,
        g_small[:, KSIZE : KSIZE + 2].T,
        g_small[:, KSIZE + 2 : KSIZE + 4].T,
        g_up,
        g_down,
    )
    dims = (0, 1, 0, 0, 0, 1, 1, 2, 1)
    return tuple(
        lax.psum_scatter(t.astype(f32), AXES, scatter_dimension=d, tiled=True)
        for t, d in zip(grads, dims)
    )


def per_device(hidden, out_grad, lengths, *weights):
    w_in, w_depth, w_point, w_kern, w_out, ln_gain, ln_bias, w_up, w_down = weights
    length = hidden.shape[2]
    half, grp, mate, core = (lax.axis_index(a) for a in AXES[1:])
    grps = lax.axis_size("grp")
    groups = grps * lax.axis_size("mate")
    wide = w_in.shape[0]
    packed = wide == ROWS and grps == 2 and lax.axis_size("slot") == 2

    mine = lax.dynamic_index_in_dim(hidden[0], half, 0, keepdims=False)
    theirs = lax.dynamic_index_in_dim(hidden[0], 1 - half, 0, keepdims=False)
    seq_len = lax.dynamic_index_in_dim(lengths[0], half, 0, keepdims=False)
    given, theirs = theirs, swap(theirs, "half")
    own_tokens = jnp.stack([mine, theirs])
    count = 4 * groups
    total = count * length
    own = 2 * length
    meta = jnp.stack([seq_len, lax.axis_index("slot"), half, grp, mate, core]).astype(jnp.int32)
    call = functools.partial(kernel_call, form=(grps, packed))

    full, met = [], []
    for i, order in enumerate((routes()[1],) * 2):
        rows = own_tokens[..., i * DA : (i + 1) * DA]
        rows = rows.reshape((1,) * len(order) + rows.shape)
        for n, bit in enumerate(order):
            got = swap(rows, *bit)
            if n == 0:
                met.append(got)
            rows = jnp.concatenate([rows, got], axis=routes()[0].index(bit))
        full.append(rows.reshape(-1, length, DA))
    full = full + [swap(t, "core") for t in full]

    if packed:
        one, mark = call(
            pack_early,
            "pack_early",
            jnp.zeros((6,), jnp.int32),
            (w_in, w_point, w_kern.reshape(wide, STRIP), w_depth, ln_gain, ln_bias),
            (((6, wide, DA), bf16),),
            (((128, 128), f32),),
            waits=(given,),
        )
        two, mark = call(
            pack_late,
            "pack_late",
            jnp.zeros((6,), jnp.int32),
            (w_up.transpose(0, 2, 1), w_down, w_out),
            (((GROUPS * LATE_ROWS, DA), bf16),),
            waits=(one,),
        )
        late = lax.all_gather(two, AXES, axis=0)
        one = one[None]
        for bit in first_bits():
            one = gather_bit(one, bit)
        early = []
        for i, order in enumerate(sides()):
            part = one[:, 3 * i : 3 * i + 3]
            for bit in order:
                part = gather_bit(part, bit)
            early += [part, swap(part, "core")]
    else:
        early, late = gathered(weights)
    waits = []
    turn = half
    cot_mine = lax.dynamic_index_in_dim(out_grad[0], turn, 0, keepdims=False)
    cot_theirs = swap(lax.dynamic_index_in_dim(out_grad[0], 1 - turn, 0, keepdims=False), "half")

    tall = length + 2 * PAD
    kept = kept_shapes(total, own, tall)

    def together(shapes, kind):
        return ((sum(math.prod(t[:-1]) for t in shapes), shapes[0][-1]), kind)

    proj, small, wide_rows, exact, inverse, par, kern, mark = call(
        front,
        "front",
        meta,
        (*full, *early),
        (
            *(together(t, kind) for t, kind in zip(kept, (bf16, bf16, bf16, f32))),
            ((16, own), f32),
            ((16, D), f32),
            ((DA, 128), bf16),
        ),
        (
            ((D, DA), f32),
            ((total, own), f32),
            ((2, tall, D), f32),
            ((2, tall, DA), f32),
            ((KSIZE, own, DA), f32),
        ),
        flops=4 * (total + own) * D * DA + 16 * own * total * DA + 2 * own * DA * (3 * D + KSIZE * DA),
        exps=HEADS * own * total + KSIZE * own * DA,
        waits=waits,
    )
    ff = UNIT * PARTS
    spans = tuple(
        (g * LATE_ROWS + lo, g * LATE_ROWS + hi)
        for lo, hi in (OUT_SPAN, FF_SPAN)
        for g in range(GROUPS)
    )
    result, d_r1, d_context, late_g, norms, mark = call(
        middle,
        "middle",
        meta,
        (exact, small, mine, theirs, cot_mine, cot_theirs, late, par),
        (
            ((own, D), bf16),
            ((own, D), f32),
            ((own, D), bf16),
            ((PARTS, GROUPS * LATE_ROWS, DA), bf16),
            ((8, D), f32),
        ),
        (
            ((GROUPS, own, ff), f32),
            ((GROUPS, own, ff), bf16),
            ((D, DA), f32),
            ((D, DA), bf16),
            ((D, DA), bf16),
        ),
        flops=6 * own * (D * D + 4 * D * ff // GROUPS),
        exps=4 * own * ff,
        in_spans={0: ((0, own),), 1: ((2 * tall + own, 2 * tall + 2 * own),), 6: spans},
        out_spans={3: spans},
    )
    if packed:
        late_g = lax.psum_scatter(late_g, ("slot", "mate", "core"), scatter_dimension=0, tiled=True)

    early_shape = (PARTS // 2, 3, ROWS, DA)
    *both, mark = call(
        back,
        "back",
        meta,
        (
            d_context, small, wide_rows, exact, proj, *full, inverse, par, kern, norms,
        ),
        (((2 * groups, length, DA), bf16),) * 4 + ((early_shape, bf16),) * 4,
        (
            ((2, tall, D), f32),
            ((2, tall, DA), f32),
            ((KSIZE, own, DA), f32),
            ((2, tall, DA), f32),
            ((own, D), f32),
            ((own, DA), f32),
            ((own, DA), f32),
            ((D, DA), bf16),
            ((D, DA), bf16),
            ((D, 128), f32),
            ((16, D), f32),
            ((2, tall, D), f32),
            ((own, DA), bf16),
            ((count, length, D), bf16),
        ),
        flops=40 * own * total * DA + 4 * total * D * DA,
    )
    d_full, early_g = both[:4], both[4:]
    res_kept = result[:length]
    res_got = jnp.where(mark == 0, swap(result[length:], "half"), 0)
    if packed:
        sums = []
        for i in range(2):
            got = swap(early_g[2 * i + 1], "core")
            sums.append((early_g[2 * i].astype(f32) + got.astype(f32)).astype(bf16))
    parts = []
    for i, order in enumerate(routes()):
        near = d_full[i].astype(f32) + swap(d_full[2 + i], "core").astype(f32)
        near = near.astype(bf16).reshape(groups, 2, length, DA)
        parts.append(scatter_blocks(near, routes()[1]))
    d_full = jnp.concatenate(parts, axis=-1).reshape(own, D)
    here = ((half * grps + grp) * 2 + mate) * 2 + core
    there = (((1 - half) * grps + grp) * 2 + mate) * 2 + core
    starts = jnp.stack([here, there]) * length
    own_mask = jnp.arange(length, dtype=jnp.int32)[None] + starts[:, None] < seq_len
    d_hidden = (d_r1 + jnp.where(own_mask.reshape(own, 1), d_full, 0.0)).astype(bf16)

    if packed:
        for i, order in enumerate(sides()):
            for bit in reversed(order):
                sums[i] = scatter_bit(sums[i], bit)
        four = sums[0].shape[0]
        rest = [t.reshape(four, -1, DA) for t in (*sums, late_g)]
        rest = jnp.concatenate(rest, axis=1)
        last = first_bits()[::-1]
        for n, bit in enumerate(last):
            rest = scatter_bit(rest, bit, bf16 if n + 1 < len(last) else f32)
        g_k, g_q, g_point, g_v, g_c, g_small = rest[0, : 6 * ROWS].reshape(6, ROWS, DA)
        late_g = rest[0, 6 * ROWS :]
        late_g = late_g.reshape(GROUPS, LATE_ROWS, DA)
        grads = (
            jnp.concatenate([g_q, g_k, g_v, g_c], axis=1),
            g_small[:, :KSIZE].T,
            g_point,
            g_small[:, 128 : 128 + STRIP].reshape(-1),
            jnp.concatenate([t[2 * UNIT :][:ROWS] for t in late_g], axis=1),
            g_small[:, KSIZE : KSIZE + 2].T,
            g_small[:, KSIZE + 2 : KSIZE + 4].T,
            late_g[:, :UNIT].transpose(0, 2, 1),
            late_g[:, UNIT : 2 * UNIT],
        )
    else:
        grads = scattered(early_g, late_g)

    got = swap(d_hidden[length:], "half")
    kept = d_hidden[:length]

    def in_order(kept, got):
        return jnp.where(half == 0, jnp.stack([kept, got]), jnp.stack([got, kept]))[None]

    return (in_order(res_kept, res_got), in_order(kept, got), *grads)


def solution(mesh):
    slots, seqs = mesh.shape["slot"], mesh.shape["seq"]
    fine = Mesh(mesh.devices.reshape(slots, 2, seqs // 8, 2, 2), AXES)
    seq = AXES[1:]
    placed = (
        P("slot", None, seq, None),
        P("slot", None, seq, None),
        P("slot", None),
        P(AXES, None),
        P(None, AXES),
        P(AXES, None),
        P(AXES),
        P(AXES, None),
        P(None, AXES),
        P(None, AXES),
        P(None, None, AXES),
        P(None, AXES, None),
    )
    return jax.shard_map(
        per_device,
        mesh=fine,
        in_specs=placed,
        out_specs=(placed[0], placed[1]) + placed[3:],
        check_vma=False,
    )
```

```python
import functools
import math

import jax
import jax.numpy as jnp
from jax import lax
from jax.experimental import pallas as pl
from jax.experimental.pallas import tpu as pltpu
from jax.sharding import Mesh, PartitionSpec as P

D = 768
HEADS = 6
HEAD_DIM = 64
KSIZE = 9
GROUPS = 2
DA = 384
HALF = KSIZE // 2
PAD = 16
PARTS = 32
ROWS = D // PARTS
UNIT = 2 * ROWS
OUT_SPAN = (2 * UNIT, 2 * UNIT + 32)
FF_SPAN = (0, 2 * UNIT)
LATE_ROWS = 128
VMEM_LIMIT = 60 << 20

norm_eps = 1e-12
neg_fill = -1e30
bf16 = jnp.bfloat16
f32 = jnp.float32

AXES = ("slot", "half", "grp", "mate", "core")


def swap(value, axis, step=1):
    count = lax.axis_size(axis)
    return lax.ppermute(value, axis, [(i, i ^ step) for i in range(count)])


def bits_of(axis):
    step = lax.axis_size(axis) // 2
    bits = []
    while step >= 1:
        bits.append((axis, step))
        step //= 2
    return bits


def first_bits():
    return bits_of("half") + bits_of("grp")


def sides():
    mate, slot = bits_of("mate"), bits_of("slot")
    return (slot + mate, mate + slot)


def routes():
    bits = bits_of("grp") + bits_of("mate")
    return (bits, bits[::-1])


def gather_bit(arr, bit):
    return jnp.concatenate([arr, swap(arr, *bit)], axis=0)


def scatter_bit(arr, bit, kind=bf16):
    n = arr.shape[0] // 2
    got = swap(arr[n:], *bit)
    return (arr[:n].astype(f32) + got.astype(f32)).astype(kind)


def scatter_blocks(arr, order):
    bits = routes()[0]
    arr = arr.reshape((2,) * len(bits) + arr.shape[1:])
    for n, bit in enumerate(reversed(order)):
        dim = bits.index(bit)
        got = swap(lax.slice_in_dim(arr, 1, 2, axis=dim), *bit)
        arr = lax.slice_in_dim(arr, 0, 1, axis=dim).astype(f32) + got.astype(f32)
        if n + 1 < len(order):
            arr = arr.astype(bf16)
    return arr.reshape(arr.shape[len(bits) :])


def dot(left, right):
    return jnp.dot(left, right, preferred_element_type=f32)


def dot_nt(left, right):
    return lax.dot_general(left, right, (((1,), (1,)), ((), ())), preferred_element_type=f32)


def dot_tn(left, right):
    return lax.dot_general(left, right, (((0,), (0,)), ((), ())), preferred_element_type=f32)


def norm_parts(value):
    centre = value - jnp.mean(value, axis=-1, keepdims=True)
    spread = jnp.mean(centre * centre, axis=-1, keepdims=True)
    inv = lax.rsqrt(spread + norm_eps)
    return centre * inv, inv


def norm_back(hat, inv, grad, gain):
    scaled = grad * gain
    return inv * (
        scaled
        - jnp.mean(scaled, axis=-1, keepdims=True)
        - hat * jnp.mean(scaled * hat, axis=-1, keepdims=True)
    )


class Staged:
    def __init__(self, ref, fetch=(), store=()):
        self.ref, self.fetch, self.store = ref, dict(fetch), dict(store)
        self.flying = []

    @property
    def shape(self):
        return self.ref.shape

    def rows(self, span):
        if span in self.fetch:
            self.fetch.pop(span).wait()
        return self.ref

    def settle(self):
        for span in list(self.fetch):
            self.fetch.pop(span).wait()

    def __getitem__(self, at):
        self.settle()
        return self.ref[at]

    def __setitem__(self, at, value):
        self.ref[at] = value

    def flush(self, *spans):
        for span in spans or list(self.store):
            copy = self.store.pop(span)
            copy.start()
            self.flying.append(copy)

    def finish(self):
        self.flush(*self.store)
        for copy in self.flying:
            copy.wait()


def once(method):
    def found(self, *args):
        key = (method.__name__, *args)
        if key not in self.known:
            self.known[key] = method(self, *args)
        return self.known[key]

    return found


class Numbers:
    def __init__(self, ref, grps, packed):
        self.seq_len = ref[0]
        self.slot, self.half, self.grp, self.mate, self.core = (ref[i] for i in range(1, 6))
        self.grps, self.packed = grps, packed
        self.side = self.core if packed else 0
        self.known = {}

    @once
    def owner(self, n):
        h, m = n % 2, n // 2 % 2
        g, c = n // 4 % self.grps, n // (4 * self.grps)
        left = (self.half ^ h) * self.grps + (self.grp ^ g)
        return (left * 2 + (self.mate ^ m)) * 2 + (self.core ^ c)

    def place(self, block):
        count = 8 * self.grps
        block = jnp.clip(block, 0, count - 1)
        c, m = block & 1, (block >> 1) & 1
        g, h = (block >> 2) & (self.grps - 1), block >> (1 + self.grps.bit_length())
        left = (c ^ self.core) * self.grps + (g ^ self.grp)
        return (left * 2 + (m ^ self.mate)) * 2 + (h ^ self.half)

    @once
    def weight_place(self, which, k):
        if not self.packed:
            return k
        slot, half, grp, mate = (k // 8) % 2, (k // 4) % 2, (k // 2) % 2, k % 2
        slot, half, grp, mate = slot ^ self.slot, half ^ self.half, grp ^ self.grp, mate ^ self.mate
        if which == 1:
            return ((slot * 2 + mate) * 2 + grp) * 2 + half
        return ((mate * 2 + slot) * 2 + grp) * 2 + half

    @once
    def sum_place_of(self, k, core):
        if not self.packed:
            return 2 * k + core
        slot, half, grp, mate = (k // 8) % 2, (k // 4) % 2, (k // 2) % 2, k % 2
        return ((slot * 2 + mate) * 2 + core) * 4 + (grp ^ self.grp) * 2 + (half ^ self.half)


class View:
    def __init__(self, ref, lo, shape, span=None):
        self.ref, self.lo, self.shape, self.span = ref, lo, shape, span

    def find(self, at):
        at = at if isinstance(at, tuple) else (at,)
        lo = self.lo
        if len(self.shape) == 3:
            lo, at = lo + at[0] * self.shape[1], at[1:]
        rows = at[0] if at and at[0] is not Ellipsis else slice(None)
        start, stop, _ = rows.indices(self.shape[-2])
        return (slice(lo + start, lo + stop), *(at[1:] or (slice(None),)))

    def __getitem__(self, at):
        if self.span is not None:
            return self.ref.rows(self.span)[self.find(at)]
        return self.ref[self.find(at)]

    def __setitem__(self, at, value):
        self.ref[self.find(at)] = value


def views(ref, shapes, spans=None):
    found, lo = [], 0
    for i, shape in enumerate(shapes):
        span = None if spans is None else spans[i]
        found.append(View(ref, lo, shape, span))
        lo += math.prod(shape[:-1])
    return found


def flush(*arrays):
    for arr in arrays:
        if isinstance(arr, Staged):
            arr.flush()


def staged(shape, kind):
    return len(shape) > 1 and shape[-2] % 16 == 0 and math.prod(shape) * jnp.dtype(kind).itemsize >= 1 << 17


def kernel_call(body, name, meta, args, outs, scratch=(), flops=0, exps=0, waits=(), form=(), in_spans={}, out_spans={}):
    moved = sum(a.size * a.dtype.itemsize for a in args)
    moved += sum(math.prod(s) * jnp.dtype(d).itemsize for s, d in outs)
    ins_at = [i for i, a in enumerate(args) if staged(a.shape, a.dtype)]
    outs_at = [i for i, (s, d) in enumerate(outs) if staged(s, d)]
    places = [pltpu.VMEM(args[i].shape, args[i].dtype) for i in ins_at]
    places += [pltpu.VMEM(*outs[i]) for i in outs_at]

    def whole(*refs):
        refs = list(refs)

        def take(n):
            got = refs[:n]
            del refs[:n]
            return got

        (numbers,) = take(1)
        ins, _, results = take(len(args)), take(len(waits)), take(len(outs))
        (zero,) = take(1)
        mine = take(len(scratch))
        in_place = dict(zip(ins_at, take(len(ins_at))))
        out_place = dict(zip(outs_at, take(len(outs_at))))
        in_sems, out_sems = take(2)
        zero[0] = 0


        def copies(source, target, spans, sems, n):
            made = {}
            for j, (lo, hi) in enumerate(spans):
                at = (slice(None),) * (len(source.shape) - 2) + (slice(lo, hi),)
                pair = (source.at[at], target.at[at]) if hi else (source, target)
                made[lo, hi] = pltpu.make_async_copy(*pair, sems.at[n, j])
            return made

        fetches = []
        for n, i in enumerate(ins_at):
            made = copies(ins[i], in_place[i], in_spans.get(i, ((0, 0),)), in_sems, n)
            fetches += [(j, copy) for j, copy in enumerate(made.values())]
            ins[i] = Staged(in_place[i], fetch=made)
        for _, copy in sorted(fetches, key=lambda t: t[0]):
            copy.start()
        for n, i in enumerate(outs_at):
            made = copies(out_place[i], results[i], out_spans.get(i, ((0, 0),)), out_sems, n)
            results[i] = Staged(out_place[i], store=made)
        body(Numbers(numbers, *form), *ins, *results, *mine)
        for i in ins_at:
            ins[i].settle()
        for i in outs_at:
            results[i].finish()

    def space(i, chosen):
        return pl.BlockSpec(memory_space=pl.ANY if i in chosen else pltpu.VMEM)

    *results, mark = pl.pallas_call(
        whole,
        out_shape=[jax.ShapeDtypeStruct(s, d) for s, d in outs]
        + [jax.ShapeDtypeStruct((1,), jnp.int32)],
        in_specs=[pl.BlockSpec(memory_space=pltpu.SMEM)]
        + [space(i, ins_at) for i in range(len(args))]
        + [pl.BlockSpec(memory_space=pl.ANY)] * len(waits),
        out_specs=[space(i, outs_at) for i in range(len(outs))]
        + [pl.BlockSpec(memory_space=pltpu.SMEM)],
        scratch_shapes=[pltpu.VMEM(s, d) for s, d in scratch]
        + places
        + [pltpu.SemaphoreType.DMA((max(len(t), 1), 4)) for t in (ins_at, outs_at)],
        compiler_params=pltpu.CompilerParams(vmem_limit_bytes=VMEM_LIMIT),
        cost_estimate=pl.CostEstimate(flops=flops, bytes_accessed=moved, transcendentals=exps),
        name=name,
    )(meta, *args, *waits)
    return *results, mark[0]


def rows_of(ref, piece):
    return ref[piece * D : (piece + 1) * D, :]


def row_iota(shape):
    return lax.broadcasted_iota(jnp.int32, shape, 0)


def head_mask(shape, half):
    lane = lax.broadcasted_iota(jnp.int32, shape, 1)
    return (lane < HEAD_DIM) if half == 0 else (lane >= HEAD_DIM)


def tap_spread(j):
    r = lax.broadcasted_iota(jnp.int32, (128, DA), 0)
    c = lax.broadcasted_iota(jnp.int32, (128, DA), 1)
    hit = jnp.zeros((128, DA), jnp.bool_)
    for h in range(HEADS):
        hit = hit | ((r == h * KSIZE + j) & (c >= h * HEAD_DIM) & (c < (h + 1) * HEAD_DIM))
    return jnp.where(hit, 1.0, 0.0).astype(bf16)


def tap_pick(j):
    r = lax.broadcasted_iota(jnp.int32, (DA, 128), 0)
    c = lax.broadcasted_iota(jnp.int32, (DA, 128), 1)
    hit = jnp.zeros((DA, 128), jnp.bool_)
    for h in range(HEADS):
        hit = hit | ((r == h * HEAD_DIM) & (c == h * KSIZE + j))
    return jnp.where(hit, 1.0, 0.0).astype(bf16)


def head_sums():
    r = lax.broadcasted_iota(jnp.int32, (DA, DA), 0)
    c = lax.broadcasted_iota(jnp.int32, (DA, DA), 1)
    hit = jnp.zeros((DA, DA), jnp.bool_)
    for h in range(HEADS):
        lo, hi = h * HEAD_DIM, (h + 1) * HEAD_DIM
        hit = hit | ((r >= lo) & (r < hi) & (c >= lo) & (c < hi))
    return jnp.where(hit, 1.0, 0.0).astype(bf16)


def on_even(meta, shape):
    return jnp.zeros(shape, jnp.int32) + meta.side == 0


def fill_rows(own, got, at, piece, even, out):
    for k in range(PARTS // 2):
        one, two = own[at(k), piece].astype(f32), got[at(k), piece].astype(f32)
        out[2 * k * ROWS : (2 * k + 1) * ROWS, :] = jnp.where(even, one, two)
        out[(2 * k + 1) * ROWS : (2 * k + 2) * ROWS, :] = jnp.where(even, two, one)


def deal_rows(value, at, piece, even, keep, send):
    for k in range(PARTS // 2):
        one = value[2 * k * ROWS : (2 * k + 1) * ROWS]
        two = value[(2 * k + 1) * ROWS : (2 * k + 2) * ROWS]
        keep[at(k), piece] = jnp.where(even, one, two).astype(bf16)
        send[at(k), piece] = jnp.where(even, two, one).astype(bf16)


def weave(width, odd):
    r = lax.broadcasted_iota(jnp.int32, (D, DA), 0)
    c = lax.broadcasted_iota(jnp.int32, (D, DA), 1)
    return jnp.where(r == 2 * c + odd, 1.0, 0.0).astype(bf16)


def shift_lanes(width, odd):
    r = lax.broadcasted_iota(jnp.int32, (128, 128), 0)
    c = lax.broadcasted_iota(jnp.int32, (128, 128), 1)
    return jnp.where((r < width) & (c == r + odd * width), 1.0, 0.0).astype(bf16)


STRIP = DA * HEADS * KSIZE // D


def conv_forward(
    meta, full_a, full_b, more_a, more_b, mats, par, kern, query, ext, conv, depth_out, key_conv, mixed, taps, context,
    ext32, conv32, logits,
):
    near, size, _ = full_a.shape
    blocks = 2 * near
    seq_len = meta.seq_len

    def slab(place, lo, hi):
        here = jnp.minimum(place, near - 1)
        there = jnp.maximum(place - near, 0)
        pick = jnp.zeros((hi - lo, D), jnp.int32) + place < near
        one = jnp.concatenate([full_a[here, lo:hi, :], full_b[here, lo:hi, :]], axis=1)
        two = jnp.concatenate([more_a[there, lo:hi, :], more_b[there, lo:hi, :]], axis=1)
        return jnp.where(pick, one.astype(f32), two.astype(f32))

    for b in range(2):
        base = meta.owner(b) * size
        head = slab(meta.place(meta.owner(b) - 1), size - PAD, size)
        row = row_iota((PAD, D))
        at = row + (base - PAD)
        head = jnp.where((row >= PAD - HALF) & (at >= 0) & (at < seq_len), head, 0.0)
        tail = slab(meta.place(meta.owner(b) + 1), 0, PAD)
        tail = jnp.where((row < HALF) & (row + (base + size) < seq_len), tail, 0.0)
        body = jnp.concatenate([full_a[b], full_b[b]], axis=1).astype(f32)
        body = jnp.where(row_iota((size, D)) + base < seq_len, body, 0.0)
        ext32[b, :PAD, :] = head
        ext32[b, PAD : PAD + size, :] = body
        ext32[b, PAD + size :, :] = tail
        ext[b] = ext32[b].astype(bf16)
    for b in range(2):
        for c in range(0, D, 128):
            acc = par[0:1, c : c + 128] * ext32[b, PAD - HALF : PAD - HALF + size, c : c + 128]
            for j in range(1, KSIZE):
                lo = PAD - HALF + j
                acc = acc + par[j : j + 1, c : c + 128] * ext32[b, lo : lo + size, c : c + 128]
            depth_out[b * size : (b + 1) * size, c : c + 128] = acc.astype(bf16)
    for b in range(2):
        vals = dot(ext[b], rows_of(mats, 4)).astype(bf16)
        conv[b] = vals
        conv32[b] = vals.astype(f32)
    kc = dot(depth_out[...], rows_of(mats, 2))
    key_conv[...] = kc
    mix = (kc * query[...].astype(f32)).astype(bf16)
    mixed[...] = mix
    for j in range(KSIZE):
        wide = dot(kern[...], tap_spread(j)).astype(bf16)
        logits[j] = dot(mix, wide)
    step = 32
    for r in range(0, 2 * size, step):
        b, o = r // size, r % size
        vals = [logits[j, r : r + step, :] for j in range(KSIZE)]
        top = vals[0]
        for v in vals[1:]:
            top = jnp.maximum(top, v)
        vals = [jnp.exp(v - top) for v in vals]
        total = vals[0]
        for v in vals[1:]:
            total = total + v
        inv = 1.0 / total
        acc = jnp.zeros((step, DA), f32)
        for j in range(KSIZE):
            k = vals[j] * inv
            taps[j, r : r + step, :] = k.astype(bf16)
            lo = PAD - HALF + j + o
            acc = acc + k * conv32[b, lo : lo + step, :]
        context[r : r + step, :] = acc.astype(bf16)


def sequence_rows(parts, n):
    full_a, full_b, more_a, more_b = parts
    near = full_a.shape[0]
    left, right, at = (full_a, full_b, 2 * n) if 2 * n < near else (more_a, more_b, 2 * n - near)
    rows = jnp.concatenate([left[at : at + 2], right[at : at + 2]], axis=2)
    return rows.reshape(-1, D)


def project_forward(
    meta, full_a, full_b, more_a, more_b, own_a, got_a, own_b, got_b,
    query, keys, values, mats, par, kern, rows32,
):
    near, size, _ = full_a.shape
    blocks = 2 * near
    chunk = 2 * size
    seq_len = meta.seq_len
    even = on_even(meta, (ROWS, DA))
    for side, own, got in ((0, own_a, got_a), (1, own_b, got_b)):
        for piece in range(3):
            fill_rows(own, got, lambda k: meta.weight_place(side, k), piece, even, rows32)
            to = side * 3 + piece
            if to < 5:
                mats[to * D : (to + 1) * D, :] = rows32[...].astype(bf16)
    par[...] = rows32[:, :128].T[:16]
    strips = rows32[:, 128:256].astype(bf16)
    wide = None
    for odd in range(2):
        part = dot(dot_tn(weave(STRIP, odd), strips).astype(bf16), shift_lanes(STRIP, odd))
        wide = part if wide is None else wide + part
    kern[...] = wide.astype(bf16)
    for n in range(near):
        x = sequence_rows((full_a, full_b, more_a, more_b), n)
        at = slice(n * chunk, (n + 1) * chunk)
        keys[at, :] = dot(x, rows_of(mats, 0)).astype(bf16)
        values[at, :] = dot(x, rows_of(mats, 3)).astype(bf16)
        if n == 0:
            q = dot(x, rows_of(mats, 1))
            row = row_iota((size, DA))
            for b in range(2):
                part = q[b * size : (b + 1) * size]
                part = jnp.where(row < seq_len - meta.owner(b) * size, part, 0.0)
                query[b * size : (b + 1) * size, :] = part.astype(bf16)


def attend_forward(meta, query, keys, values, inverse, context, scores):
    queries = query.shape[0]
    size = queries // 2
    chunk = min(keys.shape[0], 256)
    count = keys.shape[0] // chunk
    each = chunk // size
    seq_len = meta.seq_len
    inverse[...] = jnp.zeros(inverse.shape, f32)
    row = row_iota((size, queries))
    for pr in range(HEADS // 2):
        cols = slice(pr * 128, (pr + 1) * 128)
        q = query[:, cols].astype(f32) * (HEAD_DIM ** (-0.5))
        halves = []
        for h in range(2):
            qh = jnp.where(head_mask((queries, 128), h), q, 0.0).astype(bf16)
            top = jnp.full((1, queries), neg_fill, f32)
            for n in range(count):
                s = dot_nt(keys[n * chunk : (n + 1) * chunk, cols], qh)
                for i in range(each):
                    part = s[i * size : (i + 1) * size]
                    part = jnp.where(row < seq_len - meta.owner(each * n + i) * size, part, neg_fill)
                    lo = (each * n + i) * size
                    scores[lo : lo + size, :] = part
                    top = jnp.maximum(top, jnp.max(part, axis=0, keepdims=True))
            total = jnp.zeros((1, queries), f32)
            acc = jnp.zeros((128, queries), f32)
            for n in range(count):
                at = slice(n * chunk, (n + 1) * chunk)
                e = jnp.exp(scores[at, :] - top)
                total = total + jnp.sum(e, axis=0, keepdims=True)
                e = e.astype(bf16)
                acc = acc + dot_tn(values[at, cols], e)
            inv = 1.0 / total
            inverse[2 * pr + h : 2 * pr + h + 1, :] = inv
            inverse[8 + 2 * pr + h : 9 + 2 * pr + h, :] = top
            halves.append((acc * inv)[h * HEAD_DIM : (h + 1) * HEAD_DIM])
        context[:, cols] = jnp.concatenate(halves, axis=0).T


def attend_backward(meta, d_ctx, context, query, keys, values, inverse, d_keys, d_values, d_query):
    total, queries = keys.shape[0], query.shape[0]
    size = queries // 2
    chunk = min(total, 512)
    each = chunk // size
    row = row_iota((size, queries))
    scale = HEAD_DIM ** (-0.5)
    for pr in range(HEADS // 2):
        cols = slice(pr * 128, (pr + 1) * 128)
        grads = d_ctx[:, cols].astype(f32)
        prod = grads * context[:, cols]
        q = query[:, cols].astype(f32)
        d_o, d_os, q_s, q_h, deltas = [], [], [], [], []
        for h in range(2):
            mask = head_mask((queries, 128), h)
            inv = inverse[2 * pr + h : 2 * pr + h + 1, :]
            col = jnp.broadcast_to(inv, (128, queries)).T
            d_o.append(jnp.where(mask, grads, 0.0).astype(bf16))
            d_os.append(jnp.where(mask, grads * col, 0.0).astype(bf16))
            q_s.append(jnp.where(mask, q * col * scale, 0.0).astype(bf16))
            q_h.append(jnp.where(mask, q * scale, 0.0).astype(bf16))
            delta = lax.dot_general(
                jnp.ones((8, 128), f32),
                jnp.where(mask, prod, 0.0),
                (((1,), (1,)), ((), ())),
                precision=lax.Precision.HIGHEST,
                preferred_element_type=f32,
            )
            deltas.append(delta[0:1])
        acc = [jnp.zeros((128, queries), f32) for _ in range(2)]
        for n in range(total // chunk):
            at = slice(n * chunk, (n + 1) * chunk)
            k, v = keys[at, cols], values[at, cols]
            dv = jnp.zeros((chunk, 128), f32)
            dk = jnp.zeros((chunk, 128), f32)
            for h in range(2):
                e = jnp.exp(dot_nt(k, q_h[h]) - inverse[8 + 2 * pr + h : 9 + 2 * pr + h, :])
                parts = []
                for i in range(each):
                    inside = row < meta.seq_len - meta.owner(each * n + i) * size
                    parts.append(jnp.where(inside, e[i * size : (i + 1) * size], 0.0))
                e = jnp.concatenate(parts, axis=0).astype(bf16)
                dv = dv + dot(e, d_os[h])
                dp = dot_nt(v, d_o[h])
                ds = (e.astype(f32) * (dp - deltas[h])).astype(bf16)
                dk = dk + dot(ds, q_s[h])
                acc[h] = acc[h] + dot_tn(k, ds)
            d_keys[at, cols] = dk.astype(bf16)
            d_values[at, cols] = dv.astype(bf16)
        halves = []
        for h in range(2):
            inv = inverse[2 * pr + h : 2 * pr + h + 1, :] * scale
            halves.append((acc[h] * inv)[h * HEAD_DIM : (h + 1) * HEAD_DIM])
        d_query[:, cols] = jnp.concatenate(halves, axis=0).T


def middle(
    meta, exact, small, mine, theirs, cot_mine, cot_theirs, late, par,
    result, d_r1_out, d_ctx, late_g, norms,
    slope, active, rows32, out_a, out_b,
):
    size = mine.shape[0]
    seq_len = meta.seq_len
    gain0, gain1 = par[KSIZE : KSIZE + 1, :], par[KSIZE + 1 : KSIZE + 2, :]
    bias0, bias1 = par[KSIZE + 2 : KSIZE + 3, :], par[KSIZE + 3 : KSIZE + 4, :]
    near = PARTS // 4
    part = near * UNIT
    count = 4
    outs = (out_a, out_b)

    for g in range(GROUPS):
        span = (g * LATE_ROWS + 2 * UNIT, (g + 1) * LATE_ROWS)
        for v in range(PARTS):
            block = late.rows(span)[v, span[0] : span[1], :].astype(f32)
            rows32[v * ROWS : (v + 1) * ROWS, :] = block[:ROWS]
        outs[g][...] = rows32[...].astype(bf16)

    def rows(g, lo, c):
        span = (g * LATE_ROWS, g * LATE_ROWS + 2 * UNIT)
        lo = g * LATE_ROWS + lo
        return late.rows(span)[c * near : (c + 1) * near, lo : lo + UNIT, :].reshape(part, DA)

    def deal(value, g, lo, c):
        lo = g * LATE_ROWS + lo
        for k in range(near):
            v = c * near + k
            at = meta.sum_place_of(v // 2, v % 2)
            late_g[at, lo : lo + UNIT, :] = value[k * UNIT : (k + 1) * UNIT].astype(bf16)

    tall = size + 2 * PAD
    lo = 2 * tall + 2 * size
    ctx_a = exact[: 2 * size, :].astype(bf16)
    ctx_c = small[lo : lo + 2 * size, :]
    ctx = jnp.concatenate([ctx_a, ctx_c], axis=1)
    branch = jnp.concatenate([dot(ctx, t[...]) for t in outs], axis=1)
    tokens = jnp.concatenate([mine[...], theirs[...]], axis=0).astype(f32)
    hat1, inv1 = norm_parts(tokens + branch)
    first = hat1 * gain0 + bias0
    low = first.astype(bf16)
    lows = [low[:, :DA], low[:, DA:]]
    downs = []
    for g in range(GROUPS):
        acc = None
        for c in range(count):
            at = slice(c * part, (c + 1) * part)
            v = dot_nt(lows[g], rows(g, 0, c))
            phi = 0.5 * (1.0 + lax.erf(v * 0.7071067811865476))
            act = (v * phi).astype(bf16)
            active[g, :, at] = act
            slope[g, :, at] = phi + v * (jnp.exp(-0.5 * v * v) * 0.3989422804014327)
            term = dot(act, rows(g, UNIT, c))
            acc = term if acc is None else acc + term
        downs.append(acc)
    hat2, inv2 = norm_parts(first + jnp.concatenate(downs, axis=1))
    result[...] = (hat2 * gain1 + bias1).astype(bf16)
    flush(result)

    row = row_iota((size, D))
    grad = jnp.concatenate(
        [
            jnp.where(row < seq_len - meta.owner(b) * size, t[...].astype(f32), 0.0)
            for b, t in enumerate((cot_mine, cot_theirs))
        ],
        axis=0,
    )
    norms[...] = jnp.zeros(norms.shape, f32)
    norms[1:2, :] = jnp.sum(grad * hat2, axis=0, keepdims=True)
    norms[3:4, :] = jnp.sum(grad, axis=0, keepdims=True)
    d_r2 = norm_back(hat2, inv2, grad, gain1)
    d_down = d_r2.astype(bf16)
    firsts = []
    for g in range(GROUPS):
        dd = d_down[:, g * DA : (g + 1) * DA]
        acc = None
        for c in range(count):
            at = slice(c * part, (c + 1) * part)
            da = dot_nt(dd, rows(g, UNIT, c))
            di = (da * slope[g, :, at]).astype(bf16)
            deal(dot_tn(active[g, :, at], dd), g, UNIT, c)
            deal(dot_tn(di, lows[g]), g, 0, c)
            term = dot(di, rows(g, 0, c))
            acc = term if acc is None else acc + term
        firsts.append(acc)
        late_g.flush((g * LATE_ROWS, g * LATE_ROWS + 2 * UNIT))
    d_first = d_r2 + jnp.concatenate(firsts, axis=1)
    norms[0:1, :] = jnp.sum(d_first * hat1, axis=0, keepdims=True)
    norms[2:3, :] = jnp.sum(d_first, axis=0, keepdims=True)
    d_r1 = norm_back(hat1, inv1, d_first, gain0)
    d_r1_out[...] = d_r1
    flush(d_r1_out)
    d_branch = d_r1.astype(bf16)
    gap = jnp.zeros((32 - ROWS, DA), f32)
    for g in range(GROUPS):
        value = dot_tn(ctx, d_branch[:, g * DA : (g + 1) * DA])
        lo = g * LATE_ROWS + 2 * UNIT
        for v in range(PARTS):
            at = meta.sum_place_of(v // 2, v % 2)
            block = jnp.concatenate([value[v * ROWS : (v + 1) * ROWS], gap], axis=0)
            late_g[at, lo : lo + 32, :] = block.astype(bf16)
    d_context = dot_nt(d_branch[:, :DA], out_a[...]) + dot_nt(d_branch[:, DA:], out_b[...])
    d_ctx[...] = d_context.astype(bf16)


def conv_backward(
    meta, d_ctx, ext, query, conv, depth_out, key_conv, mixed, taps, mats, par, kern,
    d_query, d_ext, g_point, g_c, g_kern, g_depth,
    ext32, conv32, d_kern, d_conv, d_dep,
):
    size = query.shape[0] // 2
    for b in range(2):
        ext32[b] = ext[b].astype(f32)
        conv32[b] = conv[b].astype(f32)
    d_conv[...] = jnp.zeros(d_conv.shape, f32)
    sums = head_sums()
    for j in range(KSIZE):
        for b in range(2):
            lo = PAD - HALF + j
            rows = slice(b * size, (b + 1) * size)
            grad = d_ctx[rows, DA:].astype(f32)
            prod = (grad * conv32[b, lo : lo + size, :]).astype(bf16)
            d_kern[j, rows, :] = dot(prod, sums)
            d_conv[b, lo : lo + size, :] += taps[j, rows, :].astype(f32) * grad
    picks = [tap_pick(j) for j in range(KSIZE)]
    compact = jnp.zeros((2 * size, 128), f32)
    total = jnp.zeros((2 * size, DA), f32)
    for j in range(KSIZE):
        total = total + taps[j].astype(f32) * d_kern[j]
    for j in range(KSIZE):
        dl = (taps[j].astype(f32) * (d_kern[j] - total)).astype(bf16)
        compact = compact + dot(dl, picks[j])
    compact = compact.astype(bf16)
    wide = dot_tn(mixed[...], compact).astype(bf16)
    strips = None
    for odd in range(2):
        r = lax.broadcasted_iota(jnp.int32, (128, 128), 0)
        c = lax.broadcasted_iota(jnp.int32, (128, 128), 1)
        pick = jnp.where((c < STRIP) & (r == c + odd * STRIP), 1.0, 0.0).astype(bf16)
        part = dot(weave(STRIP, odd), dot(wide, pick).astype(bf16))
        strips = part if strips is None else strips + part
    g_kern[...] = strips
    d_mixed = dot_nt(compact, kern[...])
    d_kc = (d_mixed * query[...].astype(f32)).astype(bf16)
    d_query[...] = d_mixed * key_conv[...]
    g_point[...] = dot_tn(depth_out[...], d_kc).astype(bf16)
    d_dep[...] = dot_nt(d_kc, rows_of(mats, 2))
    gc = None
    for b in range(2):
        dc = d_conv[b].astype(bf16)
        d_ext[b] = dot_nt(dc, rows_of(mats, 4))
        part = dot_tn(ext[b], dc)
        gc = part if gc is None else gc + part
    g_c[...] = gc.astype(bf16)
    g_depth[...] = jnp.zeros(g_depth.shape, f32)
    for c in range(0, D, 128):
        cols = slice(c, c + 128)
        for j in range(KSIZE):
            lo = PAD - HALF + j
            acc = jnp.zeros((1, 128), f32)
            for b in range(2):
                dd = d_dep[b * size : (b + 1) * size, cols]
                acc = acc + jnp.sum(dd * ext32[b, lo : lo + size, cols], axis=0, keepdims=True)
                d_ext[b, lo : lo + size, cols] += par[j : j + 1, cols] * dd
            g_depth[j : j + 1, cols] = acc


def project_backward(
    meta, d_keys, d_values, d_query, d_ext, mats, full_a, full_b, more_a, more_b, d_full,
):
    near, size, _ = full_a.shape
    blocks = 2 * near
    chunk = 2 * size
    dq = d_query[...]
    for n in range(blocks // 2):
        at = slice(n * chunk, (n + 1) * chunk)
        both = dot_nt(d_keys[at, :], rows_of(mats, 0))
        both = both + dot_nt(d_values[at, :], rows_of(mats, 3))
        if n == 0:
            both = both + dot_nt(dq, rows_of(mats, 1))
            both = both + jnp.concatenate(
                [d_ext[b, PAD : PAD + size, :] for b in range(2)], axis=0
            )
        d_full[2 * n : 2 * n + 2] = both.astype(bf16).reshape(2, size, D)
    for b in range(2):
        base = meta.owner(b) * size
        before, after = meta.place(meta.owner(b) - 1), meta.place(meta.owner(b) + 1)
        rim = jnp.where(row_iota((PAD, D)) + (base - PAD) >= 0, d_ext[b, :PAD, :], 0.0)
        old = d_full[before, size - PAD :, :].astype(f32)
        d_full[before, size - PAD :, :] = (old + rim).astype(bf16)
        inside = row_iota((PAD, D)) + (base + size) < blocks * size
        rim = jnp.where(inside, d_ext[b, PAD + size :, :], 0.0)
        old = d_full[after, :PAD, :].astype(f32)
        d_full[after, :PAD, :] = (old + rim).astype(bf16)
    for n in range(blocks):
        left, right, at = (full_a, full_b, n) if n < near else (more_a, more_b, n - near)
        rows = d_full[n]
        left[at] = rows[:, :DA]
        right[at] = rows[:, DA:]


def project_grads(
    meta, full_a, full_b, more_a, more_b, d_keys, d_values, ext, d_query, g_point, g_c, g_kern,
    g_depth, norms, keep_a, send_a, keep_b, send_b,
):
    near, size, _ = full_a.shape
    blocks = 2 * near
    even = on_even(meta, (ROWS, DA))
    x = jnp.concatenate(
        [sequence_rows((full_a, full_b, more_a, more_b), n) for n in range(near)], axis=0
    )
    own = jnp.concatenate([ext[b, PAD : PAD + size, :] for b in range(2)], axis=0)
    dq = d_query[...]
    rows = jnp.concatenate(
        [g_depth[:KSIZE, :], norms[:4, :], jnp.zeros((128 - KSIZE - 4, D), f32)], axis=0
    )
    small = jnp.concatenate([rows.T, g_kern[...], jnp.zeros((D, 128), f32)], axis=1)
    g_kv = dot_tn(x, jnp.concatenate([d_keys[...], d_values[...]], axis=1))
    for side, keep, send, values in (
        (0, keep_a, send_a, (g_kv[:, :DA], dot_tn(own, dq), g_point[...].astype(f32))),
        (1, keep_b, send_b, (g_kv[:, DA:], g_c[...].astype(f32), small)),
    ):
        for piece, value in enumerate(values):
            deal_rows(value, lambda k: meta.weight_place(side, k), piece, even, keep, send)


def pack_early(meta, w_in, w_point, kern, w_depth, ln_gain, ln_bias, early, turn):
    for to, at in ((0, 1), (1, 0), (3, 2), (4, 3)):
        early[to] = w_in[:, at * DA : (at + 1) * DA]
    early[2] = w_point[...]
    wide = w_in.shape[0]
    turn[...] = jnp.zeros(turn.shape, f32)
    turn[:KSIZE, :wide] = w_depth[...].astype(f32)
    turn[KSIZE : KSIZE + 2, :wide] = ln_gain[...].astype(f32)
    turn[KSIZE + 2 : KSIZE + 4, :wide] = ln_bias[...].astype(f32)
    small = turn[...].T[:wide]
    early[5] = jnp.zeros(early.shape[1:], bf16)
    early[5, :, :128] = small.astype(bf16)
    early[5, :, 128 : 128 + STRIP] = kern[...]


def pack_late(meta, w_up, w_down, w_out, late):
    wide = w_out.shape[0]
    for g in range(GROUPS):
        lo = g * LATE_ROWS
        late[lo : lo + UNIT, :] = w_up[g]
        late[lo + UNIT : lo + 2 * UNIT, :] = w_down[g]
        out = w_out[:, g * DA : (g + 1) * DA].astype(f32)
        out = jnp.concatenate([out, jnp.zeros((32 - wide, DA), f32)], axis=0)
        late[lo + 2 * UNIT : lo + LATE_ROWS, :] = out.astype(bf16)


def kept_shapes(total, own, tall):
    return (
        ((5 * D, DA), (own, DA), (total, DA), (total, DA)),
        ((2, tall, DA), (own, DA), (own, DA), (KSIZE, own, DA)),
        ((2, tall, D), (own, D)),
        ((own, DA), (own, DA)),
    )


def front(
    meta, full_a, full_b, more_a, more_b, own_a, got_a, own_b, got_b,
    proj, small, wide, exact, inverse, par, kern,
    rows32, scores, ext32, conv32, logits,
):
    near, size, _ = full_a.shape
    shapes = kept_shapes(2 * near * size, 2 * size, size + 2 * PAD)
    mats, query, keys, values = views(proj, shapes[0])
    conv, mixed, context_c, taps = views(small, shapes[1])
    ext, depth_out = views(wide, shapes[2])
    context_a, key_conv = views(exact, shapes[3])
    full = (full_a, full_b, more_a, more_b)
    project_forward(
        meta, *full, own_a, got_a, own_b, got_b, query, keys, values, mats, par, kern, rows32
    )
    flush(proj)
    attend_forward(meta, query, keys, values, inverse, context_a, scores)
    conv_forward(
        meta, *full, mats, par, kern, query, ext, conv, depth_out, key_conv, mixed, taps, context_c,
        ext32, conv32, logits,
    )


def back(
    meta, d_ctx, small, wide, exact, proj, full_a, full_b, more_a, more_b, inverse, par, kern, norms,
    here_a, here_b, there_a, there_b, keep_a, send_a, keep_b, send_b,
    ext32, conv32, d_kern, d_conv, d_dep, dq_c, dq_a, g_point, g_c, g_kern, g_depth, d_ext, d_query,
    d_full,
):
    near, size, _ = full_a.shape
    shapes = kept_shapes(2 * near * size, 2 * size, size + 2 * PAD)
    mats, query, keys, values = views(proj, shapes[0])
    conv, mixed, context_c, taps = views(small, shapes[1])
    ext, depth_out = views(wide, shapes[2])
    context_a, key_conv = views(exact, shapes[3])
    conv_backward(
        meta, d_ctx, ext, query, conv, depth_out, key_conv, mixed, taps, mats, par, kern,
        dq_c, d_ext, g_point, g_c, g_kern, g_depth, ext32, conv32, d_kern, d_conv, d_dep,
    )
    attend_backward(
        meta, d_ctx, context_a, query, keys, values, inverse, keys, values, dq_a
    )
    d_query[...] = (dq_a[...] + dq_c[...]).astype(bf16)
    project_backward(
        meta, keys, values, d_query, d_ext, mats, here_a, here_b, there_a, there_b, d_full
    )
    flush(here_a, here_b, there_a, there_b)
    project_grads(
        meta, full_a, full_b, more_a, more_b, keys, values, ext, d_query, g_point, g_c, g_kern,
        g_depth, norms, keep_a, send_a, keep_b, send_b,
    )


def blocks_of(full):
    cut = full.reshape(full.shape[0], PARTS // 2, 2, ROWS, DA).transpose(2, 1, 0, 3, 4)
    return cut[0], cut[1]


def whole_of(keep, send):
    both = jnp.stack([keep, send]).transpose(2, 1, 0, 3, 4)
    return both.reshape(both.shape[0], D, DA)


def gathered(weights):
    dims = (0, 1, 0, 0, 0, 1, 1, 2, 1)
    w_in, w_depth, w_point, w_kern, w_out, gain, bias, w_up, w_down = (
        lax.all_gather(t, AXES, axis=d, tiled=True) for t, d in zip(weights, dims)
    )
    w_q, w_k, w_v, w_c = (w_in[:, i * DA : (i + 1) * DA] for i in range(4))
    small = jnp.concatenate([w_depth.T, gain.T, bias.T], axis=1)
    small = jnp.pad(small, ((0, 0), (0, 128 - small.shape[1])))
    strips = jnp.pad(w_kern.reshape(D, STRIP), ((0, 0), (0, 256 - STRIP)))
    small = jnp.concatenate([small, strips], axis=1)
    early = blocks_of(jnp.stack([w_k, w_q, w_point])) + blocks_of(jnp.stack([w_v, w_c, small]))
    late = []
    for g in range(GROUPS):
        out = w_out[:, g * DA : (g + 1) * DA].reshape(PARTS, ROWS, DA)
        side = jnp.concatenate(
            [
                w_up[g].T.reshape(PARTS, UNIT, DA),
                w_down[g].reshape(PARTS, UNIT, DA),
                jnp.pad(out, ((0, 0), (0, 32 - ROWS), (0, 0))),
            ],
            axis=1,
        )
        late.append(side)
    late = jnp.concatenate(late, axis=1)
    return early, late


def scattered(early_g, late):
    g_k, g_q, g_point = whole_of(*early_g[:2])
    g_v, g_c, g_small = whole_of(*early_g[2:])
    late = late.reshape(PARTS, GROUPS, LATE_ROWS, DA)
    g_up = jnp.stack([late[:, g, :UNIT].reshape(-1, DA).T for g in range(GROUPS)])
    g_down = jnp.stack([late[:, g, UNIT : 2 * UNIT].reshape(-1, DA) for g in range(GROUPS)])
    g_out = jnp.concatenate(
        [late[:, g, 2 * UNIT : 2 * UNIT + ROWS].reshape(D, DA) for g in range(GROUPS)], axis=1
    )
    grads = (
        jnp.concatenate([g_q, g_k, g_v, g_c], axis=1),
        g_small[:, :KSIZE].T,
        g_point,
        g_small[:, 128 : 128 + STRIP].reshape(-1),
        g_out,
        g_small[:, KSIZE : KSIZE + 2].T,
        g_small[:, KSIZE + 2 : KSIZE + 4].T,
        g_up,
        g_down,
    )
    dims = (0, 1, 0, 0, 0, 1, 1, 2, 1)
    return tuple(
        lax.psum_scatter(t.astype(f32), AXES, scatter_dimension=d, tiled=True)
        for t, d in zip(grads, dims)
    )


def per_device(hidden, out_grad, lengths, *weights):
    w_in, w_depth, w_point, w_kern, w_out, ln_gain, ln_bias, w_up, w_down = weights
    length = hidden.shape[2]
    half, grp, mate, core = (lax.axis_index(a) for a in AXES[1:])
    grps = lax.axis_size("grp")
    groups = grps * lax.axis_size("mate")
    wide = w_in.shape[0]
    packed = wide == ROWS and grps == 2 and lax.axis_size("slot") == 2

    mine = lax.dynamic_index_in_dim(hidden[0], half, 0, keepdims=False)
    theirs = lax.dynamic_index_in_dim(hidden[0], 1 - half, 0, keepdims=False)
    seq_len = lax.dynamic_index_in_dim(lengths[0], half, 0, keepdims=False)
    given, theirs = theirs, swap(theirs, "half")
    own_tokens = jnp.stack([mine, theirs])
    count = 4 * groups
    total = count * length
    own = 2 * length
    meta = jnp.stack([seq_len, lax.axis_index("slot"), half, grp, mate, core]).astype(jnp.int32)
    call = functools.partial(kernel_call, form=(grps, packed))

    full, met = [], []
    for i, order in enumerate((routes()[1],) * 2):
        rows = own_tokens[..., i * DA : (i + 1) * DA]
        rows = rows.reshape((1,) * len(order) + rows.shape)
        for n, bit in enumerate(order):
            got = swap(rows, *bit)
            if n == 0:
                met.append(got)
            rows = jnp.concatenate([rows, got], axis=routes()[0].index(bit))
        full.append(rows.reshape(-1, length, DA))
    full = full + [swap(t, "core") for t in full]

    if packed:
        one, mark = call(
            pack_early,
            "pack_early",
            jnp.zeros((6,), jnp.int32),
            (w_in, w_point, w_kern.reshape(wide, STRIP), w_depth, ln_gain, ln_bias),
            (((6, wide, DA), bf16),),
            (((128, 128), f32),),
            waits=(given,),
        )
        two, mark = call(
            pack_late,
            "pack_late",
            jnp.zeros((6,), jnp.int32),
            (w_up.transpose(0, 2, 1), w_down, w_out),
            (((GROUPS * LATE_ROWS, DA), bf16),),
            waits=(one,),
        )
        late = lax.all_gather(two, AXES, axis=0)
        one = one[None]
        for bit in first_bits():
            one = gather_bit(one, bit)
        early = []
        for i, order in enumerate(sides()):
            part = one[:, 3 * i : 3 * i + 3]
            for bit in order:
                part = gather_bit(part, bit)
            early += [part, swap(part, "core")]
    else:
        early, late = gathered(weights)
    waits = []
    turn = half
    cot_mine = lax.dynamic_index_in_dim(out_grad[0], turn, 0, keepdims=False)
    cot_theirs = swap(lax.dynamic_index_in_dim(out_grad[0], 1 - turn, 0, keepdims=False), "half")

    tall = length + 2 * PAD
    kept = kept_shapes(total, own, tall)

    def together(shapes, kind):
        return ((sum(math.prod(t[:-1]) for t in shapes), shapes[0][-1]), kind)

    proj, small, wide_rows, exact, inverse, par, kern, mark = call(
        front,
        "front",
        meta,
        (*full, *early),
        (
            *(together(t, kind) for t, kind in zip(kept, (bf16, bf16, bf16, f32))),
            ((16, own), f32),
            ((16, D), f32),
            ((DA, 128), bf16),
        ),
        (
            ((D, DA), f32),
            ((total, own), f32),
            ((2, tall, D), f32),
            ((2, tall, DA), f32),
            ((KSIZE, own, DA), f32),
        ),
        flops=4 * (total + own) * D * DA + 16 * own * total * DA + 2 * own * DA * (3 * D + KSIZE * DA),
        exps=HEADS * own * total + KSIZE * own * DA,
        waits=waits,
    )
    ff = UNIT * PARTS
    spans = tuple(
        (g * LATE_ROWS + lo, g * LATE_ROWS + hi)
        for lo, hi in (OUT_SPAN, FF_SPAN)
        for g in range(GROUPS)
    )
    result, d_r1, d_context, late_g, norms, mark = call(
        middle,
        "middle",
        meta,
        (exact, small, mine, theirs, cot_mine, cot_theirs, late, par),
        (
            ((own, D), bf16),
            ((own, D), f32),
            ((own, D), bf16),
            ((PARTS, GROUPS * LATE_ROWS, DA), bf16),
            ((8, D), f32),
        ),
        (
            ((GROUPS, own, ff), f32),
            ((GROUPS, own, ff), bf16),
            ((D, DA), f32),
            ((D, DA), bf16),
            ((D, DA), bf16),
        ),
        flops=6 * own * (D * D + 4 * D * ff // GROUPS),
        exps=4 * own * ff,
        in_spans={0: ((0, own),), 1: ((2 * tall + own, 2 * tall + 2 * own),), 6: spans},
        out_spans={3: spans},
    )
    if packed:
        late_g = lax.psum_scatter(late_g, ("slot", "mate", "core"), scatter_dimension=0, tiled=True)

    early_shape = (PARTS // 2, 3, ROWS, DA)
    *both, mark = call(
        back,
        "back",
        meta,
        (
            d_context, small, wide_rows, exact, proj, *full, inverse, par, kern, norms,
        ),
        (((2 * groups, length, DA), bf16),) * 4 + ((early_shape, bf16),) * 4,
        (
            ((2, tall, D), f32),
            ((2, tall, DA), f32),
            ((KSIZE, own, DA), f32),
            ((2, tall, DA), f32),
            ((own, D), f32),
            ((own, DA), f32),
            ((own, DA), f32),
            ((D, DA), bf16),
            ((D, DA), bf16),
            ((D, 128), f32),
            ((16, D), f32),
            ((2, tall, D), f32),
            ((own, DA), bf16),
            ((count, length, D), bf16),
        ),
        flops=40 * own * total * DA + 4 * total * D * DA,
    )
    d_full, early_g = both[:4], both[4:]
    res_kept = result[:length]
    res_got = jnp.where(mark == 0, swap(result[length:], "half"), 0)
    if packed:
        sums = []
        for i in range(2):
            got = swap(early_g[2 * i + 1], "core")
            sums.append((early_g[2 * i].astype(f32) + got.astype(f32)).astype(bf16))
    parts = []
    for i, order in enumerate(routes()):
        near = d_full[i].astype(f32) + swap(d_full[2 + i], "core").astype(f32)
        near = near.astype(bf16).reshape(groups, 2, length, DA)
        parts.append(scatter_blocks(near, routes()[1]))
    d_full = jnp.concatenate(parts, axis=-1).reshape(own, D)
    here = ((half * grps + grp) * 2 + mate) * 2 + core
    there = (((1 - half) * grps + grp) * 2 + mate) * 2 + core
    starts = jnp.stack([here, there]) * length
    own_mask = jnp.arange(length, dtype=jnp.int32)[None] + starts[:, None] < seq_len
    d_hidden = (d_r1 + jnp.where(own_mask.reshape(own, 1), d_full, 0.0)).astype(bf16)

    if packed:
        for i, order in enumerate(sides()):
            for bit in reversed(order):
                sums[i] = scatter_bit(sums[i], bit)
        four = sums[0].shape[0]
        rest = [t.reshape(four, -1, DA) for t in (*sums, late_g)]
        rest = jnp.concatenate(rest, axis=1)
        last = first_bits()[::-1]
        rest = [rest[:, :208], rest[:, 208:]]
        for n, bit in enumerate(last):
            rest = [scatter_bit(t, bit, bf16 if n + 1 < len(last) else f32) for t in rest]
        rest = jnp.concatenate(rest, axis=1)
        g_k, g_q, g_point, g_v, g_c, g_small = rest[0, : 6 * ROWS].reshape(6, ROWS, DA)
        late_g = rest[0, 6 * ROWS :]
        late_g = late_g.reshape(GROUPS, LATE_ROWS, DA)
        grads = (
            jnp.concatenate([g_q, g_k, g_v, g_c], axis=1),
            g_small[:, :KSIZE].T,
            g_point,
            g_small[:, 128 : 128 + STRIP].reshape(-1),
            jnp.concatenate([t[2 * UNIT :][:ROWS] for t in late_g], axis=1),
            g_small[:, KSIZE : KSIZE + 2].T,
            g_small[:, KSIZE + 2 : KSIZE + 4].T,
            late_g[:, :UNIT].transpose(0, 2, 1),
            late_g[:, UNIT : 2 * UNIT],
        )
    else:
        grads = scattered(early_g, late_g)

    got = swap(d_hidden[length:], "half")
    kept = d_hidden[:length]

    def in_order(kept, got):
        return jnp.where(half == 0, jnp.stack([kept, got]), jnp.stack([got, kept]))[None]

    return (in_order(res_kept, res_got), in_order(kept, got), *grads)


def solution(mesh):
    slots, seqs = mesh.shape["slot"], mesh.shape["seq"]
    fine = Mesh(mesh.devices.reshape(slots, 2, seqs // 8, 2, 2), AXES)
    seq = AXES[1:]
    placed = (
        P("slot", None, seq, None),
        P("slot", None, seq, None),
        P("slot", None),
        P(AXES, None),
        P(None, AXES),
        P(AXES, None),
        P(AXES),
        P(AXES, None),
        P(None, AXES),
        P(None, AXES),
        P(None, None, AXES),
        P(None, AXES, None),
    )
    return jax.shard_map(
        per_device,
        mesh=fine,
        in_specs=placed,
        out_specs=(placed[0], placed[1]) + placed[3:],
        check_vma=False,
    )
```
